256 devices in a mesh: dp: 16 (over z, core), mp: 16 (over x, y).
Axes of the slice: x: 4, y: 4, z: 8, core: 2. Of those that a mesh axis runs over, the one named last changes fastest.
Arguments:
- hidden_in: bfloat16 [64, 64, 7168], P('dp', None, 'mp'), may hold values from -6 to 6
- norm_gain: bfloat16 [7168], P('mp'), may hold values from 0.099609375 to 1.8984375
- w_query: bfloat16 [7168, 7168], P('dp', 'mp'), may hold values from -0.070868339 to 0.070868339
- w_key: bfloat16 [7168, 1024], P('dp', 'mp'), may hold values from -0.070868339 to 0.070868339
- w_value: bfloat16 [7168, 1024], P('dp', 'mp'), may hold values from -0.0625 to 0.0625
- w_out: bfloat16 [7168, 7168], P('mp', 'dp'), may hold values from -0.09375 to 0.09375
- key_cache: bfloat16 [64, 16, 1, 2048, 128], P('dp', 'mp'), may hold values from -52 to 52
- value_cache: bfloat16 [64, 16, 1, 2048, 128], P('dp', 'mp'), may hold values from -3 to 3
- cache_len: int32 [64], P('dp'), may hold values from 256 to 4096, as said below
- tree_parent: int32 [64, 64], P('dp'), may hold values from 0 to 62, as said below
- valid_nodes: int32 [64, 64], P('dp'), may hold values from 0 to 1, as said below
- accepted_path: int32 [64, 8], P('dp'), may hold values from 0 to 63, as said below
- slot_owner: int32 [64], replicated, may hold values from 0 to 63, each once
Outputs:
- layer_out: bfloat16 [64, 64, 7168], P('dp', None, 'mp')
- accepted_kv: bfloat16 [64, 8, 2, 1024], P('dp', None, None, 'mp')
The draws below stay inside these ranges and needn't reach their ends.
Inputs may be any that keep to these rules, and one draw needn't show every extreme that they name: `cache_len`: some request holds exactly 4096 positions in every draw. `tree_parent`: node 0 is its own parent; every other node's parent is one of the three nodes before it. `valid_nodes`: the 1 entries of each request form a prefix of 32 to 64 nodes. `accepted_path`: each row is a chain in which every node is the parent of the next (node 0 may repeat at the start), ending at the request's last real node. `slot_owner`: each slot is named once.
All inputs are finite; a program needn't handle non-finite values.
Results may differ from the reference program's by a relative error of at most 0.007.
The reference program's roundings to bfloat16 on the way count: a program that leaves them out, or rounds other values in their place, can miss the bound.
Values may be sent and summed in bfloat16 or wider, within the bound.
No kernel may reach another device: no remote copies, remote signals or barrier semaphores. Data moves between devices by JAX's collectives and lax.ppermute only.
A program may use at most 128 MiB of HBM per device.

```python
import math
import jax
import jax.numpy as jnp
from jax import lax

D = 7168
QH = 56
KV = 8
HEAD = 128
TREE = 64
ACC = 8
CACHE = 4096
REQS = 64
HALF = 2048
SLABS = 16
KV_GRP = 1
GROUP = 7


def tree_parts(key):
    steps_back = jax.random.randint(jax.random.fold_in(key, 11), (REQS, TREE), 1, 4)
    nodes = jnp.arange(TREE, dtype=jnp.int32)
    parents = jnp.maximum(nodes[None, :] - steps_back, 0).astype(jnp.int32)
    counts = jax.random.randint(jax.random.fold_in(key, 12), (REQS,), TREE // 2, TREE + 1).astype(jnp.int32)
    return (parents, counts)


def query_base(key):
    normal_entries = jax.random.normal(jax.random.fold_in(key, 51), (D, QH * HEAD), jnp.float32)
    return jnp.clip(normal_entries, -6.0, 6.0)


def draw_w_query(key, part):
    base = query_base(key)
    return (base * D ** (-0.5)).astype(jnp.bfloat16)


def draw_w_key(key, part):
    base = query_base(key)
    key = jax.random.fold_in(key, 53)
    picked = base.reshape(D, KV, GROUP, HEAD)[:, :, 0, :].reshape(D, KV * HEAD)
    fresh = jax.random.normal(key, (D, KV * HEAD), jnp.float32)
    mixed = jnp.clip(0.9 * picked + 0.436 * fresh, -6.0, 6.0)
    return (mixed * D ** (-0.5)).astype(jnp.bfloat16)


def draw_tree_parent(key, part):
    parents, counts = tree_parts(key)
    return parents


def draw_valid_nodes(key, part):
    parents, counts = tree_parts(key)
    nodes = jnp.arange(TREE, dtype=jnp.int32)
    return (nodes[None, :] < counts[:, None]).astype(jnp.int32)


def draw_accepted_path(key, part):
    parents, counts = tree_parts(key)
    current = (counts - 1).astype(jnp.int32)
    chain = [current]
    for turns in range(ACC - 1):
        current = jnp.take_along_axis(parents, current[:, None], axis=1)[:, 0]
        chain.append(current)
    return jnp.stack(chain[::-1], 1).astype(jnp.int32)


def draw_cache_len(key, part):
    lengths = jax.random.randint(jax.random.fold_in(key, 21), (REQS,), CACHE // 16, CACHE + 1)
    chosen = jax.random.randint(jax.random.fold_in(key, 22), (), 0, REQS)
    lengths = jnp.where(jnp.arange(REQS, dtype=jnp.int32) == chosen, CACHE, lengths)
    return lengths.astype(jnp.int32)


def draw_key_cache(key, part):
    shape = (REQS, SLABS, KV_GRP, HALF, HEAD)
    base = jnp.clip(jax.random.normal(jax.random.fold_in(key, 31), shape, jnp.float32), -6.0, 6.0)
    return base.astype(jnp.bfloat16)


def draw_value_cache(key, part):
    shape = (REQS, SLABS, KV_GRP, HALF, HEAD)
    means = jax.random.uniform(jax.random.fold_in(key, 41), (REQS, SLABS, KV_GRP, 16, HEAD), jnp.float32, -1.5, 1.5)
    means = jnp.repeat(means, HALF // 16, axis=3)
    noise = jnp.clip(jax.random.normal(jax.random.fold_in(key, 43), shape, jnp.float32), -2.5, 2.5) * 0.5
    values = means + noise
    return values.astype(jnp.bfloat16)


def strengthened(entries, rng, source, target, shards_of, factor):
    owner, partner = [(jnp.arange(entries.shape[dim]) // (entries.shape[dim] // shards_of)).reshape([-1 if axis == dim else 1 for axis in range(entries.ndim)]) for dim in (source, target)]
    chosen = jax.random.permutation(rng, shards_of)[partner]
    strong = (owner == chosen) | (owner == (partner + shards_of // 2) % shards_of)
    return jnp.where(strong, factor * entries, entries)


def levels(own_key, shape, cuts, smallest, largest):
    factor_of = 1.0
    for axis_at, parts in cuts:
        steps = jax.random.uniform(jax.random.fold_in(jax.random.fold_in(own_key, 6), axis_at), (parts,), jnp.float32, smallest / len(cuts), largest / len(cuts))
        factor_of = factor_of * jnp.repeat(jnp.exp(steps), shape[axis_at] // parts).reshape((-1,) + (1,) * (len(shape) - 1 - axis_at))
    return factor_of


def gaussian(own_key, extent, scale, most, shards=(), kind=jnp.bfloat16):
    level = levels(own_key, extent, shards, -0.22, 0.18) if shards else 1.0
    array = jax.random.normal(own_key, extent, jnp.float32) * scale * level
    return jnp.minimum(jnp.maximum(array, -most), most).astype(kind)


def noise_with(key, shape, deviation, bound, pieces, heavy, kind=jnp.bfloat16):
    array = deviation * jax.random.normal(key, shape, jnp.float32)
    if pieces:
        array = array * levels(key, shape, pieces, -0.22, 0.18)
    return jnp.clip(strengthened(array, jax.random.fold_in(key, 3), *heavy), -bound, bound).astype(kind)


def setup_inputs(seed: int = 0) -> dict:
    key_list = jax.random.split(jax.random.key(seed), 14)
    return {
        "hidden_in": gaussian(key_list[0], (REQS, TREE, D), 1.0, 6.0, ((0, 16), (2, 16))),
        "norm_gain": jnp.clip(1.0 + 0.18 * jax.random.normal(key_list[1], (D,), jnp.float32), 0.099609375, 1.8984375).astype(jnp.bfloat16),
        "w_query": draw_w_query(jax.random.fold_in(key_list[13], 71), 0),
        "w_key": draw_w_key(jax.random.fold_in(key_list[13], 71), 0),
        "w_value": gaussian(key_list[4], (D, KV * HEAD), D ** -0.5, 0.0625, ((0, 16), (1, 16))),
        "w_out": noise_with(key_list[5], (QH * HEAD, D), (QH * HEAD) ** -0.5, 0.09375, ((0, 16), (1, 16)), (0, 1, 16, 2.0)),
        "key_cache": draw_key_cache(jax.random.fold_in(key_list[13], 71), 0),
        "value_cache": draw_value_cache(jax.random.fold_in(key_list[13], 71), 0),
        "cache_len": draw_cache_len(jax.random.fold_in(key_list[13], 71), 0),
        "tree_parent": draw_tree_parent(jax.random.fold_in(key_list[13], 71), 0),
        "valid_nodes": draw_valid_nodes(jax.random.fold_in(key_list[13], 71), 0),
        "accepted_path": draw_accepted_path(jax.random.fold_in(key_list[13], 71), 0),
        "slot_owner": jax.random.permutation(key_list[12], REQS).astype(jnp.int32),
    }


epsilon = 1e-05
rope_base = 5000000.0
masked_score = -1e+30

def tree_closure(parents):
    width = parents.shape[-1]
    nodes = jnp.arange(width, dtype=jnp.int32)
    onehot = (parents[..., None] == nodes).astype(jnp.float32)
    reach = jnp.minimum(jnp.eye(width, dtype=jnp.float32) + onehot, 1.0)
    for rounds in range((width - 1).bit_length()):
        reach = jnp.minimum(jnp.einsum('rij,rjk->rik', reach, reach, precision=lax.Precision.HIGHEST), 1.0)
    return reach

def rotate(values, positions):
    head_dim = values.shape[-1]
    half_dim = head_dim // 2
    freq_steps = jnp.arange(half_dim, dtype=jnp.float32)
    inverse = jnp.exp(freq_steps * (-2.0 * math.log(rope_base) / head_dim))
    angles = positions[..., None] * inverse
    cosine = jnp.concatenate([jnp.cos(angles), jnp.cos(angles)], -1)[..., None, :]
    sine = jnp.concatenate([jnp.sin(angles), jnp.sin(angles)], -1)[..., None, :]
    turned = jnp.concatenate([-values[..., half_dim:], values[..., :half_dim]], -1)
    return values * cosine + turned * sine

def relayout(slabs):
    grouped = slabs.reshape(SLABS // 2, 2, KV_GRP, HALF, HEAD)
    return grouped.transpose(0, 2, 1, 3, 4).reshape(KV, CACHE, HEAD)

def reference(hidden_in, norm_gain, w_query, w_key, w_value, w_out, key_cache, value_cache, cache_len, tree_parent, valid_nodes, accepted_path, slot_owner):
    widened = hidden_in.astype(jnp.float32)
    meansq = lax.optimization_barrier(jnp.mean(widened * widened, -1, keepdims=True))
    normed = (widened * lax.rsqrt(meansq + epsilon) * norm_gain.astype(jnp.float32)).astype(jnp.bfloat16)
    flat = normed.reshape(REQS * TREE, D)
    query = jnp.dot(flat, w_query, preferred_element_type=jnp.float32).astype(jnp.bfloat16)
    key_new = jnp.dot(flat, w_key, preferred_element_type=jnp.float32).astype(jnp.bfloat16)
    value_new = jnp.dot(flat, w_value, preferred_element_type=jnp.float32).astype(jnp.bfloat16)
    reach = tree_closure(tree_parent)
    depth = lax.optimization_barrier(jnp.sum(reach, -1)) - 1.0
    position = cache_len[:, None].astype(jnp.float32) + depth
    rot_query = rotate(query.reshape(REQS, TREE, QH, HEAD).astype(jnp.float32), position).astype(jnp.bfloat16)
    rot_key = rotate(key_new.reshape(REQS, TREE, KV, HEAD).astype(jnp.float32), position).astype(jnp.bfloat16)
    node_values = value_new.reshape(REQS, TREE, KV, HEAD)
    scale = 1.0 / math.sqrt(HEAD)

    def one_request(packed):
        query_r, key_r, value_r, kslab, vslab, length, reach_r, valid_r = packed
        queries = query_r.reshape(TREE, KV, GROUP, HEAD).transpose(1, 2, 0, 3).reshape(KV, GROUP * TREE, HEAD).astype(jnp.float32)
        cached_keys = relayout(kslab).astype(jnp.float32)
        cached_values = relayout(vslab).astype(jnp.float32)
        scores_cache = jnp.einsum('gqd,gkd->gqk', queries, cached_keys) * scale
        live = jnp.arange(CACHE, dtype=jnp.int32) < length
        scores_cache = jnp.where(live[None, None, :], scores_cache, masked_score)
        tree_keys = key_r.transpose(1, 0, 2).astype(jnp.float32)
        tree_values = value_r.transpose(1, 0, 2).astype(jnp.float32)
        scores_tree = jnp.einsum('gqd,gkd->gqk', queries, tree_keys) * scale
        tiled = jnp.tile(reach_r, (GROUP, 1)) > 0.5
        scores_tree = jnp.where(tiled[None], scores_tree, masked_score)
        highest = jnp.maximum(lax.optimization_barrier(jnp.max(scores_cache, -1)), lax.optimization_barrier(jnp.max(scores_tree, -1)))
        probs_cache = jnp.exp(scores_cache - highest[..., None]).astype(jnp.bfloat16).astype(jnp.float32)
        probs_tree = jnp.exp(scores_tree - highest[..., None]).astype(jnp.bfloat16).astype(jnp.float32)
        totals = lax.optimization_barrier(jnp.sum(probs_cache, -1)) + lax.optimization_barrier(jnp.sum(probs_tree, -1))
        summed = jnp.einsum('gqk,gkd->gqd', probs_cache, cached_values) + jnp.einsum('gqk,gkd->gqd', probs_tree, tree_values)
        attended = (summed / totals[..., None]).astype(jnp.bfloat16)
        attended = attended.reshape(KV, GROUP, TREE, HEAD).transpose(2, 0, 1, 3).reshape(TREE, QH * HEAD)
        return attended * valid_r[:, None].astype(jnp.bfloat16)
    attended_all = lax.map(one_request, (rot_query, rot_key, node_values, key_cache, value_cache, cache_len, reach, valid_nodes))
    projected = jnp.dot(attended_all.reshape(REQS * TREE, QH * HEAD), w_out, preferred_element_type=jnp.float32)
    layer_out = (widened.reshape(REQS * TREE, D) + projected).astype(jnp.bfloat16).reshape(REQS, TREE, D)
    kv_rows = jnp.stack([rot_key.reshape(REQS, TREE, KV * HEAD), node_values.reshape(REQS, TREE, KV * HEAD)], 2)
    chosen = jax.vmap(lambda rows_of, picks: jnp.take(rows_of, picks, axis=0))(kv_rows, accepted_path)
    accepted_kv = jnp.zeros_like(chosen).at[slot_owner].set(chosen)
    return (layer_out, accepted_kv)
```

```python
import functools
import math

import jax
import jax.numpy as jnp
from jax import lax
from jax.experimental import pallas as pl
from jax.experimental.pallas import tpu as pltpu
from jax.sharding import PartitionSpec as P

GROUP = 7
SIDE = 4
epsilon = 1e-05
rope_base = 5000000.0
masked_score = -1e30
bf16 = jnp.bfloat16
f32 = jnp.float32
VMEM = pltpu.VMEM


def whole():
    return pl.BlockSpec(memory_space=VMEM)


def scalars():
    return pl.BlockSpec(memory_space=pltpu.SMEM)


def params(mib):
    return pltpu.CompilerParams(vmem_limit_bytes=mib * 2**20)


def shift_dp(block, step):
    return lax.ppermute(block, "dp", [(i, (i + step) % 16) for i in range(16)])


def other_core(block):
    return lax.ppermute(block, "dp", [(i, i ^ 1) for i in range(16)])


def shift_y(block, step):
    return lax.ppermute(block, "mp", [(i, i // 4 * 4 + (i + step) % 4) for i in range(16)])


def shift_x(block, step):
    return lax.ppermute(block, "mp", [(i, (i + 4 * step) % 16) for i in range(16)])


def partner(block):
    return lax.ppermute(block, "mp", [(i, i ^ 1) for i in range(16)])


def tree_closure(parents):
    width = parents.shape[-1]
    nodes = jnp.arange(width, dtype=jnp.int32)
    onehot = (parents[..., None] == nodes).astype(f32)
    reach = jnp.minimum(jnp.eye(width, dtype=f32) + onehot, 1.0)
    for _ in range((width - 1).bit_length()):
        small = reach.astype(bf16)
        reach = jnp.minimum(
            jnp.einsum("rij,rjk->rik", small, small, preferred_element_type=f32), 1.0
        )
    return reach


def project_kernel(order, x_ref, *refs):
    full, halves = refs[:14], refs[14:18]
    out_ref, total, inv_ref, joined = refs[18:]
    rows = out_ref.shape[0]
    half_rows = halves[0].shape[0]
    for c in range(2):
        joined[c, :half_rows] = halves[2 * c][...]
        joined[c, half_rows:] = halves[2 * c + 1][...]
    width = x_ref.shape[0] * x_ref.shape[2]

    @pl.loop(0, rows // 32)
    def _(chunk):
        at = pl.ds(pl.multiple_of(chunk * 32, 32), 32)
        squares = jnp.zeros((32, x_ref.shape[2]), f32)
        for b in range(x_ref.shape[0]):
            part = x_ref[b, at, :].astype(f32)
            squares = squares + part * part
        mean = jnp.sum(squares, -1, keepdims=True) / width
        inv_ref[at, :] = jnp.broadcast_to(lax.rsqrt(mean + epsilon), (32, 128))

    inverse = inv_ref[:, :1]
    for slot in range(16):
        block = order[slot]
        gain = x_ref[block, rows : rows + 16, :][:1].astype(f32)
        normed = (x_ref[block, :rows, :].astype(f32) * inverse * gain).astype(bf16)
        weight = full[slot][...] if slot < 14 else joined[slot - 14]
        term = jnp.dot(normed, weight, preferred_element_type=f32)
        if slot == 0:
            total[...] = term
        else:
            total[...] += term
    out_ref[...] = total[...].astype(bf16)


def project(order, gathered, blocks):
    rows = gathered.shape[1] - 16
    columns = blocks[0].shape[1]
    return pl.pallas_call(
        project_kernel,
        out_shape=jax.ShapeDtypeStruct((rows, columns), bf16),
        in_specs=[scalars()] + [whole()] * 19,
        out_specs=whole(),
        scratch_shapes=[
            pltpu.VMEM((rows, columns), f32),
            pltpu.VMEM((rows, 128), f32),
            pltpu.VMEM((2,) + blocks[0].shape, bf16),
        ],
        compiler_params=params(40),
        name="project",
    )(order, gathered, *blocks)


def attention_kernel(
    facts, own_ref, oth_ref, cos_ref, sin_ref, reach_ref, pick_ref, key_ref, value_ref,
    kept_ref, sent_ref, stats_ref, chosen_ref, scores, top,
):
    request = pl.program_id(0)
    first = facts[0] == 0
    count = facts[1 + request]
    nodes = own_ref.shape[0]
    q_cols = 448
    cosine, sine = cos_ref[...], sin_ref[...]
    own, other = own_ref[...].astype(f32), oth_ref[...].astype(f32)

    def paired(lo, hi):
        low = jnp.where(first, own[:, lo:hi], other[:, lo:hi])
        high = jnp.where(first, other[:, lo:hi], own[:, lo:hi])
        return jnp.concatenate([low, high], 1)

    def turned(u):
        return (u * cosine + pltpu.roll(u, 64, 1) * sine).astype(bf16)

    query = paired(0, q_cols)
    queries = jnp.concatenate(
        [turned(query[:, 128 * g : 128 * g + 128]) for g in range(GROUP)], 0
    )
    rot_key = turned(paired(q_cols, q_cols + 64))
    node_value = paired(q_cols + 64, q_cols + 128).astype(bf16)

    wide = rot_key.astype(f32)
    own_key = jnp.where(first, wide[:, :64], wide[:, 64:])
    kv_rows = jnp.concatenate([own_key, own[:, q_cols + 64 : q_cols + 128]], 1).astype(bf16)
    chosen_ref[0] = jnp.dot(pick_ref[0], kv_rows, preferred_element_type=f32).astype(bf16)

    span = scores.shape[2]
    rows = GROUP * nodes
    tree = lax.dot_general(queries, rot_key, (((1,), (1,)), ((), ())), preferred_element_type=f32)
    reach = jnp.concatenate([reach_ref[0]] * GROUP, 0)
    tree = jnp.where(jnp.logical_and(reach > 0.5, first), tree, masked_score)
    top[...] = jnp.broadcast_to(jnp.max(tree, -1, keepdims=True), top.shape)
    pieces = scores.shape[0]
    for c in range(pieces):

        @pl.when(count > c * span)
        def _(c=c):
            part = lax.dot_general(
                queries, key_ref[0, c * span : (c + 1) * span, :],
                (((1,), (1,)), ((), ())), preferred_element_type=f32,
            )
            live = lax.broadcasted_iota(jnp.int32, (1, span), 1) + c * span < count
            part = jnp.where(live, part, masked_score)
            scores[c] = part
            top[...] = jnp.maximum(top[...], jnp.max(part, -1, keepdims=True))

    highest = top[:, :1]
    factor = math.log2(math.e) / math.sqrt(128.0)
    ones = jnp.ones((span, 128), bf16)
    weights = jnp.where(
        jnp.logical_and(reach > 0.5, first), jnp.exp2((tree - highest) * factor), 0.0
    ).astype(bf16)
    summed = jnp.dot(
        weights, jnp.concatenate([node_value, ones[:nodes]], 1), preferred_element_type=f32
    )

    def add(c, carried):
        weights = jnp.exp2((scores[c] - highest) * factor).astype(bf16)
        at = pl.ds(pl.multiple_of(c * span, span), span)
        return carried + jnp.dot(
            weights,
            jnp.concatenate([value_ref[0, at, :], ones], 1),
            preferred_element_type=f32,
        )

    summed = lax.fori_loop(0, (count + span - 1) // span, add, summed)
    total = summed[:, 128:129]
    some = total > 0.0
    safe = jnp.where(some, total, 1.0)
    mean = summed[:, :128] / safe
    level = jnp.where(some, highest * (1.0 / math.sqrt(128.0)) + jnp.log(safe), masked_score)
    every = jnp.concatenate([mean[g * nodes : (g + 1) * nodes] for g in range(GROUP)], 1)
    low, high = every[:, :q_cols], every[:, q_cols:]
    kept_ref[...] = jnp.where(first, low, high)
    levels = jnp.concatenate(
        [level[g * nodes : (g + 1) * nodes] for g in range(GROUP)]
        + [jnp.zeros((nodes, 128 - GROUP), f32)], 1,
    )
    stats_ref[...] = levels
    coarse = levels[:, :16].astype(bf16).astype(f32)
    finer = (levels[:, :16] - coarse).astype(bf16).astype(f32)
    finest = levels[:, :16] - coarse - finer
    sent_ref[...] = jnp.concatenate(
        [jnp.where(first, high, low), coarse, finer, finest, jnp.zeros((nodes, 16), f32)], 1
    ).astype(bf16)


def attention(facts, own, other, cosine, sine, reach, pick, keys, values):
    requests, half_len, head = keys.shape
    nodes = own.shape[0] // requests
    columns = own.shape[1]

    def rows_of(width):
        return pl.BlockSpec((nodes, width), lambda r, facts: (r, 0))

    def request_of(*shape):
        return pl.BlockSpec((1,) + shape, lambda r, facts: (r, 0, 0))

    span = 512
    return pl.pallas_call(
        attention_kernel,
        grid_spec=pltpu.PrefetchScalarGridSpec(
            num_scalar_prefetch=1,
            grid=(requests,),
            in_specs=[
                rows_of(columns), rows_of(columns), rows_of(head), rows_of(head),
                request_of(nodes, nodes), request_of(*pick.shape[1:]),
                request_of(half_len, head), request_of(half_len, head),
            ],
            out_specs=[rows_of(448), rows_of(512), rows_of(128), request_of(pick.shape[1], 128)],
            scratch_shapes=[
                pltpu.VMEM((half_len // span, GROUP * nodes, span), f32),
                pltpu.VMEM((GROUP * nodes, 128), f32),
            ],
        ),
        out_shape=[
            jax.ShapeDtypeStruct((requests * nodes, 448), f32),
            jax.ShapeDtypeStruct((requests * nodes, 512), bf16),
            jax.ShapeDtypeStruct((requests * nodes, 128), f32),
            jax.ShapeDtypeStruct((requests, pick.shape[1], 128), bf16),
        ],
        compiler_params=params(28),
        name="attention",
    )(facts, own, other, cosine, sine, reach, pick, keys, values)


def combine_kernel(facts, kept_ref, stats_ref, got_ref, valid_ref, out_ref):
    first = facts[0] == 0
    got = got_ref[...].astype(f32)
    theirs = got[:, 448:464] + got[:, 464:480] + got[:, 480:496]
    ours = stats_ref[:, :16]
    highest = jnp.maximum(ours, theirs)
    own_factor = jnp.exp(ours - highest)
    other_factor = jnp.exp(theirs - highest)
    both = own_factor + other_factor

    def spread(part):
        rows = part.shape[0]
        every = jnp.concatenate(
            [jnp.broadcast_to(part[:, g : g + 1], (rows, 128)) for g in range(GROUP)], 1
        )
        return jnp.where(first, every[:, :448], every[:, 448:])

    mixed = kept_ref[...] * spread(own_factor / both) + got[:, :448] * spread(other_factor / both)
    out_ref[...] = mixed.astype(bf16) * valid_ref[...]


def combine(facts, kept, stats, got, valid):
    return pl.pallas_call(
        combine_kernel,
        out_shape=jax.ShapeDtypeStruct(kept.shape, bf16),
        in_specs=[scalars()] + [whole()] * 4,
        out_specs=whole(),
        compiler_params=params(16),
        name="combine",
    )(facts, kept, stats, got, valid)


def out_kernel(steps, place, att_ref, weight_ref, *outs):
    half = att_ref.shape[0] // 2
    x, y = place[0], place[1]
    for k, step in enumerate(steps):
        for along in range(SIDE):
            block = along * SIDE + lax.rem(y + step, SIDE)
            outs[2 * k][along] = jnp.dot(
                att_ref[:half, :], weight_ref[block], preferred_element_type=f32
            ).astype(outs[2 * k].dtype)
        for along in range(SIDE):
            block = lax.rem(x + step, SIDE) * SIDE + along
            outs[2 * k + 1][along] = jnp.dot(
                att_ref[half:, :], weight_ref[block], preferred_element_type=f32
            ).astype(outs[2 * k + 1].dtype)


def out_terms(steps, place, att, weights):
    half, columns = att.shape[0] // 2, weights.shape[2]
    return pl.pallas_call(
        functools.partial(out_kernel, steps),
        out_shape=[
            jax.ShapeDtypeStruct((SIDE, half, columns), bf16 if step else f32)
            for step in steps
            for _ in range(2)
        ],
        in_specs=[scalars(), whole(), whole()],
        out_specs=[whole()] * (2 * len(steps)),
        compiler_params=params(24),
        name="out_terms",
    )(place, att, weights)


def partial_kernel(place, own_ref, *refs):
    got, outs = refs[:3], refs[3:]
    for step in range(SIDE):
        at = lax.rem(place[0] + step, SIDE)
        value = own_ref[at]
        for part in got:
            value = value + part[at].astype(f32)
        outs[step][...] = value.astype(outs[step].dtype)


def partial_sums(place, own, got):
    shape = own.shape[1:]
    return pl.pallas_call(
        partial_kernel,
        out_shape=[jax.ShapeDtypeStruct(shape, bf16 if step else f32) for step in range(SIDE)],
        in_specs=[scalars()] + [whole()] * 4,
        out_specs=[whole()] * SIDE,
        compiler_params=params(16),
        name="partial_sums",
    )(place, own, *got)


def final_kernel(hidden_ref, *refs):
    out_ref = refs[-1]
    half = hidden_ref.shape[0] // 2
    for h in range(2):
        own, *got = refs[4 * h : 4 * h + 4]
        value = own[...]
        for part in got:
            value = value + part[...].astype(f32)
        at = slice(h * half, (h + 1) * half)
        out_ref[at] = (hidden_ref[at].astype(f32) + value).astype(bf16)


def final(hidden, parts):
    return pl.pallas_call(
        final_kernel,
        out_shape=jax.ShapeDtypeStruct(hidden.shape, bf16),
        in_specs=[whole()] * 9,
        out_specs=whole(),
        compiler_params=params(16),
        name="final",
    )(hidden, *parts)


def shards(
    hidden_in,
    norm_gain,
    w_query,
    w_key,
    w_value,
    w_out,
    key_cache,
    value_cache,
    cache_len,
    tree_parent,
    valid_nodes,
    accepted_path,
    slot_owner,
):
    req_dev, tree_size, part_width = hidden_in.shape
    row_count = req_dev * tree_size
    head_dim = key_cache.shape[-1]
    half_len = key_cache.shape[3]
    dp, mp = lax.axis_index("dp"), lax.axis_index("mp")
    half_index = mp % 2
    hidden = hidden_in.reshape(row_count, part_width)

    weights = jnp.concatenate([w_query, w_key, w_value], 1)
    packed = jnp.concatenate([hidden, jnp.broadcast_to(norm_gain[None], (16, part_width))], 0)
    gathered = lax.all_gather(packed, "mp")

    full, order = [weights, other_core(weights)], [dp, dp ^ 1]
    up = down = weights
    for step in range(1, 4):
        up, down = shift_dp(up, 2), shift_dp(down, -2)
        full += [up, down, other_core(up), other_core(down)]
        order += [dp - 2 * step, dp + 2 * step, (dp ^ 1) - 2 * step, (dp ^ 1) + 2 * step]
    cut = weights.shape[0] // 2
    up, down = shift_dp(up[:cut], 2), shift_dp(down[cut:], -2)
    halves = [up, down, other_core(up), other_core(down)]
    order += [dp + 8, (dp ^ 1) + 8]
    order = (jnp.stack(order) % 16).astype(jnp.int32)

    reach = tree_closure(tree_parent)
    depth = jnp.sum(reach, -1) - 1.0
    position = (cache_len[:, None].astype(f32) + depth).reshape(row_count, 1)
    half_dim = head_dim // 2
    inverse = jnp.exp(
        jnp.arange(half_dim, dtype=f32) * (-2.0 * math.log(rope_base) / head_dim)
    )
    angles = position * inverse
    cosine, sine = jnp.cos(angles), jnp.sin(angles)
    cosine = jnp.concatenate([cosine, cosine], -1)
    sine = jnp.concatenate([-sine, sine], -1)
    pick = (
        jnp.pad(accepted_path, ((0, 0), (0, 8)))[..., None]
        == jnp.arange(tree_size, dtype=jnp.int32)
    ).astype(bf16)
    counts = jnp.clip(cache_len - half_index * half_len, 0, half_len)
    facts = jnp.concatenate([half_index[None], counts]).astype(jnp.int32)
    valid = valid_nodes.reshape(row_count, 1).astype(bf16)
    place = jnp.stack([mp // SIDE, mp % SIDE]).astype(jnp.int32)

    own = project(order, gathered, full + halves)
    other = partner(own)

    w_out_late, _ = lax.optimization_barrier((w_out, gathered[0, 0, 0]))
    w_out_all = lax.all_gather(w_out_late, "dp")

    kept, sent, stats, chosen = attention(
        facts, own, other, cosine, sine, reach, pick, key_cache[:, 0, 0], value_cache[:, 0, 0]
    )
    attended = combine(facts, kept, stats, partner(sent), valid)

    a2, b2, a1, b1 = out_terms((2, 1), place, attended, w_out_all)
    a3, b3, a0, b0 = out_terms((3, 0), place, attended, w_out_all)
    got_a = [shift_y(a2, 2), shift_y(a1, 1), shift_y(a3, 3)]
    got_b = [shift_x(b2, 2), shift_x(b1, 1), shift_x(b3, 3)]
    a = partial_sums(place[:1], a0, got_a)
    b = partial_sums(place[1:], b0, got_b)
    parts = [a[0]] + [shift_x(a[s], s) for s in (2, 1, 3)]
    parts += [b[0]] + [shift_y(b[s], s) for s in (2, 1, 3)]
    layer_out = final(hidden, parts).reshape(req_dev, tree_size, part_width)

    every_row = lax.all_gather(chosen[:, : accepted_path.shape[1]], "dp", axis=0, tiled=True)
    total_reqs = slot_owner.shape[0]
    my_slots = dp * req_dev + jnp.arange(req_dev, dtype=jnp.int32)
    senders = (slot_owner[None, :] == my_slots[:, None]).astype(bf16)
    accepted_kv = (
        jnp.dot(senders, every_row.reshape(total_reqs, -1), preferred_element_type=f32)
        .astype(bf16)
        .reshape(req_dev, accepted_path.shape[1], 2, -1)
    )
    return (layer_out, accepted_kv)


def solution(mesh):
    placed = (
        P("dp", None, "mp"),
        P("mp"),
        P("dp", "mp"),
        P("dp", "mp"),
        P("dp", "mp"),
        P("mp", "dp"),
        P("dp", "mp", None, None, None),
        P("dp", "mp", None, None, None),
        P("dp"),
        P("dp", None),
        P("dp", None),
        P("dp", None),
        P(),
    )
    return jax.shard_map(
        shards,
        mesh=mesh,
        in_specs=placed,
        out_specs=(P("dp", None, "mp"), P("dp", None, None, "mp")),
        check_vma=False,
    )
```

```python
import functools
import math

import jax
import jax.numpy as jnp
from jax import lax
from jax.experimental import pallas as pl
from jax.experimental.pallas import tpu as pltpu
from jax.sharding import PartitionSpec as P

GROUP = 7
SIDE = 4
epsilon = 1e-05
rope_base = 5000000.0
masked_score = -1e30
bf16 = jnp.bfloat16
f32 = jnp.float32
VMEM = pltpu.VMEM


def whole():
    return pl.BlockSpec(memory_space=VMEM)


def scalars():
    return pl.BlockSpec(memory_space=pltpu.SMEM)


def params(mib):
    return pltpu.CompilerParams(vmem_limit_bytes=mib * 2**20)


DP, CORES, Z = 16, 2, 8
WEIGHT_CHAINS = 2
LAG = 3
EARLY = (8, 12)


def moved(block, target):
    route = []
    for d in range(DP):
        for m in range(SIDE * SIDE):
            z, core, x, y = target(d // CORES, d % CORES, m // SIDE, m % SIDE)
            to = (z % Z * CORES + core) * SIDE * SIDE + x % SIDE * SIDE + y % SIDE
            route.append((d * SIDE * SIDE + m, to))
    return lax.ppermute(block, ("dp", "mp"), route)


def other_core(block):
    return moved(block, lambda z, c, x, y: (z, c ^ 1, x, y))


def along_z(block):
    return moved(block, lambda z, c, x, y: (z + 1 - 2 * c, c, x, y))


def first_axis(block, step):
    return moved(block, lambda z, c, x, y: (z, c, x, y + step) if c == 0 else (z, c, x + step, y))


def second_axis(block, step):
    return moved(block, lambda z, c, x, y: (z, c, x + step, y) if c == 0 else (z, c, x, y + step))


def partner(block):
    return moved(block, lambda z, c, x, y: (z, c, x, y ^ 1))


def tree_closure(parents):
    width = parents.shape[-1]
    nodes = jnp.arange(width, dtype=jnp.int32)
    onehot = (parents[..., None] == nodes).astype(f32)
    reach = jnp.minimum(jnp.eye(width, dtype=f32) + onehot, 1.0)
    for _ in range((width - 1).bit_length()):
        small = reach.astype(bf16)
        reach = jnp.minimum(
            jnp.einsum("rij,rjk->rik", small, small, preferred_element_type=f32), 1.0
        )
    return reach


def dense_tiles(array, width=448):
    half = array.shape[0] // 2
    rest = array[:, 384:width]
    folded = jnp.concatenate([rest[:half].astype(f32), rest[half:].astype(f32)], 1)
    return [array[:, 128 * t : 128 * t + 128] for t in range(3)] + [folded.astype(array.dtype)]


def unfolded(tile):
    wide = tile.astype(f32)
    return jnp.concatenate([wide[:, :64], wide[:, 64:]], 0).astype(tile.dtype)


def store_tiles(ref, base, array):
    rows = array.shape[0]
    for t, tile in enumerate(dense_tiles(array)):
        ref[base + t * rows : base + t * rows + tile.shape[0], :] = tile.astype(ref.dtype)


def pack_kernel(hidden_ref, gain_ref, query_ref, key_ref, value_ref, out_ref, x_ref, w_ref, o_ref):
    rows = hidden_ref.shape[0]
    store_tiles(x_ref, 0, hidden_ref[...])
    x_ref[rows * 7 // 2 :, :] = gain_ref[...]
    store_tiles(w_ref, 0, query_ref[...])
    both = jnp.concatenate([key_ref[...], value_ref[...]], 0)
    store_tiles(w_ref, query_ref.shape[0] * 7 // 2, both)
    store_tiles(o_ref, 0, out_ref[...])


def pack(hidden, gain, w_query, w_key, w_value, w_out):
    rows, width = hidden.shape
    def dense(n):
        return jax.ShapeDtypeStruct((n, 128), bf16)

    return pl.pallas_call(
        pack_kernel,
        out_shape=[dense(rows * 7 // 2 + 32), dense(width * 9 // 2), dense(width * 7 // 2)],
        in_specs=[whole()] * 6,
        out_specs=[whole()] * 3,
        compiler_params=params(16),
        name="pack",
    )(hidden, gain, w_query, w_key, w_value, w_out)


def norm_kernel(place, *refs):
    arrived, (out_ref, squares, folds, inverse) = refs[:5], refs[5:]
    slots = [(arrived[j], i) for j in range(3) for i in range(SIDE)]
    slots += [(arrived[3 + i // 2], i % 2) for i in range(SIDE)]
    rows = out_ref.shape[1]
    half = rows // 2

    @pl.loop(0, rows // 32)
    def _(chunk):
        total = jnp.zeros((32, 128), f32)
        for ref, i in slots:
            for t in range(3):
                at = pl.ds(pl.multiple_of(t * rows + chunk * 32, 32), 32)
                part = ref[i, at, :].astype(f32)
                total = total + part * part
        squares[pl.ds(pl.multiple_of(chunk * 32, 32), 32), :] = total

    @pl.loop(0, half // 32)
    def _(chunk):
        total = jnp.zeros((32, 128), f32)
        at = pl.ds(pl.multiple_of(3 * rows + chunk * 32, 32), 32)
        for ref, i in slots:
            part = ref[i, at, :].astype(f32)
            total = total + part * part
        folds[pl.ds(pl.multiple_of(chunk * 32, 32), 32), :] = total

    rest = folds[...]
    rest = jnp.concatenate(
        [jnp.sum(rest[:, :64], -1, keepdims=True), jnp.sum(rest[:, 64:], -1, keepdims=True)], 0
    )
    mean = (jnp.sum(squares[...], -1, keepdims=True) + rest) / (16 * 448)
    inverse[...] = jnp.broadcast_to(lax.rsqrt(mean + epsilon), inverse.shape)
    for slot, (ref, i) in enumerate(slots):
        block = place[slot]
        gain = ref[i, 3 * rows + half : 3 * rows + half + 16, :].astype(f32)
        for t in range(3):
            part = ref[i, t * rows : (t + 1) * rows, :].astype(f32)
            out_ref[block, :, 128 * t : 128 * t + 128] = (
                part * inverse[...] * gain[t : t + 1]
            ).astype(bf16)
        part = unfolded(ref[i, 3 * rows : 3 * rows + half, :]).astype(f32)
        out_ref[block, :, 384:448] = (part * inverse[:, :64] * gain[3:4, :64]).astype(bf16)


def norm(place, arrived, rows):
    return pl.pallas_call(
        norm_kernel,
        out_shape=jax.ShapeDtypeStruct((16, rows, 448), bf16),
        in_specs=[scalars()] + [whole()] * 5,
        out_specs=whole(),
        scratch_shapes=[
            pltpu.VMEM((rows, 128), f32),
            pltpu.VMEM((rows // 2, 128), f32),
            pltpu.VMEM((rows, 128), f32),
        ],
        compiler_params=params(24),
        cost_estimate=pl.CostEstimate(flops=16 * 10**6, bytes_accessed=8 * 10**6, transcendentals=0),
        name="norm",
    )(place, *arrived)


def weight_rows(chains, start, stop):
    each, found = chains[0].shape[0], []
    for c, ref in enumerate(chains):
        lo, hi = max(start, c * each), min(stop, (c + 1) * each)
        if lo < hi:
            found.append(ref[lo - c * each : hi - c * each, :])
    return found[0] if len(found) == 1 else jnp.concatenate(found, 0)


def tiles_of(chains, base, rows):
    parts = [weight_rows(chains, base + t * rows, base + (t + 1) * rows) for t in range(3)]
    last = weight_rows(chains, base + 3 * rows, base + 3 * rows + rows // 2)
    return jnp.concatenate(parts + [unfolded(last)], 1)


def project_kernel(count, start, last, order, normed_ref, *refs):
    per = WEIGHT_CHAINS
    weights, rest = refs[: count * per], refs[count * per :]
    if start == 0:
        outs = rest
        total = None
    else:
        total, outs = rest[0][...], rest[1:]
    for k in range(count):
        chains = weights[k * per : (k + 1) * per]
        normed = normed_ref[order[start + k]]
        query = jnp.dot(normed, tiles_of(chains, 0, 448), preferred_element_type=f32)
        pair = lax.dot_general(
            normed, tiles_of(chains, 1568, 128), (((1,), (1,)), ((), ())), preferred_element_type=f32
        )
        term = jnp.concatenate([query, jnp.zeros((query.shape[0], 64), f32), pair], 1)
        total = term if total is None else total + term
    if last:
        half = total.shape[0] // 2
        rounded = total.astype(bf16)
        for h in range(2):
            outs[h][...] = rounded[h * half : (h + 1) * half]
    else:
        outs[0][...] = total


def project(start, last, order, normed, slots, total=None):
    rows = normed.shape[1]
    count = len(slots)
    flat = [chain for slot in slots for chain in slot]
    extra = [] if total is None else [total]
    if last:
        shape = [jax.ShapeDtypeStruct((rows // 2, 640), bf16)] * 2
    else:
        shape = [jax.ShapeDtypeStruct((rows, 640), f32)]
    return pl.pallas_call(
        functools.partial(project_kernel, count, start, last),
        out_shape=shape,
        in_specs=[scalars()] + [whole()] * (1 + len(flat) + len(extra)),
        out_specs=[whole()] * len(shape),
        compiler_params=params(32),
        cost_estimate=pl.CostEstimate(
            flops=2 * rows * 448 * 576 * count, bytes_accessed=10**6 * count, transcendentals=0
        ),
        name="project",
    )(order, normed, *flat, *extra)


def attention_kernel(
    facts, own_ref, oth_ref, cos_ref, sin_ref, reach_ref, pick_ref, key_ref, value_ref,
    kept_ref, sent_ref, stats_ref, chosen_ref, scores,
):
    request = pl.program_id(0)
    first = facts[0] == 0
    count = facts[1 + request]
    nodes = own_ref.shape[0]
    q_cols = 448
    cosine, sine = cos_ref[...], sin_ref[...]
    own, other = own_ref[...].astype(f32), oth_ref[...].astype(f32)

    def paired(lo, hi):
        low = jnp.where(first, own[:, lo:hi], other[:, lo:hi])
        high = jnp.where(first, other[:, lo:hi], own[:, lo:hi])
        return jnp.concatenate([low, high], 1)

    def turned(u):
        return (u * cosine + pltpu.roll(u, 64, 1) * sine).astype(bf16)

    query = paired(0, q_cols)
    queries = jnp.concatenate(
        [turned(query[:, 128 * g : 128 * g + 128]) for g in range(GROUP)], 0
    )
    rot_key = turned(paired(512, 576))
    node_value = paired(576, 640).astype(bf16)

    wide = rot_key.astype(f32)
    own_key = jnp.where(first, wide[:, :64], wide[:, 64:])
    kv_rows = jnp.concatenate([own_key, own[:, 576:640]], 1).astype(bf16)
    chosen_ref[0] = jnp.dot(pick_ref[0], kv_rows, preferred_element_type=f32).astype(bf16)

    pieces, rows, span = scores.shape
    nt = (((1,), (1,)), ((), ()))
    tree = lax.dot_general(queries, rot_key, nt, preferred_element_type=f32)
    reach = jnp.concatenate([reach_ref[0]] * GROUP, 0)
    tree = jnp.where(jnp.logical_and(reach > 0.5, first), tree, masked_score)
    highest = jnp.full((rows, 128), masked_score, f32)
    for c in range(pieces):
        part = lax.dot_general(
            queries, key_ref[0, c * span : (c + 1) * span, :], nt, preferred_element_type=f32
        )
        live = lax.broadcasted_iota(jnp.int32, (1, span), 1) + c * span < count
        part = jnp.where(live, part, masked_score)
        scores[c] = part
        for t in range(span // 128):
            highest = jnp.maximum(highest, part[:, 128 * t : 128 * t + 128])
    highest = jnp.maximum(
        jnp.max(highest, -1, keepdims=True), jnp.max(tree, -1, keepdims=True)
    )

    factor = math.log2(math.e) / math.sqrt(128.0)
    ones = jnp.ones((span, 128), bf16)
    weights = jnp.exp2((tree - highest) * factor).astype(bf16)
    summed = jnp.dot(
        weights, jnp.concatenate([node_value, ones[:nodes]], 1), preferred_element_type=f32
    )
    for c in range(pieces):
        weights = jnp.exp2((scores[c] - highest) * factor).astype(bf16)
        values = jnp.concatenate([value_ref[0, c * span : (c + 1) * span, :], ones], 1)
        summed = summed + jnp.dot(weights, values, preferred_element_type=f32)

    total = summed[:, 128:129]
    mean = summed[:, :128] / total
    some = jnp.logical_or(first, count > 0)
    level = jnp.where(some, highest * (1.0 / math.sqrt(128.0)) + jnp.log(total), masked_score)
    every = jnp.concatenate([mean[g * nodes : (g + 1) * nodes] for g in range(GROUP)], 1)
    low, high = every[:, :q_cols], every[:, q_cols:]
    kept_ref[...] = jnp.where(first, low, high)
    levels = jnp.concatenate(
        [level[g * nodes : (g + 1) * nodes] for g in range(GROUP)]
        + [jnp.zeros((nodes, 128 - GROUP), f32)], 1,
    )
    stats_ref[...] = levels
    coarse = levels[:, :16].astype(bf16).astype(f32)
    finer = (levels[:, :16] - coarse).astype(bf16).astype(f32)
    finest = levels[:, :16] - coarse - finer
    sent_ref[...] = jnp.concatenate(
        [jnp.where(first, high, low), coarse, finer, finest, jnp.zeros((nodes, 16), f32)], 1
    ).astype(bf16)


def attention(half, facts, own, other, cosine, sine, reach, pick, keys, values):
    half_len, head = keys.shape[-2:]
    requests = keys.shape[0] // 2
    nodes = own.shape[0] // requests
    columns = own.shape[1]
    base = half * requests

    def rows_of(width, at=0):
        return pl.BlockSpec((nodes, width), lambda r, facts: (at + r, 0))

    def request_of(*shape, at=0):
        return pl.BlockSpec((1,) + shape, lambda r, facts: (at + r, 0, 0))

    span = 512
    return pl.pallas_call(
        attention_kernel,
        grid_spec=pltpu.PrefetchScalarGridSpec(
            num_scalar_prefetch=1,
            grid=(requests,),
            in_specs=[
                rows_of(columns), rows_of(columns), rows_of(head, base), rows_of(head, base),
                request_of(nodes, nodes, at=base), request_of(*pick.shape[1:], at=base),
                request_of(half_len, head, at=base), request_of(half_len, head, at=base),
            ],
            out_specs=[rows_of(448), rows_of(512), rows_of(128), request_of(pick.shape[1], 128)],
            scratch_shapes=[pltpu.VMEM((half_len // span, GROUP * nodes, span), f32)],
        ),
        out_shape=[
            jax.ShapeDtypeStruct((requests * nodes, 448), f32),
            jax.ShapeDtypeStruct((requests * nodes, 512), bf16),
            jax.ShapeDtypeStruct((requests * nodes, 128), f32),
            jax.ShapeDtypeStruct((requests, pick.shape[1], 128), bf16),
        ],
        compiler_params=params(28),
        cost_estimate=pl.CostEstimate(
            flops=requests * 448 * 2112 * 128 * 6,
            bytes_accessed=requests * 2**20,
            transcendentals=requests * 448 * 2112,
        ),
        name="attention",
    )(facts, own, other, cosine, sine, reach, pick, keys, values)


def out_kernel(place, kept_ref, stats_ref, got_ref, valid_ref, *refs):
    weights, outs = refs[:16], refs[16:]
    first = place[32] == 0
    got = got_ref[...].astype(f32)
    theirs = got[:, 448:464] + got[:, 464:480] + got[:, 480:496]
    ours = stats_ref[:, :16]
    highest = jnp.maximum(ours, theirs)
    own_factor = jnp.exp(ours - highest)
    other_factor = jnp.exp(theirs - highest)
    both = own_factor + other_factor

    def spread(part):
        rows = part.shape[0]
        every = jnp.concatenate(
            [jnp.broadcast_to(part[:, g : g + 1], (rows, 128)) for g in range(GROUP)], 1
        )
        return jnp.where(first, every[:, :448], every[:, 448:])

    mixed = kept_ref[...] * spread(own_factor / both) + got[:, :448] * spread(other_factor / both)
    attended = mixed.astype(bf16) * valid_ref[...]
    for slot, weight in enumerate(weights):
        terms = jnp.dot(attended, tiles_of([weight], 0, 448), preferred_element_type=f32)
        tiles = dense_tiles(terms)
        along = place[16 + slot]
        for step, out in enumerate(outs):

            @pl.when(place[slot] == step)
            def _(out=out, tiles=tiles, along=along):
                rows = tiles[0].shape[0]
                for t, tile in enumerate(tiles):
                    out[along, t * rows : t * rows + tile.shape[0], :] = tile.astype(out.dtype)


def out_terms(place, kept, stats, got, valid, weights):
    rows = kept.shape[0] * 7 // 2
    return pl.pallas_call(
        out_kernel,
        out_shape=[
            jax.ShapeDtypeStruct((SIDE, rows, 128), bf16 if step else f32) for step in range(SIDE)
        ],
        in_specs=[scalars()] + [whole()] * 20,
        out_specs=[whole()] * SIDE,
        compiler_params=params(24),
        cost_estimate=pl.CostEstimate(
            flops=2 * kept.shape[0] * 448 * 7168, bytes_accessed=9 * 10**6, transcendentals=0
        ),
        name="out_terms",
    )(place, kept, stats, got, valid, *weights)


def partial_kernel(place, own_ref, *refs):
    got, outs = refs[:3], refs[3:]
    for step in range(SIDE):
        at = lax.rem(place[0] + step, SIDE)
        value = own_ref[at]
        for part in got:
            value = value + part[at].astype(f32)
        outs[step][...] = value.astype(outs[step].dtype)


def partial_sums(place, own, got):
    shape = own.shape[1:]
    return pl.pallas_call(
        partial_kernel,
        out_shape=[jax.ShapeDtypeStruct(shape, bf16 if step else f32) for step in range(SIDE)],
        in_specs=[scalars()] + [whole()] * 4,
        out_specs=[whole()] * SIDE,
        compiler_params=params(16),
        name="partial_sums",
    )(place, own, *got)


def final_kernel(hidden_ref, *refs):
    out_ref = refs[-1]
    half = hidden_ref.shape[0] // 2
    for h in range(2):
        own, *got = refs[SIDE * h : SIDE * h + SIDE]
        value = own[...]
        for part in got:
            value = value + part[...].astype(f32)
        at = slice(h * half, (h + 1) * half)
        dense = jnp.concatenate(
            [value[t * half : (t + 1) * half] for t in range(3)] + [unfolded(value[3 * half :])], 1
        )
        out_ref[at] = (hidden_ref[at].astype(f32) + dense).astype(bf16)


def final(hidden, parts):
    return pl.pallas_call(
        final_kernel,
        out_shape=jax.ShapeDtypeStruct(hidden.shape, bf16),
        in_specs=[whole()] * 9,
        out_specs=whole(),
        compiler_params=params(16),
        name="final",
    )(hidden, *parts)


def after(value, *others):
    return lax.optimization_barrier((value,) + tuple(o[(slice(0, 1),) * o.ndim] for o in others))[0]


def shards(
    hidden_in,
    norm_gain,
    w_query,
    w_key,
    w_value,
    w_out,
    key_cache,
    value_cache,
    cache_len,
    tree_parent,
    valid_nodes,
    accepted_path,
    slot_owner,
):
    req_dev, tree_size, part_width = hidden_in.shape
    row_count = req_dev * tree_size
    head_dim = key_cache.shape[-1]
    half_len = key_cache.shape[3]
    dp, mp = lax.axis_index("dp"), lax.axis_index("mp")
    z, core = dp // CORES, dp % CORES
    x, y = mp // SIDE, mp % SIDE
    me_first, me_second = jnp.where(core == 0, y, x), jnp.where(core == 0, x, y)
    half_index = mp % 2
    hidden = hidden_in.reshape(row_count, part_width)

    gain = jnp.pad(jnp.pad(norm_gain, (0, 64)).reshape(4, 128), ((0, 28), (0, 0)))
    packed, weights, out_weights = pack(hidden, gain, w_query, w_key.T, w_value.T, w_out)

    cut = packed.shape[0] // 2
    before, behind = first_axis(packed, 1), first_axis(packed, -1)
    across = jnp.concatenate([first_axis(before[:cut], 1), first_axis(behind[cut:], -1)])
    line = jnp.stack([packed, before, behind, across])
    before, behind = second_axis(line, 1), second_axis(line, -1)
    arrived = [line, before, behind, second_axis(before[:2], 1), second_axis(behind[2:], -1)]
    offsets = (0, -1, 1, 2)
    near = [(me_first + o) % SIDE for o in offsets]
    far = [(me_second + o) % SIDE for o in offsets]
    blocks = jnp.stack(
        [jnp.where(core == 0, s * SIDE + f, f * SIDE + s) for s in far for f in near]
    ).astype(jnp.int32)

    each = weights.shape[0] // WEIGHT_CHAINS
    chains = [weights[c * each : (c + 1) * each] for c in range(WEIGHT_CHAINS)]
    slots, marks = [], []
    for step in range(Z):
        if step:
            chains = [along_z(chain) for chain in chains]
        marks.append(chains[0])
        slots += [chains, [other_core(chain) for chain in chains]]
    sign = 1 - 2 * core
    order = []
    for step in range(Z):
        order += [
            (z - step * sign) % Z * CORES + core, (z + step * sign) % Z * CORES + 1 - core
        ]
    order = jnp.stack(order).astype(jnp.int32)

    chain = after(out_weights, marks[LAG]) if LAG else out_weights
    out_blocks = []
    for step in range(Z):
        if step:
            chain = along_z(chain)
        out_blocks += [chain, other_core(chain)]
    out_x, out_y = order // SIDE, order % SIDE
    out_first = jnp.where(core == 0, out_y, out_x)
    out_second = jnp.where(core == 0, out_x, out_y)
    place = jnp.concatenate(
        [(out_first - me_first) % SIDE, out_second, half_index[None]]
    ).astype(jnp.int32)

    reach = tree_closure(tree_parent)
    depth = jnp.sum(reach, -1) - 1.0
    position = (cache_len[:, None].astype(f32) + depth).reshape(row_count, 1)
    half_dim = head_dim // 2
    inverse = jnp.exp(
        jnp.arange(half_dim, dtype=f32) * (-2.0 * math.log(rope_base) / head_dim)
    )
    angles = position * inverse
    cosine, sine = jnp.cos(angles), jnp.sin(angles)
    cosine = jnp.concatenate([cosine, cosine], -1)
    sine = jnp.concatenate([-sine, sine], -1)
    picks = accepted_path.shape[1]
    pick = (
        jnp.pad(accepted_path, ((0, 0), (0, 16 - picks)))[..., None]
        == jnp.arange(tree_size, dtype=jnp.int32)
    ).astype(bf16)
    counts = jnp.clip(cache_len - half_index * half_len, 0, half_len)
    valid = valid_nodes.reshape(row_count, 1).astype(bf16)

    normed = norm(blocks, arrived, row_count)
    bounds = (0,) + EARLY + (len(slots),)
    total = None
    for lo, hi in zip(bounds[:-1], bounds[1:]):
        total = project(
            lo, hi == len(slots), order, normed, slots[lo:hi], total and total[0]
        )

    half_rows = row_count // 2
    sums, chosen = [], []
    for half in range(2):
        own = total[half]
        at = slice(half * half_rows, (half + 1) * half_rows)
        group = slice(half * req_dev // 2, (half + 1) * req_dev // 2)
        facts = jnp.concatenate([half_index[None], counts[group]]).astype(jnp.int32)
        kept, sent, stats, rows = attention(
            half, facts, own, partner(own), cosine, sine, reach, pick,
            key_cache[:, 0, 0], value_cache[:, 0, 0],
        )
        chosen.append(rows[:, :picks])
        terms = out_terms(place, kept, stats, partner(sent), valid[at], out_blocks)
        sums.append((terms[0], [first_axis(terms[s], s) for s in (2, 1, 3)]))
    parts = []
    for own, got in sums:
        mine = partial_sums(me_second[None].astype(jnp.int32), own, got)
        parts += [mine[0]] + [second_axis(mine[s], s) for s in (2, 1, 3)]
    layer_out = final(hidden, parts).reshape(req_dev, tree_size, part_width)

    every_row = jnp.concatenate(chosen)[None]
    for bit in range(4):
        def flipped(z, c, x, y, bit=bit):
            d = (z * CORES + c) ^ 1 << bit
            return d // CORES, d % CORES, x, y

        every_row = jnp.concatenate([every_row, moved(every_row, flipped)])
    total_reqs = slot_owner.shape[0]
    requests = jnp.arange(total_reqs, dtype=jnp.int32)
    sender = (dp ^ requests // req_dev) * req_dev + requests % req_dev
    owner = jnp.sum(jnp.where(sender[:, None] == requests, slot_owner[None, :], 0), 1)
    my_slots = dp * req_dev + jnp.arange(req_dev, dtype=jnp.int32)
    senders = (owner[None, :] == my_slots[:, None]).astype(bf16)
    accepted_kv = (
        jnp.dot(senders, every_row.reshape(total_reqs, -1), preferred_element_type=f32)
        .astype(bf16)
        .reshape(req_dev, picks, 2, -1)
    )
    return (layer_out, accepted_kv)


def solution(mesh):
    placed = (
        P("dp", None, "mp"),
        P("mp"),
        P("dp", "mp"),
        P("dp", "mp"),
        P("dp", "mp"),
        P("mp", "dp"),
        P("dp", "mp", None, None, None),
        P("dp", "mp", None, None, None),
        P("dp"),
        P("dp", None),
        P("dp", None),
        P("dp", None),
        P(),
    )
    return jax.shard_map(
        shards,
        mesh=mesh,
        in_specs=placed,
        out_specs=(P("dp", None, "mp"), P("dp", None, None, "mp")),
        check_vma=False,
    )
```

```python
import functools
import math

import jax
import jax.numpy as jnp
from jax import lax
from jax.experimental import pallas as pl
from jax.experimental.pallas import tpu as pltpu
from jax.sharding import PartitionSpec as P

GROUP = 7
SIDE = 4
epsilon = 1e-05
rope_base = 5000000.0
masked_score = -1e30
bf16 = jnp.bfloat16
f32 = jnp.float32
VMEM = pltpu.VMEM


def whole():
    return pl.BlockSpec(memory_space=VMEM)


def scalars():
    return pl.BlockSpec(memory_space=pltpu.SMEM)


def params(mib):
    return pltpu.CompilerParams(vmem_limit_bytes=mib * 2**20)


DP, CORES, Z = 16, 2, 8
BLOCKS = 16
KNOWN = (10, 14)


def moved(block, target):
    route = []
    for d in range(DP):
        for m in range(SIDE * SIDE):
            z, core, x, y = target(d // CORES, d % CORES, m // SIDE, m % SIDE)
            to = (z % Z * CORES + core) * SIDE * SIDE + x % SIDE * SIDE + y % SIDE
            route.append((d * SIDE * SIDE + m, to))
    return lax.ppermute(block, ("dp", "mp"), route)


def other_core(block):
    return moved(block, lambda z, c, x, y: (z, c ^ 1, x, y))


def along_z(block, step):
    return moved(block, lambda z, c, x, y: (z + step, c, x, y))


def first_axis(block, step):
    return moved(block, lambda z, c, x, y: (z, c, x, y + step) if c == 0 else (z, c, x + step, y))


def second_axis(block, step):
    return moved(block, lambda z, c, x, y: (z, c, x + step, y) if c == 0 else (z, c, x, y + step))


def partner(block):
    return moved(block, lambda z, c, x, y: (z, c, x, y ^ 1))


def tree_closure(parents):
    width = parents.shape[-1]
    nodes = jnp.arange(width, dtype=jnp.int32)
    onehot = (parents[..., None] == nodes).astype(f32)
    reach = jnp.minimum(jnp.eye(width, dtype=f32) + onehot, 1.0)
    for _ in range((width - 1).bit_length()):
        small = reach.astype(bf16)
        reach = jnp.minimum(
            jnp.einsum("rij,rjk->rik", small, small, preferred_element_type=f32), 1.0
        )
    return reach


def unfolded(tile):
    wide = tile.astype(f32)
    return jnp.concatenate([wide[:, :64], wide[:, 64:]], 0).astype(tile.dtype)


def folded(array):
    half = array.shape[0] // 2
    wide = array.astype(f32)
    return jnp.concatenate([wide[:half], wide[half:]], 1).astype(array.dtype)


def pack_kernel(
    hidden_ref, gain_ref, query_ref, key_ref, value_ref, out_ref, x_ref, w_ref, o1_ref, o2_ref
):
    rows = hidden_ref.shape[0]
    for t in range(3):
        x_ref[t * rows : (t + 1) * rows, :] = hidden_ref[:, 128 * t : 128 * t + 128]
    x_ref[3 * rows : 3 * rows + rows // 2, :] = folded(hidden_ref[:, 384:448])
    x_ref[3 * rows + rows // 2 :, :] = gain_ref[...]
    w_ref[:448, :384] = query_ref[:, :384]
    w_ref[:448, 384:] = jnp.concatenate(
        [query_ref[:, 384:448].astype(f32), key_ref[...].astype(f32)], 1
    ).astype(bf16)
    w_ref[448:, :] = jnp.concatenate([value_ref[...].astype(f32), jnp.zeros((64, 64), f32)], 1).astype(bf16)
    o1_ref[:448, :] = out_ref[:, :128]
    o1_ref[448:, :] = out_ref[:, 128:256]
    o2_ref[:448, :] = out_ref[:, 256:384]
    o2_ref[448:, :] = folded(out_ref[:, 384:448])


def pack(hidden, gain, w_query, w_key, w_value, w_out):
    rows = hidden.shape[0]

    def dense(n, width=128):
        return jax.ShapeDtypeStruct((n, width), bf16)

    return pl.pallas_call(
        pack_kernel,
        out_shape=[dense(rows * 7 // 2 + 32), dense(512, 512), dense(896), dense(672)],
        in_specs=[whole()] * 6,
        out_specs=[whole()] * 4,
        compiler_params=params(56),
        name="pack",
    )(hidden, gain, w_query, w_key, w_value, w_out)


def norm_kernel(x_ref, out_ref, squares, folds, inverse):
    rows = out_ref.shape[1]
    half = rows // 2

    @pl.loop(0, rows // 32)
    def _(chunk):
        total = jnp.zeros((32, 128), f32)
        for b in range(BLOCKS):
            for t in range(3):
                at = pl.ds(pl.multiple_of(t * rows + chunk * 32, 32), 32)
                part = x_ref[b, at, :].astype(f32)
                total = total + part * part
        squares[pl.ds(pl.multiple_of(chunk * 32, 32), 32), :] = total

    @pl.loop(0, half // 32)
    def _(chunk):
        total = jnp.zeros((32, 128), f32)
        at = pl.ds(pl.multiple_of(3 * rows + chunk * 32, 32), 32)
        for b in range(BLOCKS):
            part = x_ref[b, at, :].astype(f32)
            total = total + part * part
        folds[pl.ds(pl.multiple_of(chunk * 32, 32), 32), :] = total

    rest = folds[...]
    rest = jnp.concatenate(
        [jnp.sum(rest[:, :64], -1, keepdims=True), jnp.sum(rest[:, 64:], -1, keepdims=True)], 0
    )
    mean = (jnp.sum(squares[...], -1, keepdims=True) + rest) / (BLOCKS * 448)
    inverse[...] = jnp.broadcast_to(lax.rsqrt(mean + epsilon), inverse.shape)
    for b in range(BLOCKS):
        gain = x_ref[b, 3 * rows + half : 3 * rows + half + 16, :].astype(f32)
        for t in range(3):
            part = x_ref[b, t * rows : (t + 1) * rows, :].astype(f32)
            out_ref[b, :, 128 * t : 128 * t + 128] = (
                part * inverse[...] * gain[t : t + 1]
            ).astype(bf16)
        part = unfolded(x_ref[b, 3 * rows : 3 * rows + half, :]).astype(f32)
        out_ref[b, :, 384:448] = (part * inverse[:, :64] * gain[3:4, :64]).astype(bf16)


def norm(gathered, rows):
    return pl.pallas_call(
        norm_kernel,
        out_shape=jax.ShapeDtypeStruct((BLOCKS, rows, 448), bf16),
        in_specs=[whole()],
        out_specs=whole(),
        scratch_shapes=[
            pltpu.VMEM((rows, 128), f32),
            pltpu.VMEM((rows // 2, 128), f32),
            pltpu.VMEM((rows, 128), f32),
        ],
        compiler_params=params(24),
        cost_estimate=pl.CostEstimate(flops=10**7, bytes_accessed=8 * 10**6, transcendentals=0),
        name="norm",
    )(gathered)


def project_kernel(sizes, start, last, order, normed_ref, *refs):
    count = sum(sizes)
    weights, rest = refs[:count], refs[count:]
    if start == 0:
        outs, total = rest, None
    else:
        total, outs = rest[0][...], rest[1:]
    at = 0
    for k, parts in enumerate(sizes):
        block = [ref[...] for ref in weights[at : at + parts]]
        at += parts
        block = block[0] if parts == 1 else jnp.concatenate(block, 0)
        normed = normed_ref[order[start + k]]
        both = jnp.dot(normed, block[:448], preferred_element_type=f32)
        value = lax.dot_general(
            normed, block[448:, :448], (((1,), (1,)), ((), ())), preferred_element_type=f32
        )
        term = jnp.concatenate([both, value], 1)
        total = term if total is None else total + term
    if last:
        half = total.shape[0] // 2
        rounded = total.astype(bf16)
        for h in range(2):
            outs[h][...] = rounded[h * half : (h + 1) * half]
    else:
        outs[0][...] = total


def project(start, last, order, normed, slots, total=None):
    rows = normed.shape[1]
    sizes = tuple(len(slot) for slot in slots)
    flat = [part for slot in slots for part in slot]
    extra = [] if total is None else [total]
    if last:
        shape = [jax.ShapeDtypeStruct((rows // 2, 576), bf16)] * 2
    else:
        shape = [jax.ShapeDtypeStruct((rows, 576), f32)]
    return pl.pallas_call(
        functools.partial(project_kernel, sizes, start, last),
        out_shape=shape,
        in_specs=[scalars()] + [whole()] * (1 + len(flat) + len(extra)),
        out_specs=[whole()] * len(shape),
        compiler_params=params(28),
        cost_estimate=pl.CostEstimate(
            flops=2 * rows * 448 * 576 * len(slots), bytes_accessed=10**6 * len(slots), transcendentals=0
        ),
        name="project",
    )(order, normed, *flat, *extra)


def attention_kernel(
    facts, own_ref, oth_ref, cos_ref, sin_ref, reach_ref, pick_ref, key_ref, value_ref,
    kept_ref, sent_ref, stats_ref, chosen_ref, scores,
):
    request = pl.program_id(0)
    first = facts[0] == 0
    count = facts[1 + request]
    nodes = own_ref.shape[0]
    q_cols = 448
    cosine, sine = cos_ref[...], sin_ref[...]
    own, other = own_ref[...].astype(f32), oth_ref[...].astype(f32)

    def paired(lo, hi):
        low = jnp.where(first, own[:, lo:hi], other[:, lo:hi])
        high = jnp.where(first, other[:, lo:hi], own[:, lo:hi])
        return jnp.concatenate([low, high], 1)

    def turned(u):
        return (u * cosine + pltpu.roll(u, 64, 1) * sine).astype(bf16)

    query = paired(0, q_cols)
    queries = jnp.concatenate(
        [turned(query[:, 128 * g : 128 * g + 128]) for g in range(GROUP)], 0
    )
    rot_key = turned(paired(448, 512))
    node_value = paired(512, 576).astype(bf16)

    wide = rot_key.astype(f32)
    own_key = jnp.where(first, wide[:, :64], wide[:, 64:])
    kv_rows = jnp.concatenate([own_key, own[:, 512:576]], 1).astype(bf16)
    chosen_ref[0] = jnp.dot(pick_ref[0], kv_rows, preferred_element_type=f32).astype(bf16)

    pieces, rows, span = scores.shape
    nt = (((1,), (1,)), ((), ()))
    tree = lax.dot_general(queries, rot_key, nt, preferred_element_type=f32)
    reach = jnp.concatenate([reach_ref[0]] * GROUP, 0)
    tree = jnp.where(jnp.logical_and(reach > 0.5, first), tree, masked_score)
    highest = jnp.full((rows, 128), masked_score, f32)
    for c in range(pieces):
        part = lax.dot_general(
            queries, key_ref[0, c * span : (c + 1) * span, :], nt, preferred_element_type=f32
        )
        live = lax.broadcasted_iota(jnp.int32, (1, span), 1) + c * span < count
        part = jnp.where(live, part, masked_score)
        scores[c] = part
        for t in range(span // 128):
            highest = jnp.maximum(highest, part[:, 128 * t : 128 * t + 128])
    highest = jnp.maximum(
        jnp.max(highest, -1, keepdims=True), jnp.max(tree, -1, keepdims=True)
    )

    factor = math.log2(math.e) / math.sqrt(128.0)
    ones = jnp.ones((span, 128), bf16)
    weights = jnp.exp2((tree - highest) * factor).astype(bf16)
    summed = jnp.dot(
        weights, jnp.concatenate([node_value, ones[:nodes]], 1), preferred_element_type=f32
    )
    for c in range(pieces):
        weights = jnp.exp2((scores[c] - highest) * factor).astype(bf16)
        values = jnp.concatenate([value_ref[0, c * span : (c + 1) * span, :], ones], 1)
        summed = summed + jnp.dot(weights, values, preferred_element_type=f32)

    total = summed[:, 128:129]
    mean = summed[:, :128] / total
    some = jnp.logical_or(first, count > 0)
    level = jnp.where(some, highest * (1.0 / math.sqrt(128.0)) + jnp.log(total), masked_score)
    every = jnp.concatenate([mean[g * nodes : (g + 1) * nodes] for g in range(GROUP)], 1)
    low, high = every[:, :q_cols], every[:, q_cols:]
    kept_ref[...] = jnp.where(first, low, high)
    levels = jnp.concatenate(
        [level[g * nodes : (g + 1) * nodes] for g in range(GROUP)]
        + [jnp.zeros((nodes, 128 - GROUP), f32)], 1,
    )
    stats_ref[...] = levels
    coarse = levels[:, :16].astype(bf16).astype(f32)
    finer = (levels[:, :16] - coarse).astype(bf16).astype(f32)
    finest = levels[:, :16] - coarse - finer
    sent_ref[...] = jnp.concatenate(
        [jnp.where(first, high, low), coarse, finer, finest, jnp.zeros((nodes, 16), f32)], 1
    ).astype(bf16)


def attention(half, facts, own, other, cosine, sine, reach, pick, keys, values):
    half_len, head = keys.shape[-2:]
    requests = keys.shape[0] // 2
    nodes = own.shape[0] // requests
    columns = own.shape[1]
    base = half * requests

    def rows_of(width, at=0):
        return pl.BlockSpec((nodes, width), lambda r, facts: (at + r, 0))

    def request_of(*shape, at=0):
        return pl.BlockSpec((1,) + shape, lambda r, facts: (at + r, 0, 0))

    span = 512
    return pl.pallas_call(
        attention_kernel,
        grid_spec=pltpu.PrefetchScalarGridSpec(
            num_scalar_prefetch=1,
            grid=(requests,),
            in_specs=[
                rows_of(columns), rows_of(columns), rows_of(head, base), rows_of(head, base),
                request_of(nodes, nodes, at=base), request_of(*pick.shape[1:], at=base),
                request_of(half_len, head, at=base), request_of(half_len, head, at=base),
            ],
            out_specs=[rows_of(448), rows_of(512), rows_of(128), request_of(pick.shape[1], 128)],
            scratch_shapes=[pltpu.VMEM((half_len // span, GROUP * nodes, span), f32)],
        ),
        out_shape=[
            jax.ShapeDtypeStruct((requests * nodes, 448), f32),
            jax.ShapeDtypeStruct((requests * nodes, 512), bf16),
            jax.ShapeDtypeStruct((requests * nodes, 128), f32),
            jax.ShapeDtypeStruct((requests, pick.shape[1], 128), bf16),
        ],
        compiler_params=params(40),
        cost_estimate=pl.CostEstimate(
            flops=requests * 448 * 2112 * 128 * 40,
            bytes_accessed=requests * 2**24,
            transcendentals=requests * 448 * 2112,
        ),
        name="attention",
    )(facts, own, other, cosine, sine, reach, pick, keys, values)


def attend(facts, kept_ref, stats_ref, got_ref, valid_ref):
    first = facts[0] == 0
    got = got_ref[...].astype(f32)
    theirs = got[:, 448:464] + got[:, 464:480] + got[:, 480:496]
    ours = stats_ref[:, :16]
    highest = jnp.maximum(ours, theirs)
    own_factor = jnp.exp(ours - highest)
    other_factor = jnp.exp(theirs - highest)
    both = own_factor + other_factor

    def spread(part):
        rows = part.shape[0]
        every = jnp.concatenate(
            [jnp.broadcast_to(part[:, g : g + 1], (rows, 128)) for g in range(GROUP)], 1
        )
        return jnp.where(first, every[:, :448], every[:, 448:])

    mixed = kept_ref[...] * spread(own_factor / both) + got[:, :448] * spread(other_factor / both)
    return mixed.astype(bf16) * valid_ref[...]


def send_terms(place, tiles, outs):
    block = pl.program_id(0)
    along = place[1 + BLOCKS + block]
    for step, out in enumerate(outs):

        @pl.when(place[1 + block] == step)
        def _(out=out):
            base = 0
            for tile in tiles:
                out[along, base : base + tile.shape[0], :] = tile.astype(out.dtype)
                base += tile.shape[0]


def out_first_kernel(place, *refs):
    halves, (weight_ref, attended, *outs) = refs[:8], refs[8:]

    @pl.when(pl.program_id(0) == 0)
    def _():
        rows = attended.shape[0] // 2
        for h in range(2):
            attended[h * rows : (h + 1) * rows, :] = attend(place, *halves[4 * h : 4 * h + 4])

    weight = jnp.concatenate([weight_ref[0, :448, :], weight_ref[0, 448:, :]], 1)
    terms = jnp.dot(attended[...], weight, preferred_element_type=f32)
    send_terms(place, [terms[:, :128], terms[:, 128:]], outs)


def out_second_kernel(place, attended, weight_ref, earlier, *outs):
    weight = jnp.concatenate([weight_ref[0, :448, :], unfolded(weight_ref[0, 448:, :])], 1)
    terms = jnp.dot(attended[...], weight, preferred_element_type=f32)
    send_terms(place, [terms[:, :128], folded(terms[:, 128:])], outs)


def out_terms(kernel, place, arrays, weights, rows, earlier=(), attended_shape=None):
    def fixed(shape):
        return pl.BlockSpec(shape, lambda d, place: (0,) * len(shape))

    shapes = [jax.ShapeDtypeStruct(attended_shape, bf16)] if attended_shape else []
    shapes += [
        jax.ShapeDtypeStruct((SIDE, rows, 128), bf16 if step else f32) for step in range(SIDE)
    ]
    return pl.pallas_call(
        kernel,
        grid_spec=pltpu.PrefetchScalarGridSpec(
            num_scalar_prefetch=1,
            grid=(BLOCKS,),
            in_specs=[fixed(a.shape) for a in arrays]
            + [pl.BlockSpec((1,) + weights.shape[1:], lambda d, place: (d, 0, 0))]
            + [pl.BlockSpec(memory_space=pl.ANY)] * len(earlier),
            out_specs=[fixed(s.shape) for s in shapes],
        ),
        out_shape=shapes,
        compiler_params=params(48),
        cost_estimate=pl.CostEstimate(
            flops=256 * 448 * rows * 16 * 20, bytes_accessed=10**8, transcendentals=0
        ),
        name="out_terms",
    )(place, *arrays, weights, *earlier)


def partial_kernel(place, own_ref, *refs):
    got, outs = refs[:3], refs[3:]
    for step in range(SIDE):
        at = lax.rem(place[0] + step, SIDE)
        value = own_ref[at]
        for part in got:
            value = value + part[at].astype(f32)
        outs[step][...] = value.astype(outs[step].dtype)


def partial_sums(place, own, got):
    shape = own.shape[1:]
    return pl.pallas_call(
        partial_kernel,
        out_shape=[jax.ShapeDtypeStruct(shape, bf16 if step else f32) for step in range(SIDE)],
        in_specs=[scalars()] + [whole()] * 4,
        out_specs=[whole()] * SIDE,
        compiler_params=params(16),
        name="partial_sums",
    )(place, own, *got)


def final_kernel(hidden_ref, *refs):
    out_ref = refs[-1]
    rows = hidden_ref.shape[0]
    sums = []
    for h in range(2):
        own, *got = refs[SIDE * h : SIDE * h + SIDE]
        value = own[...]
        for part in got:
            value = value + part[...].astype(f32)
        sums.append(value)
    dense = jnp.concatenate(
        [sums[0][:rows], sums[0][rows:], sums[1][:rows], unfolded(sums[1][rows:])], 1
    )
    out_ref[...] = (hidden_ref[...].astype(f32) + dense).astype(bf16)


def final(hidden, parts):
    return pl.pallas_call(
        final_kernel,
        out_shape=jax.ShapeDtypeStruct(hidden.shape, bf16),
        in_specs=[whole()] * 9,
        out_specs=whole(),
        compiler_params=params(16),
        name="final",
    )(hidden, *parts)


def after(value, *others):
    return lax.optimization_barrier((value,) + tuple(o[(slice(0, 1),) * o.ndim] for o in others))[0]


def shards(
    hidden_in,
    norm_gain,
    w_query,
    w_key,
    w_value,
    w_out,
    key_cache,
    value_cache,
    cache_len,
    tree_parent,
    valid_nodes,
    accepted_path,
    slot_owner,
):
    req_dev, tree_size, part_width = hidden_in.shape
    row_count = req_dev * tree_size
    head_dim = key_cache.shape[-1]
    half_len = key_cache.shape[3]
    dp, mp = lax.axis_index("dp"), lax.axis_index("mp")
    z, core = dp // CORES, dp % CORES
    x, y = mp // SIDE, mp % SIDE
    me_first, me_second = jnp.where(core == 0, y, x), jnp.where(core == 0, x, y)
    half_index = mp % 2
    hidden = hidden_in.reshape(row_count, part_width)

    gain = jnp.pad(jnp.pad(norm_gain, (0, 64)).reshape(4, 128), ((0, 28), (0, 0)))
    packed, weights, out_one, out_two = pack(hidden, gain, w_query, w_key, w_value.T, w_out)
    gathered = lax.all_gather(packed, "mp")
    weights_one = lax.all_gather(after(out_one, gathered), "dp")
    weights_two = lax.all_gather(after(out_two, weights_one), "dp")


    slots = [[weights], [other_core(weights)]]
    order = [dp, dp ^ 1]
    up = down = weights
    for step in range(1, 4):
        up, down = along_z(up, 1), along_z(down, -1)
        slots += [[up], [down], [other_core(up)], [other_core(down)]]
        order += [dp - 2 * step, dp + 2 * step, (dp ^ 1) - 2 * step, (dp ^ 1) + 2 * step]
    cut = weights.shape[0] // 2
    up, down = along_z(up[:cut], 1), along_z(down[cut:], -1)
    slots += [[up, down], [other_core(up), other_core(down)]]
    order += [dp + 8, (dp ^ 1) + 8]
    order = (jnp.stack(order) % DP).astype(jnp.int32)

    block = jnp.arange(BLOCKS, dtype=jnp.int32)
    to_first = jnp.where(core == 0, block % SIDE, block // SIDE)
    to_second = jnp.where(core == 0, block // SIDE, block % SIDE)
    place = jnp.concatenate(
        [half_index[None], (to_first - me_first) % SIDE, to_second]
    ).astype(jnp.int32)

    reach = tree_closure(tree_parent)
    depth = jnp.sum(reach, -1) - 1.0
    position = (cache_len[:, None].astype(f32) + depth).reshape(row_count, 1)
    half_dim = head_dim // 2
    inverse = jnp.exp(
        jnp.arange(half_dim, dtype=f32) * (-2.0 * math.log(rope_base) / head_dim)
    )
    angles = position * inverse
    cosine, sine = jnp.cos(angles), jnp.sin(angles)
    cosine = jnp.concatenate([cosine, cosine], -1)
    sine = jnp.concatenate([-sine, sine], -1)
    picks = accepted_path.shape[1]
    pick = (
        jnp.pad(accepted_path, ((0, 0), (0, 16 - picks)))[..., None]
        == jnp.arange(tree_size, dtype=jnp.int32)
    ).astype(bf16)
    counts = jnp.clip(cache_len - half_index * half_len, 0, half_len)
    valid = valid_nodes.reshape(row_count, 1).astype(bf16)

    normed = norm(gathered, row_count)
    bounds = (0,) + KNOWN + (len(slots),)
    total = None
    for lo, hi in zip(bounds[:-1], bounds[1:]):
        total = project(
            lo, hi == len(slots), order, normed, slots[lo:hi], total and total[0]
        )

    half_rows = row_count // 2
    others = [partner(own) for own in total]
    arrays, chosen = [], []
    for half, own in enumerate(total):
        at = slice(half * half_rows, (half + 1) * half_rows)
        group = slice(half * req_dev // 2, (half + 1) * req_dev // 2)
        facts = jnp.concatenate([half_index[None], counts[group]]).astype(jnp.int32)
        kept, sent, stats, rows = attention(
            half, facts, own, others[half], cosine, sine, reach, pick,
            key_cache[:, 0, 0], value_cache[:, 0, 0],
        )
        chosen.append(rows)
        arrays += [kept, stats, partner(sent), valid[at]]
    attended, *first_terms = out_terms(
        out_first_kernel, place, arrays, weights_one, 2 * row_count, attended_shape=(row_count, 448)
    )
    first_got = [first_axis(first_terms[s], s) for s in (2, 1, 3)]
    second_terms = out_terms(
        out_second_kernel, place, [attended], weights_two, row_count * 3 // 2, first_got[1:2]
    )
    second_got = [first_axis(second_terms[s], s) for s in (2, 1, 3)]
    parts = []
    for own, got in ((first_terms[0], first_got), (second_terms[0], second_got)):
        mine = partial_sums(me_second[None].astype(jnp.int32), own, got)
        parts += [mine[0]] + [second_axis(mine[s], s) for s in (2, 1, 3)]
    layer_out = final(hidden, parts).reshape(req_dev, tree_size, part_width)

    rows = jnp.pad(jnp.concatenate(chosen), ((0, 0), (0, 80 - chosen[0].shape[1]), (0, 0)))
    every_row = lax.all_gather(after(rows, weights_two), "dp", axis=0, tiled=True)[:, :picks]
    total_reqs = slot_owner.shape[0]
    my_slots = dp * req_dev + jnp.arange(req_dev, dtype=jnp.int32)
    senders = (slot_owner[None, :] == my_slots[:, None]).astype(bf16)
    accepted_kv = (
        jnp.dot(senders, every_row.reshape(total_reqs, -1), preferred_element_type=f32)
        .astype(bf16)
        .reshape(req_dev, picks, 2, -1)
    )
    return (layer_out, accepted_kv)


def solution(mesh):
    placed = (
        P("dp", None, "mp"),
        P("mp"),
        P("dp", "mp"),
        P("dp", "mp"),
        P("dp", "mp"),
        P("mp", "dp"),
        P("dp", "mp", None, None, None),
        P("dp", "mp", None, None, None),
        P("dp"),
        P("dp", None),
        P("dp", None),
        P("dp", None),
        P(),
    )
    return jax.shard_map(
        shards,
        mesh=mesh,
        in_specs=placed,
        out_specs=(P("dp", None, "mp"), P("dp", None, None, "mp")),
        check_vma=False,
    )
```

```python
import functools
import math

import jax
import jax.numpy as jnp
from jax import lax
from jax.experimental import pallas as pl
from jax.experimental.pallas import tpu as pltpu
from jax.sharding import PartitionSpec as P

GROUP = 7
SIDE = 4
epsilon = 1e-05
rope_base = 5000000.0
masked_score = -1e30
bf16 = jnp.bfloat16
f32 = jnp.float32
VMEM = pltpu.VMEM


def whole():
    return pl.BlockSpec(memory_space=VMEM)


def scalars():
    return pl.BlockSpec(memory_space=pltpu.SMEM)


def params(mib):
    return pltpu.CompilerParams(vmem_limit_bytes=mib * 2**20)


DP, CORES, Z = 16, 2, 8
BLOCKS = 16
KNOWN = (10, 14)
HOLD = 10


def moved(block, target):
    route = []
    for d in range(DP):
        for m in range(SIDE * SIDE):
            z, core, x, y = target(d // CORES, d % CORES, m // SIDE, m % SIDE)
            to = (z % Z * CORES + core) * SIDE * SIDE + x % SIDE * SIDE + y % SIDE
            route.append((d * SIDE * SIDE + m, to))
    return lax.ppermute(block, ("dp", "mp"), route)


def other_core(block):
    return moved(block, lambda z, c, x, y: (z, c ^ 1, x, y))


def along_z(block, step):
    return moved(block, lambda z, c, x, y: (z + step, c, x, y))


def first_axis(block, step):
    return moved(block, lambda z, c, x, y: (z, c, x, y + step) if c == 0 else (z, c, x + step, y))


def second_axis(block, step):
    return moved(block, lambda z, c, x, y: (z, c, x + step, y) if c == 0 else (z, c, x, y + step))


def partner(block):
    return moved(block, lambda z, c, x, y: (z, c, x, y ^ 1))


def tree_closure(parents):
    width = parents.shape[-1]
    nodes = jnp.arange(width, dtype=jnp.int32)
    onehot = (parents[..., None] == nodes).astype(f32)
    reach = jnp.minimum(jnp.eye(width, dtype=f32) + onehot, 1.0)
    for _ in range((width - 1).bit_length()):
        small = reach.astype(bf16)
        reach = jnp.minimum(
            jnp.einsum("rij,rjk->rik", small, small, preferred_element_type=f32), 1.0
        )
    return reach


def unfolded(tile):
    wide = tile.astype(f32)
    return jnp.concatenate([wide[:, :64], wide[:, 64:]], 0).astype(tile.dtype)


def folded(array):
    half = array.shape[0] // 2
    wide = array.astype(f32)
    return jnp.concatenate([wide[:half], wide[half:]], 1).astype(array.dtype)


def pack_kernel(hidden_ref, gain_ref, query_ref, key_ref, value_ref, x_ref, w_ref):
    rows = hidden_ref.shape[0]
    w_ref[:448, :384] = query_ref[:, :384]
    w_ref[:448, 384:] = jnp.concatenate(
        [query_ref[:, 384:448].astype(f32), key_ref[...].astype(f32)], 1
    ).astype(bf16)
    w_ref[448:, :] = jnp.concatenate([value_ref[...].astype(f32), jnp.zeros((64, 64), f32)], 1).astype(bf16)
    for t in range(3):
        x_ref[t * rows : (t + 1) * rows, :] = hidden_ref[:, 128 * t : 128 * t + 128]
    x_ref[3 * rows : 3 * rows + rows // 2, :] = folded(hidden_ref[:, 384:448])
    gain = jnp.concatenate([gain_ref[...].astype(f32), jnp.zeros((1, 64), f32)], 1)
    gain = jnp.concatenate([gain[:, 128 * t : 128 * t + 128] for t in range(4)] + [jnp.zeros((28, 128), f32)], 0)
    x_ref[3 * rows + rows // 2 :, :] = gain.astype(bf16)


def pack(hidden, gain, w_query, w_key, w_value):
    rows = hidden.shape[0]
    return pl.pallas_call(
        pack_kernel,
        out_shape=[
            jax.ShapeDtypeStruct((rows * 7 // 2 + 32, 128), bf16),
            jax.ShapeDtypeStruct((512, 512), bf16),
        ],
        in_specs=[whole()] * 5,
        out_specs=[whole()] * 2,
        compiler_params=params(8),
        name="pack",
    )(hidden, gain, w_query, w_key, w_value)


def held_kernel(weight_ref, earlier, out_ref):
    out_ref[...] = weight_ref[...]


def held(weight, earlier):
    return pl.pallas_call(
        held_kernel,
        out_shape=jax.ShapeDtypeStruct(weight.shape, bf16),
        in_specs=[whole(), pl.BlockSpec(memory_space=pl.ANY)],
        out_specs=whole(),
        compiler_params=params(4),
        name="held",
    )(weight, earlier)


def norm_kernel(place, *refs):
    arrived, (out_ref, squares, folds, inverse) = refs[:5], refs[5:]
    slots = [(arrived[j], i) for j in range(3) for i in range(SIDE)]
    slots += [(arrived[3 + i // 2], i % 2) for i in range(SIDE)]
    rows = out_ref.shape[1]
    half = rows // 2

    @pl.loop(0, rows // 32)
    def _(chunk):
        total = jnp.zeros((32, 128), f32)
        for ref, i in slots:
            for t in range(3):
                at = pl.ds(pl.multiple_of(t * rows + chunk * 32, 32), 32)
                part = ref[i, at, :].astype(f32)
                total = total + part * part
        squares[pl.ds(pl.multiple_of(chunk * 32, 32), 32), :] = total

    @pl.loop(0, half // 32)
    def _(chunk):
        total = jnp.zeros((32, 128), f32)
        at = pl.ds(pl.multiple_of(3 * rows + chunk * 32, 32), 32)
        for ref, i in slots:
            part = ref[i, at, :].astype(f32)
            total = total + part * part
        folds[pl.ds(pl.multiple_of(chunk * 32, 32), 32), :] = total

    rest = folds[...]
    rest = jnp.concatenate(
        [jnp.sum(rest[:, :64], -1, keepdims=True), jnp.sum(rest[:, 64:], -1, keepdims=True)], 0
    )
    mean = (jnp.sum(squares[...], -1, keepdims=True) + rest) / (16 * 448)
    inverse[...] = jnp.broadcast_to(lax.rsqrt(mean + epsilon), inverse.shape)
    for slot, (ref, i) in enumerate(slots):
        block = place[slot]
        gain = ref[i, 3 * rows + half : 3 * rows + half + 16, :].astype(f32)
        for t in range(3):
            part = ref[i, t * rows : (t + 1) * rows, :].astype(f32)
            out_ref[block, :, 128 * t : 128 * t + 128] = (
                part * inverse[...] * gain[t : t + 1]
            ).astype(bf16)
        part = unfolded(ref[i, 3 * rows : 3 * rows + half, :]).astype(f32)
        out_ref[block, :, 384:448] = (part * inverse[:, :64] * gain[3:4, :64]).astype(bf16)


def norm(place, arrived, rows):
    return pl.pallas_call(
        norm_kernel,
        out_shape=jax.ShapeDtypeStruct((16, rows, 448), bf16),
        in_specs=[scalars()] + [whole()] * 5,
        out_specs=whole(),
        scratch_shapes=[
            pltpu.VMEM((rows, 128), f32),
            pltpu.VMEM((rows // 2, 128), f32),
            pltpu.VMEM((rows, 128), f32),
        ],
        compiler_params=params(16),
        cost_estimate=pl.CostEstimate(flops=16 * 10**6, bytes_accessed=8 * 10**6, transcendentals=0),
        name="norm",
    )(place, *arrived)


def project_kernel(sizes, start, last, order, normed_ref, *refs):
    count = sum(sizes)
    weights, rest = refs[:count], refs[count:]
    if start == 0:
        outs, total = rest, None
    else:
        total, outs = rest[0][...], rest[1:]
    at = 0
    for k, parts in enumerate(sizes):
        block = [ref[...] for ref in weights[at : at + parts]]
        at += parts
        block = block[0] if parts == 1 else jnp.concatenate(block, 0)
        normed = normed_ref[order[start + k]]
        both = jnp.dot(normed, block[:448], preferred_element_type=f32)
        value = lax.dot_general(
            normed, block[448:, :448], (((1,), (1,)), ((), ())), preferred_element_type=f32
        )
        term = jnp.concatenate([both, value], 1)
        total = term if total is None else total + term
    if last:
        half = total.shape[0] // 2
        rounded = total.astype(bf16)
        for h in range(2):
            outs[h][...] = rounded[h * half : (h + 1) * half]
    else:
        outs[0][...] = total


def project(start, last, order, normed, slots, total=None):
    rows = normed.shape[1]
    sizes = tuple(len(slot) for slot in slots)
    flat = [part for slot in slots for part in slot]
    extra = [] if total is None else [total]
    if last:
        shape = [jax.ShapeDtypeStruct((rows // 2, 576), bf16)] * 2
    else:
        shape = [jax.ShapeDtypeStruct((rows, 576), f32)]
    return pl.pallas_call(
        functools.partial(project_kernel, sizes, start, last),
        out_shape=shape,
        in_specs=[scalars()] + [whole()] * (1 + len(flat) + len(extra)),
        out_specs=[whole()] * len(shape),
        compiler_params=params(16),
        cost_estimate=pl.CostEstimate(
            flops=2 * rows * 448 * 576 * len(slots), bytes_accessed=10**6 * len(slots), transcendentals=0
        ),
        name="project",
    )(order, normed, *flat, *extra)


def attention_kernel(
    facts, own_ref, oth_ref, cos_ref, sin_ref, reach_ref, pick_ref, key_ref, value_ref,
    kept_ref, sent_ref, stats_ref, chosen_ref, scores,
):
    request = pl.program_id(0)
    first = facts[0] == 0
    count = facts[1 + request]
    nodes = own_ref.shape[0]
    q_cols = 448
    cosine, sine = cos_ref[...], sin_ref[...]
    own, other = own_ref[...].astype(f32), oth_ref[...].astype(f32)

    def paired(lo, hi):
        low = jnp.where(first, own[:, lo:hi], other[:, lo:hi])
        high = jnp.where(first, other[:, lo:hi], own[:, lo:hi])
        return jnp.concatenate([low, high], 1)

    def turned(u):
        return (u * cosine + pltpu.roll(u, 64, 1) * sine).astype(bf16)

    query = paired(0, q_cols)
    queries = jnp.concatenate(
        [turned(query[:, 128 * g : 128 * g + 128]) for g in range(GROUP)], 0
    )
    rot_key = turned(paired(448, 512))
    node_value = paired(512, 576).astype(bf16)

    wide = rot_key.astype(f32)
    own_key = jnp.where(first, wide[:, :64], wide[:, 64:])
    kv_rows = jnp.concatenate([own_key, own[:, 512:576]], 1).astype(bf16)
    chosen_ref[0] = jnp.dot(pick_ref[0], kv_rows, preferred_element_type=f32).astype(bf16)

    pieces, rows, span = scores.shape
    nt = (((1,), (1,)), ((), ()))
    tree = lax.dot_general(queries, rot_key, nt, preferred_element_type=f32)
    reach = jnp.concatenate([reach_ref[0]] * GROUP, 0)
    tree = jnp.where(jnp.logical_and(reach > 0.5, first), tree, masked_score)
    highest = jnp.full((rows, 128), masked_score, f32)
    for c in range(pieces):
        part = lax.dot_general(
            queries, key_ref[0, c * span : (c + 1) * span, :], nt, preferred_element_type=f32
        )
        live = lax.broadcasted_iota(jnp.int32, (1, span), 1) + c * span < count
        part = jnp.where(live, part, masked_score)
        scores[c] = part
        for t in range(span // 128):
            highest = jnp.maximum(highest, part[:, 128 * t : 128 * t + 128])
    highest = jnp.maximum(
        jnp.max(highest, -1, keepdims=True), jnp.max(tree, -1, keepdims=True)
    )

    factor = math.log2(math.e) / math.sqrt(128.0)
    ones = jnp.ones((span, 128), bf16)
    weights = jnp.exp2((tree - highest) * factor).astype(bf16)
    summed = jnp.dot(
        weights, jnp.concatenate([node_value, ones[:nodes]], 1), preferred_element_type=f32
    )
    for c in range(pieces):
        weights = jnp.exp2((scores[c] - highest) * factor).astype(bf16)
        values = jnp.concatenate([value_ref[0, c * span : (c + 1) * span, :], ones], 1)
        summed = summed + jnp.dot(weights, values, preferred_element_type=f32)

    total = summed[:, 128:129]
    mean = summed[:, :128] / total
    some = jnp.logical_or(first, count > 0)
    level = jnp.where(some, highest * (1.0 / math.sqrt(128.0)) + jnp.log(total), masked_score)
    every = jnp.concatenate([mean[g * nodes : (g + 1) * nodes] for g in range(GROUP)], 1)
    low, high = every[:, :q_cols], every[:, q_cols:]
    kept_ref[...] = jnp.where(first, low, high)
    levels = jnp.concatenate(
        [level[g * nodes : (g + 1) * nodes] for g in range(GROUP)]
        + [jnp.zeros((nodes, 128 - GROUP), f32)], 1,
    )
    stats_ref[...] = levels
    coarse = levels[:, :16].astype(bf16).astype(f32)
    finer = (levels[:, :16] - coarse).astype(bf16).astype(f32)
    finest = levels[:, :16] - coarse - finer
    sent_ref[...] = jnp.concatenate(
        [jnp.where(first, high, low), coarse, finer, finest, jnp.zeros((nodes, 16), f32)], 1
    ).astype(bf16)


def attention(half, facts, own, other, cosine, sine, reach, pick, keys, values):
    half_len, head = keys.shape[-2:]
    requests = keys.shape[0] // 2
    nodes = own.shape[0] // requests
    columns = own.shape[1]
    base = half * requests

    def rows_of(width, at=0):
        return pl.BlockSpec((nodes, width), lambda r, facts: (at + r, 0))

    def request_of(*shape, at=0):
        return pl.BlockSpec((1,) + shape, lambda r, facts: (at + r, 0, 0))

    span = 512
    return pl.pallas_call(
        attention_kernel,
        grid_spec=pltpu.PrefetchScalarGridSpec(
            num_scalar_prefetch=1,
            grid=(requests,),
            in_specs=[
                rows_of(columns), rows_of(columns), rows_of(head, base), rows_of(head, base),
                request_of(nodes, nodes, at=base), request_of(*pick.shape[1:], at=base),
                request_of(half_len, head, at=base), request_of(half_len, head, at=base),
            ],
            out_specs=[rows_of(448), rows_of(512), rows_of(128), request_of(pick.shape[1], 128)],
            scratch_shapes=[pltpu.VMEM((half_len // span, GROUP * nodes, span), f32)],
        ),
        out_shape=[
            jax.ShapeDtypeStruct((requests * nodes, 448), f32),
            jax.ShapeDtypeStruct((requests * nodes, 512), bf16),
            jax.ShapeDtypeStruct((requests * nodes, 128), f32),
            jax.ShapeDtypeStruct((requests, pick.shape[1], 128), bf16),
        ],
        compiler_params=params(14),
        cost_estimate=pl.CostEstimate(
            flops=requests * 448 * 2112 * 128 * 40,
            bytes_accessed=requests * 2**24,
            transcendentals=requests * 448 * 2112,
        ),
        name="attention",
    )(facts, own, other, cosine, sine, reach, pick, keys, values)


def attend(facts, kept_ref, stats_ref, got_ref, valid_ref):
    first = facts[0] == 0
    got = got_ref[...].astype(f32)
    theirs = got[:, 448:464] + got[:, 464:480] + got[:, 480:496]
    ours = stats_ref[:, :16]
    highest = jnp.maximum(ours, theirs)
    own_factor = jnp.exp(ours - highest)
    other_factor = jnp.exp(theirs - highest)
    both = own_factor + other_factor

    def spread(part):
        rows = part.shape[0]
        every = jnp.concatenate(
            [jnp.broadcast_to(part[:, g : g + 1], (rows, 128)) for g in range(GROUP)], 1
        )
        return jnp.where(first, every[:, :448], every[:, 448:])

    mixed = kept_ref[...] * spread(own_factor / both) + got[:, :448] * spread(other_factor / both)
    return mixed.astype(bf16) * valid_ref[...]


def out_kernel(place, order, *refs):
    halves, weights, (first_stride, second_stride), rest = refs[:8], refs[8:26], (place[1], place[2]), refs[26:]
    outs, (every, arrival) = rest[:SIDE], rest[SIDE:]
    cut = every.shape[1] // 2
    copies = []
    for slot in range(BLOCKS - 2):
        copies.append((weights[slot], every.at[order[slot]]))
    for k in range(2):
        block = every.at[order[BLOCKS - 2 + k]]
        copies.append((weights[BLOCKS - 2 + 2 * k], block.at[pl.ds(0, cut)]))
        copies.append((weights[BLOCKS - 1 + 2 * k], block.at[pl.ds(cut, cut)]))
    copies = [pltpu.make_async_copy(a, b, arrival.at[i]) for i, (a, b) in enumerate(copies)]
    for copy in copies:
        copy.start()
    attended = jnp.concatenate([attend(place, *halves[4 * h : 4 * h + 4]) for h in range(2)], 0)
    for copy in copies:
        copy.wait()
    rows = attended.shape[0]
    for step in (2, 1, 3, 0):
        for along in range(SIDE):
            block = lax.rem(place[3] + step, SIDE) * first_stride + along * second_stride
            terms = jnp.dot(attended, every[block], preferred_element_type=f32)
            out = outs[step]
            for t in range(3):
                out[along, t * rows : (t + 1) * rows, :] = terms[:, 128 * t : 128 * t + 128].astype(out.dtype)
            out[along, 3 * rows :, :] = folded(terms[:, 384:]).astype(out.dtype)


def out_terms(place, order, arrays, weights):
    rows = 256 * 7 // 2
    return pl.pallas_call(
        out_kernel,
        out_shape=[
            jax.ShapeDtypeStruct((SIDE, rows, 128), bf16 if step else f32) for step in range(SIDE)
        ],
        in_specs=[scalars()] * 2 + [whole()] * 8 + [pl.BlockSpec(memory_space=pl.ANY)] * 18,
        out_specs=[whole()] * SIDE,
        scratch_shapes=[
            pltpu.VMEM((BLOCKS, 448, 448), bf16),
            pltpu.SemaphoreType.DMA((BLOCKS + 2,)),
        ],
        compiler_params=params(24),
        cost_estimate=pl.CostEstimate(
            flops=256 * 448 * 7168 * 4, bytes_accessed=2 * 10**7, transcendentals=0
        ),
        name="out_terms",
    )(place, order, *arrays, *weights)


def partial_kernel(place, own_ref, *refs):
    got, outs = refs[:3], refs[3:]
    for step in range(SIDE):
        at = lax.rem(place[0] + step, SIDE)
        value = own_ref[at]
        for part in got:
            value = value + part[at].astype(f32)
        outs[step][...] = value.astype(outs[step].dtype)


def partial_sums(place, own, got):
    shape = own.shape[1:]
    return pl.pallas_call(
        partial_kernel,
        out_shape=[jax.ShapeDtypeStruct(shape, bf16 if step else f32) for step in range(SIDE)],
        in_specs=[scalars()] + [whole()] * 4,
        out_specs=[whole()] * SIDE,
        compiler_params=params(16),
        name="partial_sums",
    )(place, own, *got)


def final_kernel(hidden_ref, own_ref, *refs):
    got, out_ref = refs[:3], refs[3]
    rows = hidden_ref.shape[0]
    value = own_ref[...]
    for part in got:
        value = value + part[...].astype(f32)
    dense = jnp.concatenate(
        [value[t * rows : (t + 1) * rows] for t in range(3)] + [unfolded(value[3 * rows :])], 1
    )
    out_ref[...] = (hidden_ref[...].astype(f32) + dense).astype(bf16)


def final(hidden, parts):
    return pl.pallas_call(
        final_kernel,
        out_shape=jax.ShapeDtypeStruct(hidden.shape, bf16),
        in_specs=[whole()] * 5,
        out_specs=whole(),
        compiler_params=params(12),
        name="final",
    )(hidden, *parts)


def two_way(block):
    dp = lax.axis_index("dp")
    slots, order = [[block], [other_core(block)]], [dp, dp ^ 1]
    up = down = block
    for step in range(1, 4):
        up, down = along_z(up, 1), along_z(down, -1)
        slots += [[up], [down], [other_core(up)], [other_core(down)]]
        order += [dp - 2 * step, dp + 2 * step, (dp ^ 1) - 2 * step, (dp ^ 1) + 2 * step]
    cut = block.shape[0] // 2
    up, down = along_z(up[:cut], 1), along_z(down[cut:], -1)
    slots += [[up, down], [other_core(up), other_core(down)]]
    order += [dp + 8, (dp ^ 1) + 8]
    return slots, (jnp.stack(order) % DP).astype(jnp.int32)


def shards(
    hidden_in,
    norm_gain,
    w_query,
    w_key,
    w_value,
    w_out,
    key_cache,
    value_cache,
    cache_len,
    tree_parent,
    valid_nodes,
    accepted_path,
    slot_owner,
):
    req_dev, tree_size, part_width = hidden_in.shape
    row_count = req_dev * tree_size
    head_dim = key_cache.shape[-1]
    half_len = key_cache.shape[3]
    dp, mp = lax.axis_index("dp"), lax.axis_index("mp")
    z, core = dp // CORES, dp % CORES
    x, y = mp // SIDE, mp % SIDE
    me_first, me_second = jnp.where(core == 0, y, x), jnp.where(core == 0, x, y)
    half_index = mp % 2
    hidden = hidden_in.reshape(row_count, part_width)

    packed, weights = pack(hidden, norm_gain[None], w_query, w_key, w_value.T)

    slots, order = two_way(weights)

    cut = packed.shape[0] // 2
    before, behind = first_axis(packed, 1), first_axis(packed, -1)
    across = jnp.concatenate([first_axis(before[:cut], 1), first_axis(behind[cut:], -1)])
    line = jnp.stack([packed, before, behind, across])
    before, behind = second_axis(line, 1), second_axis(line, -1)
    arrived = [line, before, behind, second_axis(before[:2], 1), second_axis(behind[2:], -1)]
    offsets = (0, -1, 1, 2)
    near = [(me_first + o) % SIDE for o in offsets]
    far = [(me_second + o) % SIDE for o in offsets]
    blocks = jnp.stack(
        [jnp.where(core == 0, s * SIDE + f, f * SIDE + s) for s in far for f in near]
    ).astype(jnp.int32)

    out_slots, out_order = two_way(held(w_out, slots[HOLD][0]))
    strides = jnp.where(core == 0, jnp.array([1, SIDE]), jnp.array([SIDE, 1]))
    place = jnp.concatenate([half_index[None], strides, me_first[None]]).astype(jnp.int32)

    reach = tree_closure(tree_parent)
    depth = jnp.sum(reach, -1) - 1.0
    position = (cache_len[:, None].astype(f32) + depth).reshape(row_count, 1)
    half_dim = head_dim // 2
    inverse = jnp.exp(
        jnp.arange(half_dim, dtype=f32) * (-2.0 * math.log(rope_base) / head_dim)
    )
    angles = position * inverse
    cosine, sine = jnp.cos(angles), jnp.sin(angles)
    cosine = jnp.concatenate([cosine, cosine], -1)
    sine = jnp.concatenate([-sine, sine], -1)
    picks = accepted_path.shape[1]
    pick = (
        jnp.pad(accepted_path, ((0, 0), (0, 16 - picks)))[..., None]
        == jnp.arange(tree_size, dtype=jnp.int32)
    ).astype(bf16)
    counts = jnp.clip(cache_len - half_index * half_len, 0, half_len)
    valid = valid_nodes.reshape(row_count, 1).astype(bf16)

    normed = norm(blocks, arrived, row_count)
    bounds = (0,) + KNOWN + (len(slots),)
    total = None
    for lo, hi in zip(bounds[:-1], bounds[1:]):
        total = project(
            lo, hi == len(slots), order, normed, slots[lo:hi], total and total[0]
        )

    half_rows = row_count // 2
    others = [partner(own) for own in total]
    arrays, chosen = [], []
    for half, own in enumerate(total):
        at = slice(half * half_rows, (half + 1) * half_rows)
        group = slice(half * req_dev // 2, (half + 1) * req_dev // 2)
        facts = jnp.concatenate([half_index[None], counts[group]]).astype(jnp.int32)
        kept, sent, stats, rows = attention(
            half, facts, own, others[half], cosine, sine, reach, pick,
            key_cache[:, 0, 0], value_cache[:, 0, 0],
        )
        chosen.append(rows[:, :picks])
        arrays += [kept, stats, partner(sent), valid[at]]
    terms = out_terms(
        place, out_order, arrays, [part for slot in out_slots for part in slot]
    )
    got = [first_axis(terms[s], s) for s in (2, 1, 3)]
    mine = partial_sums(me_second[None].astype(jnp.int32), terms[0], got)
    parts = [mine[0]] + [second_axis(mine[s], s) for s in (2, 1, 3)]
    layer_out = final(hidden, parts).reshape(req_dev, tree_size, part_width)

    every_row = jnp.concatenate(chosen)[None]
    for bit in range(4):
        def flipped(z, c, x, y, bit=bit):
            d = (z * CORES + c) ^ 1 << bit
            return d // CORES, d % CORES, x, y

        every_row = jnp.concatenate([every_row, moved(every_row, flipped)])
    total_reqs = slot_owner.shape[0]
    requests = jnp.arange(total_reqs, dtype=jnp.int32)
    sender = (dp ^ requests // req_dev) * req_dev + requests % req_dev
    owner = jnp.sum(jnp.where(sender[:, None] == requests, slot_owner[None, :], 0), 1)
    my_slots = dp * req_dev + jnp.arange(req_dev, dtype=jnp.int32)
    senders = (owner[None, :] == my_slots[:, None]).astype(bf16)
    accepted_kv = (
        jnp.dot(senders, every_row.reshape(total_reqs, -1), preferred_element_type=f32)
        .astype(bf16)
        .reshape(req_dev, picks, 2, -1)
    )
    return (layer_out, accepted_kv)


def solution(mesh):
    placed = (
        P("dp", None, "mp"),
        P("mp"),
        P("dp", "mp"),
        P("dp", "mp"),
        P("dp", "mp"),
        P("mp", "dp"),
        P("dp", "mp", None, None, None),
        P("dp", "mp", None, None, None),
        P("dp"),
        P("dp", None),
        P("dp", None),
        P("dp", None),
        P(),
    )
    return jax.shard_map(
        shards,
        mesh=mesh,
        in_specs=placed,
        out_specs=(P("dp", None, "mp"), P("dp", None, None, "mp")),
        check_vma=False,
    )
```

```python
import functools
import math

import jax
import jax.numpy as jnp
from jax import lax
from jax.experimental import pallas as pl
from jax.experimental.pallas import tpu as pltpu
from jax.sharding import PartitionSpec as P

GROUP = 7
SIDE = 4
epsilon = 1e-05
rope_base = 5000000.0
masked_score = -1e30
bf16 = jnp.bfloat16
f32 = jnp.float32
VMEM = pltpu.VMEM


def whole():
    return pl.BlockSpec(memory_space=VMEM)


def scalars():
    return pl.BlockSpec(memory_space=pltpu.SMEM)


def params(mib):
    return pltpu.CompilerParams(vmem_limit_bytes=mib * 2**20)


DP, CORES, Z = 16, 2, 8
BLOCKS = 16
HOLD = 6


def moved(block, target):
    route = []
    for d in range(DP):
        for m in range(SIDE * SIDE):
            z, core, x, y = target(d // CORES, d % CORES, m // SIDE, m % SIDE)
            to = (z % Z * CORES + core) * SIDE * SIDE + x % SIDE * SIDE + y % SIDE
            route.append((d * SIDE * SIDE + m, to))
    return lax.ppermute(block, ("dp", "mp"), route)


def other_core(block):
    return moved(block, lambda z, c, x, y: (z, c ^ 1, x, y))


def along_z(block, step):
    return moved(block, lambda z, c, x, y: (z + step, c, x, y))


def first_axis(block, step):
    return moved(block, lambda z, c, x, y: (z, c, x, y + step) if c == 0 else (z, c, x + step, y))


def second_axis(block, step):
    return moved(block, lambda z, c, x, y: (z, c, x + step, y) if c == 0 else (z, c, x, y + step))


def partner(block):
    return moved(block, lambda z, c, x, y: (z, c, x, y ^ 1))


def tree_closure(parents):
    width = parents.shape[-1]
    nodes = jnp.arange(width, dtype=jnp.int32)
    onehot = (parents[..., None] == nodes).astype(f32)
    reach = jnp.minimum(jnp.eye(width, dtype=f32) + onehot, 1.0)
    for _ in range((width - 1).bit_length()):
        small = reach.astype(bf16)
        reach = jnp.minimum(
            jnp.einsum("rij,rjk->rik", small, small, preferred_element_type=f32), 1.0
        )
    return reach


def unfolded(tile):
    wide = tile.astype(f32)
    return jnp.concatenate([wide[:, :64], wide[:, 64:]], 0).astype(tile.dtype)


def folded(array):
    half = array.shape[0] // 2
    wide = array.astype(f32)
    return jnp.concatenate([wide[:half], wide[half:]], 1).astype(array.dtype)


def pack_kernel(hidden_ref, gain_ref, query_ref, key_ref, value_ref, x_ref, w_ref):
    rows = hidden_ref.shape[0]
    w_ref[:448, :384] = query_ref[:, :384]
    w_ref[:448, 384:] = jnp.concatenate(
        [query_ref[:, 384:448].astype(f32), key_ref[...].astype(f32)], 1
    ).astype(bf16)
    w_ref[448:, :] = jnp.concatenate([value_ref[...].astype(f32), jnp.zeros((64, 64), f32)], 1).astype(bf16)
    for t in range(3):
        x_ref[t * rows : (t + 1) * rows, :] = hidden_ref[:, 128 * t : 128 * t + 128]
    x_ref[3 * rows : 3 * rows + rows // 2, :] = folded(hidden_ref[:, 384:448])
    gain = jnp.concatenate([gain_ref[...].astype(f32), jnp.zeros((1, 64), f32)], 1)
    gain = jnp.concatenate([gain[:, 128 * t : 128 * t + 128] for t in range(4)] + [jnp.zeros((28, 128), f32)], 0)
    x_ref[3 * rows + rows // 2 :, :] = gain.astype(bf16)


def pack(hidden, gain, w_query, w_key, w_value):
    rows = hidden.shape[0]
    return pl.pallas_call(
        pack_kernel,
        out_shape=[
            jax.ShapeDtypeStruct((rows * 7 // 2 + 32, 128), bf16),
            jax.ShapeDtypeStruct((512, 512), bf16),
        ],
        in_specs=[whole()] * 5,
        out_specs=[whole()] * 2,
        compiler_params=params(8),
        name="pack",
    )(hidden, gain, w_query, w_key, w_value)


def held_kernel(weight_ref, earlier, out_ref):
    out_ref[...] = weight_ref[...]


def held(weight, earlier):
    return pl.pallas_call(
        held_kernel,
        out_shape=jax.ShapeDtypeStruct(weight.shape, bf16),
        in_specs=[whole(), pl.BlockSpec(memory_space=pl.ANY)],
        out_specs=whole(),
        compiler_params=params(4),
        name="held",
    )(weight, earlier)


def join_kernel(upper_ref, lower_ref, earlier, out_ref):
    cut = upper_ref.shape[0]
    out_ref[:cut, :] = upper_ref[...]
    out_ref[cut:, :] = lower_ref[...]


def join(upper, lower, earlier):
    return pl.pallas_call(
        join_kernel,
        out_shape=jax.ShapeDtypeStruct((2 * upper.shape[0], upper.shape[1]), bf16),
        in_specs=[whole(), whole(), pl.BlockSpec(memory_space=pl.ANY)],
        out_specs=whole(),
        compiler_params=params(4),
        name="join",
    )(upper, lower, earlier)


def norm_kernel(place, *refs):
    arrived, (out_ref, squares, folds, inverse) = refs[:5], refs[5:]
    slots = [(arrived[j], i) for j in range(3) for i in range(SIDE)]
    slots += [(arrived[3 + i // 2], i % 2) for i in range(SIDE)]
    rows = out_ref.shape[1]
    half = rows // 2

    @pl.loop(0, rows // 32)
    def _(chunk):
        total = jnp.zeros((32, 128), f32)
        for ref, i in slots:
            for t in range(3):
                at = pl.ds(pl.multiple_of(t * rows + chunk * 32, 32), 32)
                part = ref[i, at, :].astype(f32)
                total = total + part * part
        squares[pl.ds(pl.multiple_of(chunk * 32, 32), 32), :] = total

    @pl.loop(0, half // 32)
    def _(chunk):
        total = jnp.zeros((32, 128), f32)
        at = pl.ds(pl.multiple_of(3 * rows + chunk * 32, 32), 32)
        for ref, i in slots:
            part = ref[i, at, :].astype(f32)
            total = total + part * part
        folds[pl.ds(pl.multiple_of(chunk * 32, 32), 32), :] = total

    rest = folds[...]
    rest = jnp.concatenate(
        [jnp.sum(rest[:, :64], -1, keepdims=True), jnp.sum(rest[:, 64:], -1, keepdims=True)], 0
    )
    mean = (jnp.sum(squares[...], -1, keepdims=True) + rest) / (16 * 448)
    inverse[...] = jnp.broadcast_to(lax.rsqrt(mean + epsilon), inverse.shape)
    for slot, (ref, i) in enumerate(slots):
        block = place[slot]
        gain = ref[i, 3 * rows + half : 3 * rows + half + 16, :].astype(f32)
        for t in range(3):
            part = ref[i, t * rows : (t + 1) * rows, :].astype(f32)
            out_ref[block, :, 128 * t : 128 * t + 128] = (
                part * inverse[...] * gain[t : t + 1]
            ).astype(bf16)
        part = unfolded(ref[i, 3 * rows : 3 * rows + half, :]).astype(f32)
        out_ref[block, :, 384:448] = (part * inverse[:, :64] * gain[3:4, :64]).astype(bf16)


def norm(place, arrived, rows):
    return pl.pallas_call(
        norm_kernel,
        out_shape=jax.ShapeDtypeStruct((16, rows, 448), bf16),
        in_specs=[scalars()] + [whole()] * 5,
        out_specs=whole(),
        scratch_shapes=[
            pltpu.VMEM((rows, 128), f32),
            pltpu.VMEM((rows // 2, 128), f32),
            pltpu.VMEM((rows, 128), f32),
        ],
        compiler_params=params(16),
        cost_estimate=pl.CostEstimate(flops=16 * 10**6, bytes_accessed=8 * 10**6, transcendentals=0),
        name="norm",
    )(place, *arrived)


def project_kernel(count, start, last, order, normed_ref, *refs):
    weights, rest = refs[:count], refs[count:]
    if start == 0:
        outs, total = rest, None
    else:
        total, outs = rest[0][...], rest[1:]
    for k in range(count):
        normed = normed_ref[order[start + k]]
        both = jnp.dot(normed, weights[k][:448, :], preferred_element_type=f32)
        value = lax.dot_general(
            normed, weights[k][448:, :448], (((1,), (1,)), ((), ())), preferred_element_type=f32
        )
        term = jnp.concatenate([both, value], 1)
        total = term if total is None else total + term
    if last:
        half = total.shape[0] // 2
        rounded = total.astype(bf16)
        for h in range(2):
            outs[h][...] = rounded[h * half : (h + 1) * half]
    else:
        outs[0][...] = total


def project(start, last, order, normed, slots, *total):
    rows, count = normed.shape[1], len(slots)
    if last:
        shape = [jax.ShapeDtypeStruct((rows // 2, 576), bf16)] * 2
    else:
        shape = [jax.ShapeDtypeStruct((rows, 576), f32)]
    return pl.pallas_call(
        functools.partial(project_kernel, count, start, last),
        out_shape=shape,
        in_specs=[scalars()] + [whole()] * (1 + count + len(total)),
        out_specs=[whole()] * len(shape),
        compiler_params=params(18),
        cost_estimate=pl.CostEstimate(
            flops=2 * rows * 448 * 576 * count, bytes_accessed=10**6 * count, transcendentals=0
        ),
        name="project",
    )(order, normed, *slots, *total)


def attention_kernel(
    facts, own_ref, oth_ref, cos_ref, sin_ref, reach_ref, pick_ref, key_ref, value_ref,
    kept_ref, sent_ref, stats_ref, chosen_ref, scores,
):
    request = pl.program_id(0)
    first = facts[0] == 0
    count = facts[1 + request]
    nodes = own_ref.shape[0]
    q_cols = 448
    cosine, sine = cos_ref[...], sin_ref[...]
    own, other = own_ref[...].astype(f32), oth_ref[...].astype(f32)

    def paired(lo, hi):
        low = jnp.where(first, own[:, lo:hi], other[:, lo:hi])
        high = jnp.where(first, other[:, lo:hi], own[:, lo:hi])
        return jnp.concatenate([low, high], 1)

    def turned(u):
        return (u * cosine + pltpu.roll(u, 64, 1) * sine).astype(bf16)

    query = paired(0, q_cols)
    queries = jnp.concatenate(
        [turned(query[:, 128 * g : 128 * g + 128]) for g in range(GROUP)], 0
    )
    rot_key = turned(paired(448, 512))
    node_value = paired(512, 576).astype(bf16)

    wide = rot_key.astype(f32)
    own_key = jnp.where(first, wide[:, :64], wide[:, 64:])
    kv_rows = jnp.concatenate([own_key, own[:, 512:576]], 1).astype(bf16)
    chosen_ref[0] = jnp.dot(pick_ref[0], kv_rows, preferred_element_type=f32).astype(bf16)

    pieces, rows, span = scores.shape
    nt = (((1,), (1,)), ((), ()))
    tree = lax.dot_general(queries, rot_key, nt, preferred_element_type=f32)
    reach = jnp.concatenate([reach_ref[0]] * GROUP, 0)
    tree = jnp.where(jnp.logical_and(reach > 0.5, first), tree, masked_score)
    highest = jnp.full((rows, 128), masked_score, f32)
    for c in range(pieces):
        part = lax.dot_general(
            queries, key_ref[0, c * span : (c + 1) * span, :], nt, preferred_element_type=f32
        )
        live = lax.broadcasted_iota(jnp.int32, (1, span), 1) + c * span < count
        part = jnp.where(live, part, masked_score)
        scores[c] = part
        for t in range(span // 128):
            highest = jnp.maximum(highest, part[:, 128 * t : 128 * t + 128])
    highest = jnp.maximum(
        jnp.max(highest, -1, keepdims=True), jnp.max(tree, -1, keepdims=True)
    )

    factor = math.log2(math.e) / math.sqrt(128.0)
    ones = jnp.ones((span, 128), bf16)
    weights = jnp.exp2((tree - highest) * factor).astype(bf16)
    summed = jnp.dot(
        weights, jnp.concatenate([node_value, ones[:nodes]], 1), preferred_element_type=f32
    )
    for c in range(pieces):
        weights = jnp.exp2((scores[c] - highest) * factor).astype(bf16)
        values = jnp.concatenate([value_ref[0, c * span : (c + 1) * span, :], ones], 1)
        summed = summed + jnp.dot(weights, values, preferred_element_type=f32)

    total = summed[:, 128:129]
    mean = summed[:, :128] / total
    some = jnp.logical_or(first, count > 0)
    level = jnp.where(some, highest * (1.0 / math.sqrt(128.0)) + jnp.log(total), masked_score)
    every = jnp.concatenate([mean[g * nodes : (g + 1) * nodes] for g in range(GROUP)], 1)
    low, high = every[:, :q_cols], every[:, q_cols:]
    kept_ref[...] = jnp.where(first, low, high)
    levels = jnp.concatenate(
        [level[g * nodes : (g + 1) * nodes] for g in range(GROUP)]
        + [jnp.zeros((nodes, 128 - GROUP), f32)], 1,
    )
    stats_ref[...] = levels
    coarse = levels[:, :16].astype(bf16).astype(f32)
    finer = (levels[:, :16] - coarse).astype(bf16).astype(f32)
    finest = levels[:, :16] - coarse - finer
    sent_ref[...] = jnp.concatenate(
        [jnp.where(first, high, low), coarse, finer, finest, jnp.zeros((nodes, 16), f32)], 1
    ).astype(bf16)


def attention(half, facts, own, other, cosine, sine, reach, pick, keys, values):
    half_len, head = keys.shape[-2:]
    requests = keys.shape[0] // 2
    nodes = own.shape[0] // requests
    columns = own.shape[1]
    base = half * requests

    def rows_of(width, at=0):
        return pl.BlockSpec((nodes, width), lambda r, facts: (at + r, 0))

    def request_of(*shape, at=0):
        return pl.BlockSpec((1,) + shape, lambda r, facts: (at + r, 0, 0))

    span = 512
    return pl.pallas_call(
        attention_kernel,
        grid_spec=pltpu.PrefetchScalarGridSpec(
            num_scalar_prefetch=1,
            grid=(requests,),
            in_specs=[
                rows_of(columns), rows_of(columns), rows_of(head, base), rows_of(head, base),
                request_of(nodes, nodes, at=base), request_of(*pick.shape[1:], at=base),
                request_of(half_len, head, at=base), request_of(half_len, head, at=base),
            ],
            out_specs=[rows_of(448), rows_of(512), rows_of(128), request_of(pick.shape[1], 128)],
            scratch_shapes=[pltpu.VMEM((half_len // span, GROUP * nodes, span), f32)],
        ),
        out_shape=[
            jax.ShapeDtypeStruct((requests * nodes, 448), f32),
            jax.ShapeDtypeStruct((requests * nodes, 512), bf16),
            jax.ShapeDtypeStruct((requests * nodes, 128), f32),
            jax.ShapeDtypeStruct((requests, pick.shape[1], 128), bf16),
        ],
        compiler_params=params(14),
        cost_estimate=pl.CostEstimate(
            flops=requests * 26 * 10**9,
            bytes_accessed=requests * 2**20,
            transcendentals=requests * 448 * 2112,
        ),
        name="attention",
    )(facts, own, other, cosine, sine, reach, pick, keys, values)


def attend(facts, kept_ref, stats_ref, got_ref, valid_ref):
    first = facts[0] == 0
    got = got_ref[...].astype(f32)
    theirs = got[:, 448:464] + got[:, 464:480] + got[:, 480:496]
    ours = stats_ref[:, :16]
    highest = jnp.maximum(ours, theirs)
    own_factor = jnp.exp(ours - highest)
    other_factor = jnp.exp(theirs - highest)
    both = own_factor + other_factor

    def spread(part):
        rows = part.shape[0]
        every = jnp.concatenate(
            [jnp.broadcast_to(part[:, g : g + 1], (rows, 128)) for g in range(GROUP)], 1
        )
        return jnp.where(first, every[:, :448], every[:, 448:])

    mixed = kept_ref[...] * spread(own_factor / both) + got[:, :448] * spread(other_factor / both)
    return mixed.astype(bf16) * valid_ref[...]


def combine_kernel(place, *refs):
    out_ref = refs[8]
    rows = out_ref.shape[0] // 2
    for h in range(2):
        out_ref[h * rows : (h + 1) * rows, :] = attend(place, *refs[4 * h : 4 * h + 4])


def combine(place, arrays):
    return pl.pallas_call(
        combine_kernel,
        out_shape=jax.ShapeDtypeStruct((2 * arrays[0].shape[0], 448), bf16),
        in_specs=[scalars()] + [whole()] * 8,
        out_specs=whole(),
        compiler_params=params(8),
        name="combine",
    )(place, *arrays)


def out_kernel(steps, place, att_ref, weight_ref, *outs):
    rows = att_ref.shape[0]
    for out, step in zip(outs, steps):
        for along in range(SIDE):
            block = lax.rem(place[3] + step, SIDE) * place[1] + along * place[2]
            terms = jnp.dot(att_ref[...], weight_ref[block], preferred_element_type=f32)
            for t in range(3):
                out[along, t * rows : (t + 1) * rows, :] = terms[:, 128 * t : 128 * t + 128].astype(out.dtype)
            out[along, 3 * rows :, :] = folded(terms[:, 384:]).astype(out.dtype)


def out_terms(steps, place, attended, weights):
    rows = attended.shape[0] * 7 // 2
    return pl.pallas_call(
        functools.partial(out_kernel, steps),
        out_shape=[
            jax.ShapeDtypeStruct((SIDE, rows, 128), bf16 if step else f32) for step in steps
        ],
        in_specs=[scalars(), whole(), whole()],
        out_specs=[whole()] * len(steps),
        compiler_params=params(16),
        cost_estimate=pl.CostEstimate(
            flops=2 * 10**10, bytes_accessed=2 * 10**7, transcendentals=0
        ),
        name="out_terms",
    )(place, attended, weights)


def partial_kernel(place, own_ref, *refs):
    got, outs = refs[:3], refs[3:]
    for step in range(SIDE):
        at = lax.rem(place[0] + step, SIDE)
        value = own_ref[at]
        for part in got:
            value = value + part[at].astype(f32)
        outs[step][...] = value.astype(outs[step].dtype)


def partial_sums(place, own, got):
    shape = own.shape[1:]
    return pl.pallas_call(
        partial_kernel,
        out_shape=[jax.ShapeDtypeStruct(shape, bf16 if step else f32) for step in range(SIDE)],
        in_specs=[scalars()] + [whole()] * 4,
        out_specs=[whole()] * SIDE,
        compiler_params=params(16),
        name="partial_sums",
    )(place, own, *got)


def final_kernel(hidden_ref, own_ref, *refs):
    got, out_ref = refs[:3], refs[3]
    rows = hidden_ref.shape[0]
    value = own_ref[...]
    for part in got:
        value = value + part[...].astype(f32)
    dense = jnp.concatenate(
        [value[t * rows : (t + 1) * rows] for t in range(3)] + [unfolded(value[3 * rows :])], 1
    )
    out_ref[...] = (hidden_ref[...].astype(f32) + dense).astype(bf16)


def final(hidden, parts):
    return pl.pallas_call(
        final_kernel,
        out_shape=jax.ShapeDtypeStruct(hidden.shape, bf16),
        in_specs=[whole()] * 5,
        out_specs=whole(),
        compiler_params=params(12),
        name="final",
    )(hidden, *parts)


def two_way(block):
    dp = lax.axis_index("dp")
    slots, order = [block, other_core(block)], [dp, dp ^ 1]
    up = down = block
    for step in range(1, 4):
        up, down = along_z(up, 1), along_z(down, -1)
        slots += [up, down, other_core(up), other_core(down)]
        order += [dp - 2 * step, dp + 2 * step, (dp ^ 1) - 2 * step, (dp ^ 1) + 2 * step]
    cut = block.shape[0] // 2
    halves = along_z(up[:cut], 1), along_z(down[cut:], -1)
    order += [dp + 8, (dp ^ 1) + 8]
    return slots, halves, (jnp.stack(order) % DP).astype(jnp.int32)


def shards(
    hidden_in,
    norm_gain,
    w_query,
    w_key,
    w_value,
    w_out,
    key_cache,
    value_cache,
    cache_len,
    tree_parent,
    valid_nodes,
    accepted_path,
    slot_owner,
):
    req_dev, tree_size, part_width = hidden_in.shape
    row_count = req_dev * tree_size
    head_dim = key_cache.shape[-1]
    half_len = key_cache.shape[3]
    dp, mp = lax.axis_index("dp"), lax.axis_index("mp")
    z, core = dp // CORES, dp % CORES
    x, y = mp // SIDE, mp % SIDE
    me_first, me_second = jnp.where(core == 0, y, x), jnp.where(core == 0, x, y)
    half_index = mp % 2
    hidden = hidden_in.reshape(row_count, part_width)

    packed, weights = pack(hidden, norm_gain[None], w_query, w_key, w_value.T)

    slots, halves, order = two_way(weights)

    cut = packed.shape[0] // 2
    before, behind = first_axis(packed, 1), first_axis(packed, -1)
    across = jnp.concatenate([first_axis(before[:cut], 1), first_axis(behind[cut:], -1)])
    line = jnp.stack([packed, before, behind, across])
    before, behind = second_axis(line, 1), second_axis(line, -1)
    arrived = [line, before, behind, second_axis(before[:2], 1), second_axis(behind[2:], -1)]
    offsets = (0, -1, 1, 2)
    near = [(me_first + o) % SIDE for o in offsets]
    far = [(me_second + o) % SIDE for o in offsets]
    blocks = jnp.stack(
        [jnp.where(core == 0, s * SIDE + f, f * SIDE + s) for s in far for f in near]
    ).astype(jnp.int32)

    out_weights = lax.all_gather(held(w_out, slots[HOLD]), "dp")
    strides = jnp.where(core == 0, jnp.array([1, SIDE]), jnp.array([SIDE, 1]))
    place = jnp.concatenate([half_index[None], strides, me_first[None]]).astype(jnp.int32)

    reach = tree_closure(tree_parent)
    depth = jnp.sum(reach, -1) - 1.0
    position = (cache_len[:, None].astype(f32) + depth).reshape(row_count, 1)
    half_dim = head_dim // 2
    inverse = jnp.exp(
        jnp.arange(half_dim, dtype=f32) * (-2.0 * math.log(rope_base) / head_dim)
    )
    angles = position * inverse
    cosine, sine = jnp.cos(angles), jnp.sin(angles)
    cosine = jnp.concatenate([cosine, cosine], -1)
    sine = jnp.concatenate([-sine, sine], -1)
    picks = accepted_path.shape[1]
    pick = (
        jnp.pad(accepted_path, ((0, 0), (0, 16 - picks)))[..., None]
        == jnp.arange(tree_size, dtype=jnp.int32)
    ).astype(bf16)
    counts = jnp.clip(cache_len - half_index * half_len, 0, half_len)
    valid = valid_nodes.reshape(row_count, 1).astype(bf16)

    normed = norm(blocks, arrived, row_count)
    (known,) = project(0, False, order, normed, slots)
    furthest = join(*halves, known)
    total = project(len(slots), True, order, normed, [furthest, other_core(furthest)], known)

    half_rows = row_count // 2
    others = [partner(own) for own in total]
    arrays, chosen = [], []
    for half, own in enumerate(total):
        at = slice(half * half_rows, (half + 1) * half_rows)
        group = slice(half * req_dev // 2, (half + 1) * req_dev // 2)
        facts = jnp.concatenate([half_index[None], counts[group]]).astype(jnp.int32)
        kept, sent, stats, rows = attention(
            half, facts, own, others[half], cosine, sine, reach, pick,
            key_cache[:, 0, 0], value_cache[:, 0, 0],
        )
        chosen.append(rows[:, :picks])
        arrays += [kept, stats, partner(sent), valid[at]]
    attended = combine(place, arrays)
    two, one = out_terms((2, 1), place, attended, out_weights)
    three, here = out_terms((3, 0), place, attended, out_weights)
    got = [first_axis(two, 2), first_axis(one, 1), first_axis(three, 3)]
    mine = partial_sums(me_second[None].astype(jnp.int32), here, got)
    parts = [mine[0]] + [second_axis(mine[s], s) for s in (2, 1, 3)]
    layer_out = final(hidden, parts).reshape(req_dev, tree_size, part_width)

    every_row = jnp.concatenate(chosen)[None]
    for bit in range(4):
        def flipped(z, c, x, y, bit=bit):
            d = (z * CORES + c) ^ 1 << bit
            return d // CORES, d % CORES, x, y

        every_row = jnp.concatenate([every_row, moved(every_row, flipped)])
    total_reqs = slot_owner.shape[0]
    requests = jnp.arange(total_reqs, dtype=jnp.int32)
    sender = (dp ^ requests // req_dev) * req_dev + requests % req_dev
    owner = jnp.sum(jnp.where(sender[:, None] == requests, slot_owner[None, :], 0), 1)
    my_slots = dp * req_dev + jnp.arange(req_dev, dtype=jnp.int32)
    senders = (owner[None, :] == my_slots[:, None]).astype(bf16)
    accepted_kv = (
        jnp.dot(senders, every_row.reshape(total_reqs, -1), preferred_element_type=f32)
        .astype(bf16)
        .reshape(req_dev, picks, 2, -1)
    )
    return (layer_out, accepted_kv)


def solution(mesh):
    placed = (
        P("dp", None, "mp"),
        P("mp"),
        P("dp", "mp"),
        P("dp", "mp"),
        P("dp", "mp"),
        P("mp", "dp"),
        P("dp", "mp", None, None, None),
        P("dp", "mp", None, None, None),
        P("dp"),
        P("dp", None),
        P("dp", None),
        P("dp", None),
        P(),
    )
    return jax.shard_map(
        shards,
        mesh=mesh,
        in_specs=placed,
        out_specs=(P("dp", None, "mp"), P("dp", None, None, "mp")),
        check_vma=False,
    )
```

```python
import functools
import math

import jax
import jax.numpy as jnp
from jax import lax
from jax.experimental import pallas as pl
from jax.experimental.pallas import tpu as pltpu
from jax.sharding import PartitionSpec as P

GROUP = 7
SIDE = 4
epsilon = 1e-05
rope_base = 5000000.0
masked_score = -1e30
bf16 = jnp.bfloat16
f32 = jnp.float32
VMEM = pltpu.VMEM


def whole():
    return pl.BlockSpec(memory_space=VMEM)


def scalars():
    return pl.BlockSpec(memory_space=pltpu.SMEM)


def params(mib):
    return pltpu.CompilerParams(vmem_limit_bytes=mib * 2**20)


DP, CORES, Z = 16, 2, 8
BLOCKS = 16
HOLD = 10
CUT_COST = 2 * 10**10
ATTENTION_COST = 25 * 10**9


def moved(block, target):
    route = []
    for d in range(DP):
        for m in range(SIDE * SIDE):
            z, core, x, y = target(d // CORES, d % CORES, m // SIDE, m % SIDE)
            to = (z % Z * CORES + core) * SIDE * SIDE + x % SIDE * SIDE + y % SIDE
            route.append((d * SIDE * SIDE + m, to))
    return lax.ppermute(block, ("dp", "mp"), route)


def other_core(block):
    return moved(block, lambda z, c, x, y: (z, c ^ 1, x, y))


def along_z(block, step):
    return moved(block, lambda z, c, x, y: (z + step, c, x, y))


def first_axis(block, step):
    return moved(block, lambda z, c, x, y: (z, c, x, y + step) if c == 0 else (z, c, x + step, y))


def second_axis(block, step):
    return moved(block, lambda z, c, x, y: (z, c, x + step, y) if c == 0 else (z, c, x, y + step))


def partner(block):
    return moved(block, lambda z, c, x, y: (z, c, x, y ^ 1))


def tree_closure(parents):
    width = parents.shape[-1]
    nodes = jnp.arange(width, dtype=jnp.int32)
    onehot = (parents[..., None] == nodes).astype(f32)
    reach = jnp.minimum(jnp.eye(width, dtype=f32) + onehot, 1.0)
    for _ in range((width - 1).bit_length()):
        small = reach.astype(bf16)
        reach = jnp.minimum(
            jnp.einsum("rij,rjk->rik", small, small, preferred_element_type=f32), 1.0
        )
    return reach


def unfolded(tile):
    wide = tile.astype(f32)
    return jnp.concatenate([wide[:, :64], wide[:, 64:]], 0).astype(tile.dtype)


def folded(array):
    half = array.shape[0] // 2
    wide = array.astype(f32)
    return jnp.concatenate([wide[:half], wide[half:]], 1).astype(array.dtype)


def pack_kernel(hidden_ref, gain_ref, query_ref, key_ref, value_ref, x_ref, w_ref):
    rows = hidden_ref.shape[0]
    w_ref[:448, :384] = query_ref[:, :384]
    w_ref[:448, 384:] = jnp.concatenate(
        [query_ref[:, 384:448].astype(f32), key_ref[...].astype(f32)], 1
    ).astype(bf16)
    w_ref[448:, :] = jnp.concatenate([value_ref[...].astype(f32), jnp.zeros((64, 64), f32)], 1).astype(bf16)
    for t in range(3):
        x_ref[t * rows : (t + 1) * rows, :] = hidden_ref[:, 128 * t : 128 * t + 128]
    x_ref[3 * rows : 3 * rows + rows // 2, :] = folded(hidden_ref[:, 384:448])
    gain = jnp.concatenate([gain_ref[...].astype(f32), jnp.zeros((1, 64), f32)], 1)
    gain = jnp.concatenate([gain[:, 128 * t : 128 * t + 128] for t in range(4)] + [jnp.zeros((28, 128), f32)], 0)
    x_ref[3 * rows + rows // 2 :, :] = gain.astype(bf16)


def pack(hidden, gain, w_query, w_key, w_value):
    rows = hidden.shape[0]
    return pl.pallas_call(
        pack_kernel,
        out_shape=[
            jax.ShapeDtypeStruct((rows * 7 // 2 + 32, 128), bf16),
            jax.ShapeDtypeStruct((512, 512), bf16),
        ],
        in_specs=[whole()] * 5,
        out_specs=[whole()] * 2,
        compiler_params=params(60),
        name="pack",
    )(hidden, gain, w_query, w_key, w_value)


def held_kernel(weight_ref, earlier, out_ref):
    out_ref[...] = weight_ref[...]


def held(weight, earlier):
    return pl.pallas_call(
        held_kernel,
        out_shape=jax.ShapeDtypeStruct(weight.shape, bf16),
        in_specs=[whole(), pl.BlockSpec(memory_space=pl.ANY)],
        out_specs=whole(),
        compiler_params=params(4),
        name="held",
    )(weight, earlier)


def join_kernel(upper_ref, lower_ref, earlier, out_ref):
    cut = upper_ref.shape[0]
    out_ref[:cut, :] = upper_ref[...]
    out_ref[cut:, :] = lower_ref[...]


def join(upper, lower, earlier):
    return pl.pallas_call(
        join_kernel,
        out_shape=jax.ShapeDtypeStruct((2 * upper.shape[0], upper.shape[1]), bf16),
        in_specs=[whole(), whole(), pl.BlockSpec(memory_space=pl.ANY)],
        out_specs=whole(),
        compiler_params=params(4),
        name="join",
    )(upper, lower, earlier)


def cut_kernel(up_ref, down_ref, upper_ref, lower_ref):
    cut = upper_ref.shape[0]
    upper_ref[...] = up_ref[:cut, :]
    lower_ref[...] = down_ref[cut:, :]


def cut_blocks(up, down):
    half = jax.ShapeDtypeStruct((up.shape[0] // 2, up.shape[1]), bf16)
    return pl.pallas_call(
        cut_kernel,
        out_shape=[half, half],
        in_specs=[whole(), whole()],
        out_specs=[whole(), whole()],
        compiler_params=params(4),
        cost_estimate=pl.CostEstimate(flops=CUT_COST, bytes_accessed=10**6, transcendentals=0),
        name="cut_blocks",
    )(up, down)


def norm_kernel(place, *refs):
    arrived, (out_ref, squares, folds, inverse) = refs[:5], refs[5:]
    slots = [(arrived[j], i) for j in range(3) for i in range(SIDE)]
    slots += [(arrived[3 + i // 2], i % 2) for i in range(SIDE)]
    rows = out_ref.shape[1]
    half = rows // 2

    @pl.loop(0, rows // 32)
    def _(chunk):
        total = jnp.zeros((32, 128), f32)
        for ref, i in slots:
            for t in range(3):
                at = pl.ds(pl.multiple_of(t * rows + chunk * 32, 32), 32)
                part = ref[i, at, :].astype(f32)
                total = total + part * part
        squares[pl.ds(pl.multiple_of(chunk * 32, 32), 32), :] = total

    @pl.loop(0, half // 32)
    def _(chunk):
        total = jnp.zeros((32, 128), f32)
        at = pl.ds(pl.multiple_of(3 * rows + chunk * 32, 32), 32)
        for ref, i in slots:
            part = ref[i, at, :].astype(f32)
            total = total + part * part
        folds[pl.ds(pl.multiple_of(chunk * 32, 32), 32), :] = total

    rest = folds[...]
    rest = jnp.concatenate(
        [jnp.sum(rest[:, :64], -1, keepdims=True), jnp.sum(rest[:, 64:], -1, keepdims=True)], 0
    )
    mean = (jnp.sum(squares[...], -1, keepdims=True) + rest) / (16 * 448)
    inverse[...] = jnp.broadcast_to(lax.rsqrt(mean + epsilon), inverse.shape)
    for slot, (ref, i) in enumerate(slots):
        block = place[slot]
        gain = ref[i, 3 * rows + half : 3 * rows + half + 16, :].astype(f32)
        for t in range(3):
            part = ref[i, t * rows : (t + 1) * rows, :].astype(f32)
            out_ref[block, :, 128 * t : 128 * t + 128] = (
                part * inverse[...] * gain[t : t + 1]
            ).astype(bf16)
        part = unfolded(ref[i, 3 * rows : 3 * rows + half, :]).astype(f32)
        out_ref[block, :, 384:448] = (part * inverse[:, :64] * gain[3:4, :64]).astype(bf16)


def norm(place, arrived, rows):
    return pl.pallas_call(
        norm_kernel,
        out_shape=jax.ShapeDtypeStruct((16, rows, 448), bf16),
        in_specs=[scalars()] + [whole()] * 5,
        out_specs=whole(),
        scratch_shapes=[
            pltpu.VMEM((rows, 128), f32),
            pltpu.VMEM((rows // 2, 128), f32),
            pltpu.VMEM((rows, 128), f32),
        ],
        compiler_params=params(16),
        cost_estimate=pl.CostEstimate(flops=16 * 10**6, bytes_accessed=8 * 10**6, transcendentals=0),
        name="norm",
    )(place, *arrived)


def project_kernel(count, start, last, order, normed_ref, *refs):
    weights, rest = refs[:count], refs[count:]
    if start == 0:
        outs, total = rest, None
    else:
        total, outs = rest[0][...], rest[1:]
    for k in range(count):
        normed = normed_ref[order[start + k]]
        both = jnp.dot(normed, weights[k][:448, :], preferred_element_type=f32)
        value = lax.dot_general(
            normed, weights[k][448:, :448], (((1,), (1,)), ((), ())), preferred_element_type=f32
        )
        term = jnp.concatenate([both, value], 1)
        total = term if total is None else total + term
    if last:
        half = total.shape[0] // 2
        rounded = total.astype(bf16)
        for h in range(2):
            outs[h][...] = rounded[h * half : (h + 1) * half]
    else:
        outs[0][...] = total


def project(start, last, order, normed, slots, *total):
    rows, count = normed.shape[1], len(slots)
    if last:
        shape = [jax.ShapeDtypeStruct((rows // 2, 576), bf16)] * 2
    else:
        shape = [jax.ShapeDtypeStruct((rows, 576), f32)]
    return pl.pallas_call(
        functools.partial(project_kernel, count, start, last),
        out_shape=shape,
        in_specs=[scalars()] + [whole()] * (1 + count + len(total)),
        out_specs=[whole()] * len(shape),
        compiler_params=params(18),
        cost_estimate=pl.CostEstimate(
            flops=2 * rows * 448 * 576 * count, bytes_accessed=10**6 * count, transcendentals=0
        ),
        name="project",
    )(order, normed, *slots, *total)


def attention_kernel(
    facts, own_ref, oth_ref, cos_ref, sin_ref, reach_ref, pick_ref, key_ref, value_ref,
    kept_ref, sent_ref, stats_ref, chosen_ref, scores,
):
    request = pl.program_id(0)
    first = facts[0] == 0
    count = facts[1 + request]
    nodes = own_ref.shape[0]
    q_cols = 448
    cosine, sine = cos_ref[...], sin_ref[...]
    own, other = own_ref[...].astype(f32), oth_ref[...].astype(f32)

    def paired(lo, hi):
        low = jnp.where(first, own[:, lo:hi], other[:, lo:hi])
        high = jnp.where(first, other[:, lo:hi], own[:, lo:hi])
        return jnp.concatenate([low, high], 1)

    def turned(u):
        return (u * cosine + pltpu.roll(u, 64, 1) * sine).astype(bf16)

    query = paired(0, q_cols)
    queries = jnp.concatenate(
        [turned(query[:, 128 * g : 128 * g + 128]) for g in range(GROUP)], 0
    )
    rot_key = turned(paired(448, 512))
    node_value = paired(512, 576).astype(bf16)

    wide = rot_key.astype(f32)
    own_key = jnp.where(first, wide[:, :64], wide[:, 64:])
    kv_rows = jnp.concatenate([own_key, own[:, 512:576]], 1).astype(bf16)
    chosen_ref[0] = jnp.dot(pick_ref[0], kv_rows, preferred_element_type=f32).astype(bf16)

    pieces, rows, span = scores.shape
    nt = (((1,), (1,)), ((), ()))
    tree = lax.dot_general(queries, rot_key, nt, preferred_element_type=f32)
    reach = jnp.concatenate([reach_ref[0]] * GROUP, 0)
    tree = jnp.where(jnp.logical_and(reach > 0.5, first), tree, masked_score)
    highest = jnp.full((rows, 128), masked_score, f32)
    for c in range(pieces):
        part = lax.dot_general(
            queries, key_ref[0, c * span : (c + 1) * span, :], nt, preferred_element_type=f32
        )
        live = lax.broadcasted_iota(jnp.int32, (1, span), 1) + c * span < count
        part = jnp.where(live, part, masked_score)
        scores[c] = part
        for t in range(span // 128):
            highest = jnp.maximum(highest, part[:, 128 * t : 128 * t + 128])
    highest = jnp.maximum(
        jnp.max(highest, -1, keepdims=True), jnp.max(tree, -1, keepdims=True)
    )

    factor = math.log2(math.e) / math.sqrt(128.0)
    ones = jnp.ones((span, 128), bf16)
    weights = jnp.exp2((tree - highest) * factor).astype(bf16)
    summed = jnp.dot(
        weights, jnp.concatenate([node_value, ones[:nodes]], 1), preferred_element_type=f32
    )
    for c in range(pieces):
        weights = jnp.exp2((scores[c] - highest) * factor).astype(bf16)
        values = jnp.concatenate([value_ref[0, c * span : (c + 1) * span, :], ones], 1)
        summed = summed + jnp.dot(weights, values, preferred_element_type=f32)

    total = summed[:, 128:129]
    mean = summed[:, :128] / total
    some = jnp.logical_or(first, count > 0)
    level = jnp.where(some, highest * (1.0 / math.sqrt(128.0)) + jnp.log(total), masked_score)
    every = jnp.concatenate([mean[g * nodes : (g + 1) * nodes] for g in range(GROUP)], 1)
    low, high = every[:, :q_cols], every[:, q_cols:]
    kept_ref[...] = jnp.where(first, low, high)
    levels = jnp.concatenate(
        [level[g * nodes : (g + 1) * nodes] for g in range(GROUP)]
        + [jnp.zeros((nodes, 128 - GROUP), f32)], 1,
    )
    stats_ref[...] = levels
    coarse = levels[:, :16].astype(bf16).astype(f32)
    finer = (levels[:, :16] - coarse).astype(bf16).astype(f32)
    finest = levels[:, :16] - coarse - finer
    sent_ref[...] = jnp.concatenate(
        [jnp.where(first, high, low), coarse, finer, finest, jnp.zeros((nodes, 16), f32)], 1
    ).astype(bf16)


def attention(half, facts, own, other, cosine, sine, reach, pick, keys, values):
    half_len, head = keys.shape[-2:]
    requests = keys.shape[0] // 2
    nodes = own.shape[0] // requests
    columns = own.shape[1]
    base = half * requests

    def rows_of(width, at=0):
        return pl.BlockSpec((nodes, width), lambda r, facts: (at + r, 0))

    def request_of(*shape, at=0):
        return pl.BlockSpec((1,) + shape, lambda r, facts: (at + r, 0, 0))

    span = 512
    return pl.pallas_call(
        attention_kernel,
        grid_spec=pltpu.PrefetchScalarGridSpec(
            num_scalar_prefetch=1,
            grid=(requests,),
            in_specs=[
                rows_of(columns), rows_of(columns), rows_of(head, base), rows_of(head, base),
                request_of(nodes, nodes, at=base), request_of(*pick.shape[1:], at=base),
                request_of(half_len, head, at=base), request_of(half_len, head, at=base),
            ],
            out_specs=[rows_of(448), rows_of(512), rows_of(128), request_of(pick.shape[1], 128)],
            scratch_shapes=[pltpu.VMEM((half_len // span, GROUP * nodes, span), f32)],
        ),
        out_shape=[
            jax.ShapeDtypeStruct((requests * nodes, 448), f32),
            jax.ShapeDtypeStruct((requests * nodes, 512), bf16),
            jax.ShapeDtypeStruct((requests * nodes, 128), f32),
            jax.ShapeDtypeStruct((requests, pick.shape[1], 128), bf16),
        ],
        compiler_params=params(14),
        cost_estimate=pl.CostEstimate(
            flops=requests * ATTENTION_COST,
            bytes_accessed=requests * 2**20,
            transcendentals=requests * 448 * 2112,
        ),
        name="attention",
    )(facts, own, other, cosine, sine, reach, pick, keys, values)


def attend(facts, kept_ref, stats_ref, got_ref, valid_ref):
    first = facts[0] == 0
    got = got_ref[...].astype(f32)
    theirs = got[:, 448:464] + got[:, 464:480] + got[:, 480:496]
    ours = stats_ref[:, :16]
    highest = jnp.maximum(ours, theirs)
    own_factor = jnp.exp(ours - highest)
    other_factor = jnp.exp(theirs - highest)
    both = own_factor + other_factor

    def spread(part):
        rows = part.shape[0]
        every = jnp.concatenate(
            [jnp.broadcast_to(part[:, g : g + 1], (rows, 128)) for g in range(GROUP)], 1
        )
        return jnp.where(first, every[:, :448], every[:, 448:])

    mixed = kept_ref[...] * spread(own_factor / both) + got[:, :448] * spread(other_factor / both)
    return mixed.astype(bf16) * valid_ref[...]


def combine_kernel(place, *refs):
    out_ref = refs[9]
    rows = out_ref.shape[0] // 2
    for h in range(2):
        out_ref[h * rows : (h + 1) * rows, :] = attend(place, *refs[4 * h : 4 * h + 4])


def combine(place, arrays, earlier):
    return pl.pallas_call(
        combine_kernel,
        out_shape=jax.ShapeDtypeStruct((2 * arrays[0].shape[0], 448), bf16),
        in_specs=[scalars()] + [whole()] * 8 + [pl.BlockSpec(memory_space=pl.ANY)],
        out_specs=whole(),
        compiler_params=params(8),
        name="combine",
    )(place, *arrays, earlier)


def out_kernel(steps, place, att_ref, weight_ref, *outs):
    rows = att_ref.shape[0]
    for out, step in zip(outs, steps):
        for along in range(SIDE):
            block = lax.rem(place[3] + step, SIDE) * place[1] + along * place[2]
            terms = jnp.dot(att_ref[...], weight_ref[block], preferred_element_type=f32)
            for t in range(3):
                out[along, t * rows : (t + 1) * rows, :] = terms[:, 128 * t : 128 * t + 128].astype(out.dtype)
            out[along, 3 * rows :, :] = folded(terms[:, 384:]).astype(out.dtype)


def out_terms(steps, place, attended, weights):
    rows = attended.shape[0] * 7 // 2
    return pl.pallas_call(
        functools.partial(out_kernel, steps),
        out_shape=[
            jax.ShapeDtypeStruct((SIDE, rows, 128), bf16 if step else f32) for step in steps
        ],
        in_specs=[scalars(), whole(), whole()],
        out_specs=[whole()] * len(steps),
        compiler_params=params(16),
        cost_estimate=pl.CostEstimate(
            flops=2 * 10**10, bytes_accessed=2 * 10**7, transcendentals=0
        ),
        name="out_terms",
    )(place, attended, weights)


def partial_kernel(place, own_ref, *refs):
    got, outs = refs[:3], refs[3:]
    for step in range(SIDE):
        at = lax.rem(place[0] + step, SIDE)
        value = own_ref[at]
        for part in got:
            value = value + part[at].astype(f32)
        outs[step][...] = value.astype(outs[step].dtype)


def partial_sums(place, own, got):
    shape = own.shape[1:]
    return pl.pallas_call(
        partial_kernel,
        out_shape=[jax.ShapeDtypeStruct(shape, bf16 if step else f32) for step in range(SIDE)],
        in_specs=[scalars()] + [whole()] * 4,
        out_specs=[whole()] * SIDE,
        compiler_params=params(16),
        name="partial_sums",
    )(place, own, *got)


def final_kernel(hidden_ref, own_ref, *refs):
    got, out_ref = refs[:3], refs[3]
    rows = hidden_ref.shape[0]
    value = own_ref[...]
    for part in got:
        value = value + part[...].astype(f32)
    dense = jnp.concatenate(
        [value[t * rows : (t + 1) * rows] for t in range(3)] + [unfolded(value[3 * rows :])], 1
    )
    out_ref[...] = (hidden_ref[...].astype(f32) + dense).astype(bf16)


def final(hidden, parts):
    return pl.pallas_call(
        final_kernel,
        out_shape=jax.ShapeDtypeStruct(hidden.shape, bf16),
        in_specs=[whole()] * 5,
        out_specs=whole(),
        compiler_params=params(12),
        name="final",
    )(hidden, *parts)


def two_way(block):
    dp = lax.axis_index("dp")
    slots, order = [block, other_core(block)], [dp, dp ^ 1]
    up = down = block
    for step in range(1, 4):
        up, down = along_z(up, 1), along_z(down, -1)
        slots += [up, down, other_core(up), other_core(down)]
        order += [dp - 2 * step, dp + 2 * step, (dp ^ 1) - 2 * step, (dp ^ 1) + 2 * step]
    upper, lower = cut_blocks(up, down)
    halves = along_z(upper, 1), along_z(lower, -1)
    order += [dp + 8, (dp ^ 1) + 8]
    return slots, halves, (jnp.stack(order) % DP).astype(jnp.int32)


def shards(
    hidden_in,
    norm_gain,
    w_query,
    w_key,
    w_value,
    w_out,
    key_cache,
    value_cache,
    cache_len,
    tree_parent,
    valid_nodes,
    accepted_path,
    slot_owner,
):
    req_dev, tree_size, part_width = hidden_in.shape
    row_count = req_dev * tree_size
    head_dim = key_cache.shape[-1]
    half_len = key_cache.shape[3]
    dp, mp = lax.axis_index("dp"), lax.axis_index("mp")
    z, core = dp // CORES, dp % CORES
    x, y = mp // SIDE, mp % SIDE
    me_first, me_second = jnp.where(core == 0, y, x), jnp.where(core == 0, x, y)
    half_index = mp % 2
    hidden = hidden_in.reshape(row_count, part_width)

    packed, weights = pack(hidden, norm_gain[None], w_query, w_key, w_value.T)

    slots, halves, order = two_way(weights)

    cut = packed.shape[0] // 2
    before, behind = first_axis(packed, 1), first_axis(packed, -1)
    across = jnp.concatenate([first_axis(before[:cut], 1), first_axis(behind[cut:], -1)])
    line = jnp.stack([packed, before, behind, across])
    before, behind = second_axis(line, 1), second_axis(line, -1)
    arrived = [line, before, behind, second_axis(before[:2], 1), second_axis(behind[2:], -1)]
    offsets = (0, -1, 1, 2)
    near = [(me_first + o) % SIDE for o in offsets]
    far = [(me_second + o) % SIDE for o in offsets]
    blocks = jnp.stack(
        [jnp.where(core == 0, s * SIDE + f, f * SIDE + s) for s in far for f in near]
    ).astype(jnp.int32)

    out_weights = lax.all_gather(held(w_out, slots[HOLD]), "dp")
    strides = jnp.where(core == 0, jnp.array([1, SIDE]), jnp.array([SIDE, 1]))
    place = jnp.concatenate([half_index[None], strides, me_first[None]]).astype(jnp.int32)

    reach = tree_closure(tree_parent)
    depth = jnp.sum(reach, -1) - 1.0
    position = (cache_len[:, None].astype(f32) + depth).reshape(row_count, 1)
    half_dim = head_dim // 2
    inverse = jnp.exp(
        jnp.arange(half_dim, dtype=f32) * (-2.0 * math.log(rope_base) / head_dim)
    )
    angles = position * inverse
    cosine, sine = jnp.cos(angles), jnp.sin(angles)
    cosine = jnp.concatenate([cosine, cosine], -1)
    sine = jnp.concatenate([-sine, sine], -1)
    picks = accepted_path.shape[1]
    pick = (
        jnp.pad(accepted_path, ((0, 0), (0, 16 - picks)))[..., None]
        == jnp.arange(tree_size, dtype=jnp.int32)
    ).astype(bf16)
    counts = jnp.clip(cache_len - half_index * half_len, 0, half_len)
    valid = valid_nodes.reshape(row_count, 1).astype(bf16)

    normed = norm(blocks, arrived, row_count)
    (known,) = project(0, False, order, normed, slots)
    furthest = join(*halves, known)
    total = project(len(slots), True, order, normed, [furthest, other_core(furthest)], known)

    half_rows = row_count // 2
    others = [partner(own) for own in total]
    arrays, chosen = [], []
    for half, own in enumerate(total):
        at = slice(half * half_rows, (half + 1) * half_rows)
        group = slice(half * req_dev // 2, (half + 1) * req_dev // 2)
        facts = jnp.concatenate([half_index[None], counts[group]]).astype(jnp.int32)
        kept, sent, stats, rows = attention(
            half, facts, own, others[half], cosine, sine, reach, pick,
            key_cache[:, 0, 0], value_cache[:, 0, 0],
        )
        chosen.append(rows)
        arrays += [kept, stats, partner(sent), valid[at]]
    attended = combine(place, arrays, out_weights)
    two, one = out_terms((2, 1), place, attended, out_weights)
    three, here = out_terms((3, 0), place, attended, out_weights)
    got = [first_axis(two, 2), first_axis(one, 1), first_axis(three, 3)]
    mine = partial_sums(me_second[None].astype(jnp.int32), here, got)
    parts = [mine[0]] + [second_axis(mine[s], s) for s in (2, 1, 3)]
    layer_out = final(hidden, parts).reshape(req_dev, tree_size, part_width)

    rows = jnp.pad(jnp.concatenate(chosen), ((0, 0), (0, 80 - chosen[0].shape[1]), (0, 0)))
    every_row = lax.all_gather(rows, "dp", axis=0, tiled=True)[:, :picks]
    total_reqs = slot_owner.shape[0]
    my_slots = dp * req_dev + jnp.arange(req_dev, dtype=jnp.int32)
    senders = (slot_owner[None, :] == my_slots[:, None]).astype(bf16)
    accepted_kv = (
        jnp.dot(senders, every_row.reshape(total_reqs, -1), preferred_element_type=f32)
        .astype(bf16)
        .reshape(req_dev, picks, 2, -1)
    )
    return (layer_out, accepted_kv)


def solution(mesh):
    placed = (
        P("dp", None, "mp"),
        P("mp"),
        P("dp", "mp"),
        P("dp", "mp"),
        P("dp", "mp"),
        P("mp", "dp"),
        P("dp", "mp", None, None, None),
        P("dp", "mp", None, None, None),
        P("dp"),
        P("dp", None),
        P("dp", None),
        P("dp", None),
        P(),
    )
    return jax.shard_map(
        shards,
        mesh=mesh,
        in_specs=placed,
        out_specs=(P("dp", None, "mp"), P("dp", None, None, "mp")),
        check_vma=False,
    )
```

```python
import functools
import math

import jax
import jax.numpy as jnp
from jax import lax
from jax.experimental import pallas as pl
from jax.experimental.pallas import tpu as pltpu
from jax.sharding import PartitionSpec as P

GROUP = 7
SIDE = 4
epsilon = 1e-05
rope_base = 5000000.0
masked_score = -1e30
bf16 = jnp.bfloat16
f32 = jnp.float32
VMEM = pltpu.VMEM


def whole():
    return pl.BlockSpec(memory_space=VMEM)


def scalars():
    return pl.BlockSpec(memory_space=pltpu.SMEM)


def params(mib):
    return pltpu.CompilerParams(vmem_limit_bytes=mib * 2**20)


DP, CORES, Z = 16, 2, 8
BLOCKS = 16
CUT_COST = 2 * 10**10
ATTENTION_COST = 25 * 10**9


def moved(block, target):
    route = []
    for d in range(DP):
        for m in range(SIDE * SIDE):
            z, core, x, y = target(d // CORES, d % CORES, m // SIDE, m % SIDE)
            to = (z % Z * CORES + core) * SIDE * SIDE + x % SIDE * SIDE + y % SIDE
            route.append((d * SIDE * SIDE + m, to))
    return lax.ppermute(block, ("dp", "mp"), route)


def other_core(block):
    return moved(block, lambda z, c, x, y: (z, c ^ 1, x, y))


def along_z(block, step):
    return moved(block, lambda z, c, x, y: (z + step, c, x, y))


def first_axis(block, step):
    return moved(block, lambda z, c, x, y: (z, c, x, y + step) if c == 0 else (z, c, x + step, y))


def second_axis(block, step):
    return moved(block, lambda z, c, x, y: (z, c, x + step, y) if c == 0 else (z, c, x, y + step))


def partner(block):
    return moved(block, lambda z, c, x, y: (z, c, x, y ^ 1))


def tree_closure(parents):
    width = parents.shape[-1]
    nodes = jnp.arange(width, dtype=jnp.int32)
    onehot = (parents[..., None] == nodes).astype(f32)
    reach = jnp.minimum(jnp.eye(width, dtype=f32) + onehot, 1.0)
    for _ in range((width - 1).bit_length()):
        small = reach.astype(bf16)
        reach = jnp.minimum(
            jnp.einsum("rij,rjk->rik", small, small, preferred_element_type=f32), 1.0
        )
    return reach


def unfolded(tile):
    wide = tile.astype(f32)
    return jnp.concatenate([wide[:, :64], wide[:, 64:]], 0).astype(tile.dtype)


def folded(array):
    half = array.shape[0] // 2
    wide = array.astype(f32)
    return jnp.concatenate([wide[:half], wide[half:]], 1).astype(array.dtype)


def pack_kernel(hidden_ref, gain_ref, query_ref, key_ref, value_ref, x_ref, w_ref):
    rows = hidden_ref.shape[0]
    w_ref[:448, :384] = query_ref[:, :384]
    w_ref[:448, 384:] = jnp.concatenate(
        [query_ref[:, 384:448].astype(f32), key_ref[...].astype(f32)], 1
    ).astype(bf16)
    w_ref[448:, :] = jnp.concatenate([value_ref[...].astype(f32), jnp.zeros((64, 64), f32)], 1).astype(bf16)
    for t in range(3):
        x_ref[t * rows : (t + 1) * rows, :] = hidden_ref[:, 128 * t : 128 * t + 128]
    x_ref[3 * rows : 3 * rows + rows // 2, :] = folded(hidden_ref[:, 384:448])
    gain = jnp.concatenate([gain_ref[...].astype(f32), jnp.zeros((1, 64), f32)], 1)
    gain = jnp.concatenate([gain[:, 128 * t : 128 * t + 128] for t in range(4)] + [jnp.zeros((28, 128), f32)], 0)
    x_ref[3 * rows + rows // 2 :, :] = gain.astype(bf16)


def pack(hidden, gain, w_query, w_key, w_value):
    rows = hidden.shape[0]
    return pl.pallas_call(
        pack_kernel,
        out_shape=[
            jax.ShapeDtypeStruct((rows * 7 // 2 + 32, 128), bf16),
            jax.ShapeDtypeStruct((512, 512), bf16),
        ],
        in_specs=[whole()] * 5,
        out_specs=[whole()] * 2,
        compiler_params=params(60),
        name="pack",
    )(hidden, gain, w_query, w_key, w_value)


def join_kernel(upper_ref, lower_ref, out_ref):
    cut = upper_ref.shape[0]
    out_ref[:cut, :] = upper_ref[...]
    out_ref[cut:, :] = lower_ref[...]


def join(upper, lower):
    return pl.pallas_call(
        join_kernel,
        out_shape=jax.ShapeDtypeStruct((2 * upper.shape[0], upper.shape[1]), bf16),
        in_specs=[whole(), whole()],
        out_specs=whole(),
        compiler_params=params(4),
        name="join",
    )(upper, lower)


def cut_kernel(up_ref, down_ref, upper_ref, lower_ref):
    cut = upper_ref.shape[0]
    upper_ref[...] = up_ref[:cut, :]
    lower_ref[...] = down_ref[cut:, :]


def cut_blocks(up, down):
    half = jax.ShapeDtypeStruct((up.shape[0] // 2, up.shape[1]), bf16)
    return pl.pallas_call(
        cut_kernel,
        out_shape=[half, half],
        in_specs=[whole(), whole()],
        out_specs=[whole(), whole()],
        compiler_params=params(4),
        cost_estimate=pl.CostEstimate(flops=CUT_COST, bytes_accessed=10**6, transcendentals=0),
        name="cut_blocks",
    )(up, down)


def norm_kernel(x_ref, out_ref, squares, folds, inverse):
    rows = out_ref.shape[1]
    half = rows // 2

    @pl.loop(0, rows // 32)
    def _(chunk):
        total = jnp.zeros((32, 128), f32)
        for b in range(BLOCKS):
            for t in range(3):
                at = pl.ds(pl.multiple_of(t * rows + chunk * 32, 32), 32)
                part = x_ref[b, at, :].astype(f32)
                total = total + part * part
        squares[pl.ds(pl.multiple_of(chunk * 32, 32), 32), :] = total

    @pl.loop(0, half // 32)
    def _(chunk):
        total = jnp.zeros((32, 128), f32)
        at = pl.ds(pl.multiple_of(3 * rows + chunk * 32, 32), 32)
        for b in range(BLOCKS):
            part = x_ref[b, at, :].astype(f32)
            total = total + part * part
        folds[pl.ds(pl.multiple_of(chunk * 32, 32), 32), :] = total

    rest = folds[...]
    rest = jnp.concatenate(
        [jnp.sum(rest[:, :64], -1, keepdims=True), jnp.sum(rest[:, 64:], -1, keepdims=True)], 0
    )
    mean = (jnp.sum(squares[...], -1, keepdims=True) + rest) / (BLOCKS * 448)
    inverse[...] = jnp.broadcast_to(lax.rsqrt(mean + epsilon), inverse.shape)
    for b in range(BLOCKS):
        gain = x_ref[b, 3 * rows + half : 3 * rows + half + 16, :].astype(f32)
        for t in range(3):
            part = x_ref[b, t * rows : (t + 1) * rows, :].astype(f32)
            out_ref[b, :, 128 * t : 128 * t + 128] = (
                part * inverse[...] * gain[t : t + 1]
            ).astype(bf16)
        part = unfolded(x_ref[b, 3 * rows : 3 * rows + half, :]).astype(f32)
        out_ref[b, :, 384:448] = (part * inverse[:, :64] * gain[3:4, :64]).astype(bf16)


def norm(gathered, rows):
    return pl.pallas_call(
        norm_kernel,
        out_shape=jax.ShapeDtypeStruct((BLOCKS, rows, 448), bf16),
        in_specs=[whole()],
        out_specs=whole(),
        scratch_shapes=[
            pltpu.VMEM((rows, 128), f32),
            pltpu.VMEM((rows // 2, 128), f32),
            pltpu.VMEM((rows, 128), f32),
        ],
        compiler_params=params(16),
        cost_estimate=pl.CostEstimate(flops=10**7, bytes_accessed=8 * 10**6, transcendentals=0),
        name="norm",
    )(gathered)


def project_kernel(count, start, last, order, normed_ref, *refs):
    weights, rest = refs[:count], refs[count:]
    if start == 0:
        outs, total = rest, None
    else:
        total, outs = rest[0][...], rest[1:]
    for k in range(count):
        normed = normed_ref[order[start + k]]
        both = jnp.dot(normed, weights[k][:448, :], preferred_element_type=f32)
        value = lax.dot_general(
            normed, weights[k][448:, :448], (((1,), (1,)), ((), ())), preferred_element_type=f32
        )
        term = jnp.concatenate([both, value], 1)
        total = term if total is None else total + term
    if last:
        half = total.shape[0] // 2
        rounded = total.astype(bf16)
        for h in range(2):
            outs[h][...] = rounded[h * half : (h + 1) * half]
    else:
        outs[0][...] = total


def project(start, last, order, normed, slots, *total):
    rows, count = normed.shape[1], len(slots)
    if last:
        shape = [jax.ShapeDtypeStruct((rows // 2, 576), bf16)] * 2
    else:
        shape = [jax.ShapeDtypeStruct((rows, 576), f32)]
    return pl.pallas_call(
        functools.partial(project_kernel, count, start, last),
        out_shape=shape,
        in_specs=[scalars()] + [whole()] * (1 + count + len(total)),
        out_specs=[whole()] * len(shape),
        compiler_params=params(20),
        cost_estimate=pl.CostEstimate(
            flops=2 * rows * 448 * 576 * count, bytes_accessed=10**6 * count, transcendentals=0
        ),
        name="project",
    )(order, normed, *slots, *total)


def attention_kernel(
    facts, own_ref, oth_ref, cos_ref, sin_ref, reach_ref, pick_ref, key_ref, value_ref,
    kept_ref, sent_ref, stats_ref, chosen_ref, scores,
):
    request = pl.program_id(0)
    first = facts[0] == 0
    count = facts[1 + request]
    nodes = own_ref.shape[0]
    q_cols = 448
    cosine, sine = cos_ref[...], sin_ref[...]
    own, other = own_ref[...].astype(f32), oth_ref[...].astype(f32)

    def paired(lo, hi):
        low = jnp.where(first, own[:, lo:hi], other[:, lo:hi])
        high = jnp.where(first, other[:, lo:hi], own[:, lo:hi])
        return jnp.concatenate([low, high], 1)

    def turned(u):
        return (u * cosine + pltpu.roll(u, 64, 1) * sine).astype(bf16)

    query = paired(0, q_cols)
    queries = jnp.concatenate(
        [turned(query[:, 128 * g : 128 * g + 128]) for g in range(GROUP)], 0
    )
    rot_key = turned(paired(448, 512))
    node_value = paired(512, 576).astype(bf16)

    wide = rot_key.astype(f32)
    own_key = jnp.where(first, wide[:, :64], wide[:, 64:])
    kv_rows = jnp.concatenate([own_key, own[:, 512:576]], 1).astype(bf16)
    chosen_ref[0] = jnp.dot(pick_ref[0], kv_rows, preferred_element_type=f32).astype(bf16)

    pieces, rows, span = scores.shape
    nt = (((1,), (1,)), ((), ()))
    tree = lax.dot_general(queries, rot_key, nt, preferred_element_type=f32)
    reach = jnp.concatenate([reach_ref[0]] * GROUP, 0)
    tree = jnp.where(jnp.logical_and(reach > 0.5, first), tree, masked_score)
    highest = jnp.full((rows, 128), masked_score, f32)
    for c in range(pieces):
        part = lax.dot_general(
            queries, key_ref[0, c * span : (c + 1) * span, :], nt, preferred_element_type=f32
        )
        live = lax.broadcasted_iota(jnp.int32, (1, span), 1) + c * span < count
        part = jnp.where(live, part, masked_score)
        scores[c] = part
        for t in range(span // 128):
            highest = jnp.maximum(highest, part[:, 128 * t : 128 * t + 128])
    highest = jnp.maximum(
        jnp.max(highest, -1, keepdims=True), jnp.max(tree, -1, keepdims=True)
    )

    factor = math.log2(math.e) / math.sqrt(128.0)
    ones = jnp.ones((span, 128), bf16)
    weights = jnp.exp2((tree - highest) * factor).astype(bf16)
    summed = jnp.dot(
        weights, jnp.concatenate([node_value, ones[:nodes]], 1), preferred_element_type=f32
    )
    for c in range(pieces):
        weights = jnp.exp2((scores[c] - highest) * factor).astype(bf16)
        values = jnp.concatenate([value_ref[0, c * span : (c + 1) * span, :], ones], 1)
        summed = summed + jnp.dot(weights, values, preferred_element_type=f32)

    total = summed[:, 128:129]
    mean = summed[:, :128] / total
    some = jnp.logical_or(first, count > 0)
    level = jnp.where(some, highest * (1.0 / math.sqrt(128.0)) + jnp.log(total), masked_score)
    every = jnp.concatenate([mean[g * nodes : (g + 1) * nodes] for g in range(GROUP)], 1)
    low, high = every[:, :q_cols], every[:, q_cols:]
    kept_ref[...] = jnp.where(first, low, high)
    levels = jnp.concatenate(
        [level[g * nodes : (g + 1) * nodes] for g in range(GROUP)]
        + [jnp.zeros((nodes, 128 - GROUP), f32)], 1,
    )
    stats_ref[...] = levels
    coarse = levels[:, :16].astype(bf16).astype(f32)
    finer = (levels[:, :16] - coarse).astype(bf16).astype(f32)
    finest = levels[:, :16] - coarse - finer
    sent_ref[...] = jnp.concatenate(
        [jnp.where(first, high, low), coarse, finer, finest, jnp.zeros((nodes, 16), f32)], 1
    ).astype(bf16)


def attention(half, facts, own, other, cosine, sine, reach, pick, keys, values):
    half_len, head = keys.shape[-2:]
    requests = keys.shape[0] // 2
    nodes = own.shape[0] // requests
    columns = own.shape[1]
    base = half * requests

    def rows_of(width, at=0):
        return pl.BlockSpec((nodes, width), lambda r, facts: (at + r, 0))

    def request_of(*shape, at=0):
        return pl.BlockSpec((1,) + shape, lambda r, facts: (at + r, 0, 0))

    span = 512
    return pl.pallas_call(
        attention_kernel,
        grid_spec=pltpu.PrefetchScalarGridSpec(
            num_scalar_prefetch=1,
            grid=(requests,),
            in_specs=[
                rows_of(columns), rows_of(columns), rows_of(head, base), rows_of(head, base),
                request_of(nodes, nodes, at=base), request_of(*pick.shape[1:], at=base),
                request_of(half_len, head, at=base), request_of(half_len, head, at=base),
            ],
            out_specs=[rows_of(448), rows_of(512), rows_of(128), request_of(pick.shape[1], 128)],
            scratch_shapes=[pltpu.VMEM((half_len // span, GROUP * nodes, span), f32)],
        ),
        out_shape=[
            jax.ShapeDtypeStruct((requests * nodes, 448), f32),
            jax.ShapeDtypeStruct((requests * nodes, 512), bf16),
            jax.ShapeDtypeStruct((requests * nodes, 128), f32),
            jax.ShapeDtypeStruct((requests, pick.shape[1], 128), bf16),
        ],
        compiler_params=params(14),
        cost_estimate=pl.CostEstimate(
            flops=requests * ATTENTION_COST,
            bytes_accessed=requests * 2**20,
            transcendentals=requests * 448 * 2112,
        ),
        name="attention",
    )(facts, own, other, cosine, sine, reach, pick, keys, values)


def attend(facts, kept_ref, stats_ref, got_ref, valid_ref):
    first = facts[0] == 0
    got = got_ref[...].astype(f32)
    theirs = got[:, 448:464] + got[:, 464:480] + got[:, 480:496]
    ours = stats_ref[:, :16]
    highest = jnp.maximum(ours, theirs)
    own_factor = jnp.exp(ours - highest)
    other_factor = jnp.exp(theirs - highest)
    both = own_factor + other_factor

    def spread(part):
        rows = part.shape[0]
        every = jnp.concatenate(
            [jnp.broadcast_to(part[:, g : g + 1], (rows, 128)) for g in range(GROUP)], 1
        )
        return jnp.where(first, every[:, :448], every[:, 448:])

    mixed = kept_ref[...] * spread(own_factor / both) + got[:, :448] * spread(other_factor / both)
    return mixed.astype(bf16) * valid_ref[...]


def combine_kernel(place, *refs):
    out_ref = refs[8]
    rows = out_ref.shape[0] // 2
    for h in range(2):
        out_ref[h * rows : (h + 1) * rows, :] = attend(place, *refs[4 * h : 4 * h + 4])


def combine(place, arrays):
    return pl.pallas_call(
        combine_kernel,
        out_shape=jax.ShapeDtypeStruct((2 * arrays[0].shape[0], 448), bf16),
        in_specs=[scalars()] + [whole()] * 8,
        out_specs=whole(),
        compiler_params=params(8),
        name="combine",
    )(place, *arrays)


def out_kernel(steps, place, att_ref, weight_hbm, *refs):
    outs, (weight_ref, arrival) = refs[: len(steps)], refs[len(steps) :]
    rows = att_ref.shape[0]
    copies = []
    for step in steps:
        for along in range(SIDE):
            block = lax.rem(place[3] + step, SIDE) * place[1] + along * place[2]
            slot = len(copies)
            copies.append(
                pltpu.make_async_copy(weight_hbm.at[block], weight_ref.at[slot], arrival.at[slot])
            )
            copies[slot].start()
    for slot, copy in enumerate(copies):
        copy.wait()
        out, along = outs[slot // SIDE], slot % SIDE
        terms = jnp.dot(att_ref[...], weight_ref[slot], preferred_element_type=f32)
        for t in range(3):
            out[along, t * rows : (t + 1) * rows, :] = terms[:, 128 * t : 128 * t + 128].astype(out.dtype)
        out[along, 3 * rows :, :] = folded(terms[:, 384:]).astype(out.dtype)


def out_terms(steps, place, attended, weights):
    rows = attended.shape[0] * 7 // 2
    return pl.pallas_call(
        functools.partial(out_kernel, steps),
        out_shape=[
            jax.ShapeDtypeStruct((SIDE, rows, 128), bf16 if step else f32) for step in steps
        ],
        in_specs=[scalars(), whole(), pl.BlockSpec(memory_space=pl.ANY)],
        out_specs=[whole()] * len(steps),
        scratch_shapes=[
            pltpu.VMEM((SIDE * len(steps),) + weights.shape[1:], bf16),
            pltpu.SemaphoreType.DMA((SIDE * len(steps),)),
        ],
        compiler_params=params(58),
        cost_estimate=pl.CostEstimate(flops=2 * 10**10, bytes_accessed=2 * 10**7, transcendentals=0),
        name="out_terms",
    )(place, attended, weights)


def partial_kernel(place, own_ref, *refs):
    got, outs = refs[:3], refs[3:]
    for step in range(SIDE):
        at = lax.rem(place[0] + step, SIDE)
        value = own_ref[at]
        for part in got:
            value = value + part[at].astype(f32)
        outs[step][...] = value.astype(outs[step].dtype)


def partial_sums(place, own, got):
    shape = own.shape[1:]
    return pl.pallas_call(
        partial_kernel,
        out_shape=[jax.ShapeDtypeStruct(shape, bf16 if step else f32) for step in range(SIDE)],
        in_specs=[scalars()] + [whole()] * 4,
        out_specs=[whole()] * SIDE,
        compiler_params=params(16),
        name="partial_sums",
    )(place, own, *got)


def final_kernel(hidden_ref, own_ref, *refs):
    got, out_ref = refs[:3], refs[3]
    rows = hidden_ref.shape[0]
    value = own_ref[...]
    for part in got:
        value = value + part[...].astype(f32)
    dense = jnp.concatenate(
        [value[t * rows : (t + 1) * rows] for t in range(3)] + [unfolded(value[3 * rows :])], 1
    )
    out_ref[...] = (hidden_ref[...].astype(f32) + dense).astype(bf16)


def final(hidden, parts):
    return pl.pallas_call(
        final_kernel,
        out_shape=jax.ShapeDtypeStruct(hidden.shape, bf16),
        in_specs=[whole()] * 5,
        out_specs=whole(),
        compiler_params=params(12),
        name="final",
    )(hidden, *parts)


def two_way(block):
    dp = lax.axis_index("dp")
    slots, order = [block, other_core(block)], [dp, dp ^ 1]
    up = down = block
    for step in range(1, 4):
        up, down = along_z(up, 1), along_z(down, -1)
        slots += [up, down, other_core(up), other_core(down)]
        order += [dp - 2 * step, dp + 2 * step, (dp ^ 1) - 2 * step, (dp ^ 1) + 2 * step]
    upper, lower = cut_blocks(up, down)
    halves = along_z(upper, 1), along_z(lower, -1)
    order += [dp + 8, (dp ^ 1) + 8]
    return slots, halves, (jnp.stack(order) % DP).astype(jnp.int32)


def shards(
    hidden_in,
    norm_gain,
    w_query,
    w_key,
    w_value,
    w_out,
    key_cache,
    value_cache,
    cache_len,
    tree_parent,
    valid_nodes,
    accepted_path,
    slot_owner,
):
    req_dev, tree_size, part_width = hidden_in.shape
    row_count = req_dev * tree_size
    head_dim = key_cache.shape[-1]
    half_len = key_cache.shape[3]
    dp, mp = lax.axis_index("dp"), lax.axis_index("mp")
    z, core = dp // CORES, dp % CORES
    x, y = mp // SIDE, mp % SIDE
    me_first, me_second = jnp.where(core == 0, y, x), jnp.where(core == 0, x, y)
    half_index = mp % 2
    hidden = hidden_in.reshape(row_count, part_width)

    packed, weights = pack(hidden, norm_gain[None], w_query, w_key, w_value.T)

    slots, halves, order = two_way(weights)

    gathered = lax.all_gather(packed, "mp")

    out_weights = lax.all_gather(w_out, "dp")
    strides = jnp.where(core == 0, jnp.array([1, SIDE]), jnp.array([SIDE, 1]))
    place = jnp.concatenate([half_index[None], strides, me_first[None]]).astype(jnp.int32)

    reach = tree_closure(tree_parent)
    depth = jnp.sum(reach, -1) - 1.0
    position = (cache_len[:, None].astype(f32) + depth).reshape(row_count, 1)
    half_dim = head_dim // 2
    inverse = jnp.exp(
        jnp.arange(half_dim, dtype=f32) * (-2.0 * math.log(rope_base) / head_dim)
    )
    angles = position * inverse
    cosine, sine = jnp.cos(angles), jnp.sin(angles)
    cosine = jnp.concatenate([cosine, cosine], -1)
    sine = jnp.concatenate([-sine, sine], -1)
    picks = accepted_path.shape[1]
    pick = (
        jnp.pad(accepted_path, ((0, 0), (0, 16 - picks)))[..., None]
        == jnp.arange(tree_size, dtype=jnp.int32)
    ).astype(bf16)
    counts = jnp.clip(cache_len - half_index * half_len, 0, half_len)
    valid = valid_nodes.reshape(row_count, 1).astype(bf16)

    normed = norm(gathered, row_count)
    furthest = join(*halves)
    total = project(0, True, order, normed, slots + [furthest, other_core(furthest)])

    half_rows = row_count // 2
    others = [partner(own) for own in total]
    arrays, chosen = [], []
    for half, own in enumerate(total):
        at = slice(half * half_rows, (half + 1) * half_rows)
        group = slice(half * req_dev // 2, (half + 1) * req_dev // 2)
        facts = jnp.concatenate([half_index[None], counts[group]]).astype(jnp.int32)
        kept, sent, stats, rows = attention(
            half, facts, own, others[half], cosine, sine, reach, pick,
            key_cache[:, 0, 0], value_cache[:, 0, 0],
        )
        chosen.append(rows)
        arrays += [kept, stats, partner(sent), valid[at]]
    attended = combine(place, arrays)
    two, one = out_terms((2, 1), place, attended, out_weights)
    three, here = out_terms((3, 0), place, attended, out_weights)
    got = [first_axis(two, 2), first_axis(one, 1), first_axis(three, 3)]
    mine = partial_sums(me_second[None].astype(jnp.int32), here, got)
    parts = [mine[0]] + [second_axis(mine[s], s) for s in (2, 1, 3)]
    layer_out = final(hidden, parts).reshape(req_dev, tree_size, part_width)

    rows = jnp.pad(jnp.concatenate(chosen), ((0, 0), (0, 80 - chosen[0].shape[1]), (0, 0)))
    every_row = lax.all_gather(rows, "dp", axis=0, tiled=True)[:, :picks]
    total_reqs = slot_owner.shape[0]
    my_slots = dp * req_dev + jnp.arange(req_dev, dtype=jnp.int32)
    senders = (slot_owner[None, :] == my_slots[:, None]).astype(bf16)
    accepted_kv = (
        jnp.dot(senders, every_row.reshape(total_reqs, -1), preferred_element_type=f32)
        .astype(bf16)
        .reshape(req_dev, picks, 2, -1)
    )
    return (layer_out, accepted_kv)


def solution(mesh):
    placed = (
        P("dp", None, "mp"),
        P("mp"),
        P("dp", "mp"),
        P("dp", "mp"),
        P("dp", "mp"),
        P("mp", "dp"),
        P("dp", "mp", None, None, None),
        P("dp", "mp", None, None, None),
        P("dp"),
        P("dp", None),
        P("dp", None),
        P("dp", None),
        P(),
    )
    return jax.shard_map(
        shards,
        mesh=mesh,
        in_specs=placed,
        out_specs=(P("dp", None, "mp"), P("dp", None, None, "mp")),
        check_vma=False,
    )
```

```python
import functools
import math

import jax
import jax.numpy as jnp
from jax import lax
from jax.experimental import pallas as pl
from jax.experimental.pallas import tpu as pltpu
from jax.sharding import PartitionSpec as P

GROUP = 7
SIDE = 4
epsilon = 1e-05
rope_base = 5000000.0
masked_score = -1e30
bf16 = jnp.bfloat16
f32 = jnp.float32
VMEM = pltpu.VMEM


def whole():
    return pl.BlockSpec(memory_space=VMEM)


def scalars():
    return pl.BlockSpec(memory_space=pltpu.SMEM)


def params(mib):
    return pltpu.CompilerParams(vmem_limit_bytes=mib * 2**20)


DP, CORES, Z = 16, 2, 8
BLOCKS = 16
CUT_COST = 2 * 10**10
ATTENTION_COST = 25 * 10**9


def moved(block, target):
    route = []
    for d in range(DP):
        for m in range(SIDE * SIDE):
            z, core, x, y = target(d // CORES, d % CORES, m // SIDE, m % SIDE)
            to = (z % Z * CORES + core) * SIDE * SIDE + x % SIDE * SIDE + y % SIDE
            route.append((d * SIDE * SIDE + m, to))
    return lax.ppermute(block, ("dp", "mp"), route)


def other_core(block):
    return moved(block, lambda z, c, x, y: (z, c ^ 1, x, y))


def along_z(block, step):
    return moved(block, lambda z, c, x, y: (z + step, c, x, y))


def first_axis(block, step):
    return moved(block, lambda z, c, x, y: (z, c, x, y + step) if c == 0 else (z, c, x + step, y))


def second_axis(block, step):
    return moved(block, lambda z, c, x, y: (z, c, x + step, y) if c == 0 else (z, c, x, y + step))


def partner(block):
    return moved(block, lambda z, c, x, y: (z, c, x, y ^ 1))


def tree_closure(parents):
    width = parents.shape[-1]
    nodes = jnp.arange(width, dtype=jnp.int32)
    onehot = (parents[..., None] == nodes).astype(f32)
    reach = jnp.minimum(jnp.eye(width, dtype=f32) + onehot, 1.0)
    for _ in range((width - 1).bit_length()):
        small = reach.astype(bf16)
        reach = jnp.minimum(
            jnp.einsum("rij,rjk->rik", small, small, preferred_element_type=f32), 1.0
        )
    return reach


def unfolded(tile):
    wide = tile.astype(f32)
    return jnp.concatenate([wide[:, :64], wide[:, 64:]], 0).astype(tile.dtype)


def folded(array):
    half = array.shape[0] // 2
    wide = array.astype(f32)
    return jnp.concatenate([wide[:half], wide[half:]], 1).astype(array.dtype)


def pack_kernel(hidden_ref, gain_ref, x_ref):
    rows = hidden_ref.shape[0]
    for t in range(3):
        x_ref[t * rows : (t + 1) * rows, :] = hidden_ref[:, 128 * t : 128 * t + 128]
    x_ref[3 * rows : 3 * rows + rows // 2, :] = folded(hidden_ref[:, 384:448])
    gain = gain_ref[...].astype(f32).reshape(1, 448)
    gain = jnp.concatenate([gain, jnp.zeros((1, 64), f32)], 1)
    gain = jnp.concatenate(
        [gain[:, 128 * t : 128 * t + 128] for t in range(4)] + [jnp.zeros((28, 128), f32)], 0
    )
    x_ref[3 * rows + rows // 2 :, :] = gain.astype(bf16)


def pack(hidden, gain):
    rows = hidden.shape[0]
    return pl.pallas_call(
        pack_kernel,
        out_shape=jax.ShapeDtypeStruct((rows * 7 // 2 + 32, 128), bf16),
        in_specs=[whole()] * 2,
        out_specs=whole(),
        compiler_params=params(60),
        name="pack",
    )(hidden, gain)


def pack_weights_kernel(query_ref, key_ref, value_ref, w_ref):
    w_ref[:448, :384] = query_ref[:, :384]
    key = jnp.concatenate([key_ref[...].astype(f32), jnp.zeros((64, 64), f32)], 1).T
    w_ref[:448, 384:] = jnp.concatenate([query_ref[:, 384:448].astype(f32), key[:448]], 1).astype(bf16)
    w_ref[448:, :] = jnp.concatenate([value_ref[...].astype(f32), jnp.zeros((64, 64), f32)], 1).astype(bf16)


def pack_weights(w_query, w_key, w_value):
    return pl.pallas_call(
        pack_weights_kernel,
        out_shape=jax.ShapeDtypeStruct((512, 512), bf16),
        in_specs=[whole()] * 3,
        out_specs=whole(),
        compiler_params=params(60),
        name="pack_weights",
    )(w_query, w_key, w_value)


def join_kernel(upper_ref, lower_ref, out_ref):
    cut = upper_ref.shape[0]
    out_ref[:cut, :] = upper_ref[...]
    out_ref[cut:, :] = lower_ref[...]


def join(upper, lower):
    return pl.pallas_call(
        join_kernel,
        out_shape=jax.ShapeDtypeStruct((2 * upper.shape[0], upper.shape[1]), bf16),
        in_specs=[whole(), whole()],
        out_specs=whole(),
        compiler_params=params(4),
        name="join",
    )(upper, lower)


def cut_kernel(up_ref, down_ref, upper_ref, lower_ref):
    cut = upper_ref.shape[0]
    upper_ref[...] = up_ref[:cut, :]
    lower_ref[...] = down_ref[cut:, :]


def cut_blocks(up, down):
    half = jax.ShapeDtypeStruct((up.shape[0] // 2, up.shape[1]), bf16)
    return pl.pallas_call(
        cut_kernel,
        out_shape=[half, half],
        in_specs=[whole(), whole()],
        out_specs=[whole(), whole()],
        compiler_params=params(4),
        cost_estimate=pl.CostEstimate(flops=CUT_COST, bytes_accessed=10**6, transcendentals=0),
        name="cut_blocks",
    )(up, down)


def norm_kernel(x_ref, out_ref, squares, folds, inverse):
    rows = out_ref.shape[1]
    half = rows // 2

    @pl.loop(0, rows // 32)
    def _(chunk):
        total = jnp.zeros((32, 128), f32)
        for b in range(BLOCKS):
            for t in range(3):
                at = pl.ds(pl.multiple_of(t * rows + chunk * 32, 32), 32)
                part = x_ref[b, at, :].astype(f32)
                total = total + part * part
        squares[pl.ds(pl.multiple_of(chunk * 32, 32), 32), :] = total

    @pl.loop(0, half // 32)
    def _(chunk):
        total = jnp.zeros((32, 128), f32)
        at = pl.ds(pl.multiple_of(3 * rows + chunk * 32, 32), 32)
        for b in range(BLOCKS):
            part = x_ref[b, at, :].astype(f32)
            total = total + part * part
        folds[pl.ds(pl.multiple_of(chunk * 32, 32), 32), :] = total

    rest = folds[...]
    rest = jnp.concatenate(
        [jnp.sum(rest[:, :64], -1, keepdims=True), jnp.sum(rest[:, 64:], -1, keepdims=True)], 0
    )
    mean = (jnp.sum(squares[...], -1, keepdims=True) + rest) / (BLOCKS * 448)
    inverse[...] = jnp.broadcast_to(lax.rsqrt(mean + epsilon), inverse.shape)
    for b in range(BLOCKS):
        gain = x_ref[b, 3 * rows + half : 3 * rows + half + 16, :].astype(f32)
        for t in range(3):
            part = x_ref[b, t * rows : (t + 1) * rows, :].astype(f32)
            out_ref[b, :, 128 * t : 128 * t + 128] = (
                part * inverse[...] * gain[t : t + 1]
            ).astype(bf16)
        part = unfolded(x_ref[b, 3 * rows : 3 * rows + half, :]).astype(f32)
        out_ref[b, :, 384:448] = (part * inverse[:, :64] * gain[3:4, :64]).astype(bf16)


def norm(gathered, rows):
    return pl.pallas_call(
        norm_kernel,
        out_shape=jax.ShapeDtypeStruct((BLOCKS, rows, 448), bf16),
        in_specs=[whole()],
        out_specs=whole(),
        scratch_shapes=[
            pltpu.VMEM((rows, 128), f32),
            pltpu.VMEM((rows // 2, 128), f32),
            pltpu.VMEM((rows, 128), f32),
        ],
        compiler_params=params(16),
        cost_estimate=pl.CostEstimate(flops=10**7, bytes_accessed=8 * 10**6, transcendentals=0),
        name="norm",
    )(gathered)


def project_kernel(count, start, last, order, normed_ref, *refs):
    weights, rest = refs[:count], refs[count:]
    if start == 0:
        outs, total = rest, None
    else:
        total, outs = rest[0][...], rest[1:]
    for k in range(count):
        normed = normed_ref[order[start + k]]
        both = jnp.dot(normed, weights[k][:448, :], preferred_element_type=f32)
        value = lax.dot_general(
            normed, weights[k][448:, :448], (((1,), (1,)), ((), ())), preferred_element_type=f32
        )
        term = jnp.concatenate([both, value], 1)
        total = term if total is None else total + term
    if last:
        half = total.shape[0] // 2
        rounded = total.astype(bf16)
        for h in range(2):
            outs[h][...] = rounded[h * half : (h + 1) * half]
    else:
        outs[0][...] = total


def project(start, last, order, normed, slots, *total):
    rows, count = normed.shape[1], len(slots)
    if last:
        shape = [jax.ShapeDtypeStruct((rows // 2, 576), bf16)] * 2
    else:
        shape = [jax.ShapeDtypeStruct((rows, 576), f32)]
    return pl.pallas_call(
        functools.partial(project_kernel, count, start, last),
        out_shape=shape,
        in_specs=[scalars()] + [whole()] * (1 + count + len(total)),
        out_specs=[whole()] * len(shape),
        compiler_params=params(20),
        cost_estimate=pl.CostEstimate(
            flops=2 * rows * 448 * 576 * count, bytes_accessed=10**6 * count, transcendentals=0
        ),
        name="project",
    )(order, normed, *slots, *total)


def attention_kernel(
    facts, own_ref, oth_ref, cos_ref, sin_ref, reach_ref, pick_ref, key_ref, value_ref,
    kept_ref, sent_ref, stats_ref, chosen_ref, scores,
):
    request = pl.program_id(0)
    first = facts[0] == 0
    count = facts[1 + request]
    nodes = own_ref.shape[0]
    q_cols = 448
    cosine, sine = cos_ref[...], sin_ref[...]
    own, other = own_ref[...].astype(f32), oth_ref[...].astype(f32)

    def paired(lo, hi):
        low = jnp.where(first, own[:, lo:hi], other[:, lo:hi])
        high = jnp.where(first, other[:, lo:hi], own[:, lo:hi])
        return jnp.concatenate([low, high], 1)

    def turned(u):
        return (u * cosine + pltpu.roll(u, 64, 1) * sine).astype(bf16)

    query = paired(0, q_cols)
    queries = jnp.concatenate(
        [turned(query[:, 128 * g : 128 * g + 128]) for g in range(GROUP)], 0
    )
    rot_key = turned(paired(448, 512))
    node_value = paired(512, 576).astype(bf16)

    wide = rot_key.astype(f32)
    own_key = jnp.where(first, wide[:, :64], wide[:, 64:])
    kv_rows = jnp.concatenate([own_key, own[:, 512:576]], 1).astype(bf16)
    chosen_ref[0] = jnp.dot(pick_ref[0], kv_rows, preferred_element_type=f32).astype(bf16)

    pieces, rows, span = scores.shape
    nt = (((1,), (1,)), ((), ()))
    tree = lax.dot_general(queries, rot_key, nt, preferred_element_type=f32)
    reach = jnp.concatenate([reach_ref[0]] * GROUP, 0)
    tree = jnp.where(jnp.logical_and(reach > 0.5, first), tree, masked_score)
    highest = jnp.full((rows, 128), masked_score, f32)
    for c in range(pieces):
        part = lax.dot_general(
            queries, key_ref[0, c * span : (c + 1) * span, :], nt, preferred_element_type=f32
        )
        live = lax.broadcasted_iota(jnp.int32, (1, span), 1) + c * span < count
        part = jnp.where(live, part, masked_score)
        scores[c] = part
        for t in range(span // 128):
            highest = jnp.maximum(highest, part[:, 128 * t : 128 * t + 128])
    highest = jnp.maximum(
        jnp.max(highest, -1, keepdims=True), jnp.max(tree, -1, keepdims=True)
    )

    factor = math.log2(math.e) / math.sqrt(128.0)
    ones = jnp.ones((span, 128), bf16)
    weights = jnp.exp2((tree - highest) * factor).astype(bf16)
    summed = jnp.dot(
        weights, jnp.concatenate([node_value, ones[:nodes]], 1), preferred_element_type=f32
    )
    for c in range(pieces):
        weights = jnp.exp2((scores[c] - highest) * factor).astype(bf16)
        values = jnp.concatenate([value_ref[0, c * span : (c + 1) * span, :], ones], 1)
        summed = summed + jnp.dot(weights, values, preferred_element_type=f32)

    total = summed[:, 128:129]
    mean = summed[:, :128] / total
    some = jnp.logical_or(first, count > 0)
    level = jnp.where(some, highest * (1.0 / math.sqrt(128.0)) + jnp.log(total), masked_score)
    every = jnp.concatenate([mean[g * nodes : (g + 1) * nodes] for g in range(GROUP)], 1)
    low, high = every[:, :q_cols], every[:, q_cols:]
    kept_ref[...] = jnp.where(first, low, high)
    levels = jnp.concatenate(
        [level[g * nodes : (g + 1) * nodes] for g in range(GROUP)]
        + [jnp.zeros((nodes, 128 - GROUP), f32)], 1,
    )
    stats_ref[...] = levels
    coarse = levels[:, :16].astype(bf16).astype(f32)
    finer = (levels[:, :16] - coarse).astype(bf16).astype(f32)
    finest = levels[:, :16] - coarse - finer
    sent_ref[...] = jnp.concatenate(
        [jnp.where(first, high, low), coarse, finer, finest, jnp.zeros((nodes, 16), f32)], 1
    ).astype(bf16)


def attention(half, facts, own, other, cosine, sine, reach, pick, keys, values):
    half_len, head = keys.shape[-2:]
    requests = keys.shape[0] // 2
    nodes = own.shape[0] // requests
    columns = own.shape[1]
    base = half * requests

    def rows_of(width, at=0):
        return pl.BlockSpec((nodes, width), lambda r, facts: (at + r, 0))

    def request_of(*shape, at=0):
        return pl.BlockSpec((1,) + shape, lambda r, facts: (at + r, 0, 0))

    span = 512
    return pl.pallas_call(
        attention_kernel,
        grid_spec=pltpu.PrefetchScalarGridSpec(
            num_scalar_prefetch=1,
            grid=(requests,),
            in_specs=[
                rows_of(columns), rows_of(columns), rows_of(head, base), rows_of(head, base),
                request_of(nodes, nodes, at=base), request_of(*pick.shape[1:], at=base),
                request_of(half_len, head, at=base), request_of(half_len, head, at=base),
            ],
            out_specs=[rows_of(448), rows_of(512), rows_of(128), request_of(pick.shape[1], 128)],
            scratch_shapes=[pltpu.VMEM((half_len // span, GROUP * nodes, span), f32)],
        ),
        out_shape=[
            jax.ShapeDtypeStruct((requests * nodes, 448), f32),
            jax.ShapeDtypeStruct((requests * nodes, 512), bf16),
            jax.ShapeDtypeStruct((requests * nodes, 128), f32),
            jax.ShapeDtypeStruct((requests, pick.shape[1], 128), bf16),
        ],
        compiler_params=params(56),
        cost_estimate=pl.CostEstimate(
            flops=requests * ATTENTION_COST,
            bytes_accessed=requests * 2**20,
            transcendentals=requests * 448 * 2112,
        ),
        name="attention",
    )(facts, own, other, cosine, sine, reach, pick, keys, values)


def attend(facts, kept_ref, stats_ref, got_ref, valid_ref):
    first = facts[0] == 0
    got = got_ref[...].astype(f32)
    theirs = got[:, 448:464] + got[:, 464:480] + got[:, 480:496]
    ours = stats_ref[:, :16]
    highest = jnp.maximum(ours, theirs)
    own_factor = jnp.exp(ours - highest)
    other_factor = jnp.exp(theirs - highest)
    both = own_factor + other_factor

    def spread(part):
        rows = part.shape[0]
        every = jnp.concatenate(
            [jnp.broadcast_to(part[:, g : g + 1], (rows, 128)) for g in range(GROUP)], 1
        )
        return jnp.where(first, every[:, :448], every[:, 448:])

    mixed = kept_ref[...] * spread(own_factor / both) + got[:, :448] * spread(other_factor / both)
    return mixed.astype(bf16) * valid_ref[...]


def combine_kernel(place, *refs):
    out_ref = refs[8]
    rows = out_ref.shape[0] // 2
    for h in range(2):
        out_ref[h * rows : (h + 1) * rows, :] = attend(place, *refs[4 * h : 4 * h + 4])


def combine(place, arrays):
    return pl.pallas_call(
        combine_kernel,
        out_shape=jax.ShapeDtypeStruct((2 * arrays[0].shape[0], 448), bf16),
        in_specs=[scalars()] + [whole()] * 8,
        out_specs=whole(),
        compiler_params=params(56),
        name="combine",
    )(place, *arrays)


def out_kernel(steps, place, att_ref, weight_ref, *outs):
    rows = att_ref.shape[0]
    for out, step in zip(outs, steps):
        for along in range(SIDE):
            block = lax.rem(place[3] + step, SIDE) * place[1] + along * place[2]
            terms = jnp.dot(att_ref[...], weight_ref[block], preferred_element_type=f32)
            for t in range(3):
                out[along, t * rows : (t + 1) * rows, :] = terms[:, 128 * t : 128 * t + 128].astype(out.dtype)
            out[along, 3 * rows :, :] = folded(terms[:, 384:]).astype(out.dtype)


def out_terms(steps, place, attended, weights):
    rows = attended.shape[0] * 7 // 2
    return pl.pallas_call(
        functools.partial(out_kernel, steps),
        out_shape=[
            jax.ShapeDtypeStruct((SIDE, rows, 128), bf16 if step else f32) for step in steps
        ],
        in_specs=[scalars(), whole(), whole()],
        out_specs=[whole()] * len(steps),
        compiler_params=params(16),
        cost_estimate=pl.CostEstimate(
            flops=2 * 10**10, bytes_accessed=2 * 10**7, transcendentals=0
        ),
        name="out_terms",
    )(place, attended, weights)


def partial_kernel(place, own_ref, *refs):
    got, outs = refs[:3], refs[3:]
    for step in range(SIDE):
        at = lax.rem(place[0] + step, SIDE)
        value = own_ref[at]
        for part in got:
            value = value + part[at].astype(f32)
        outs[step][...] = value.astype(outs[step].dtype)


def partial_sums(place, own, got):
    shape = own.shape[1:]
    return pl.pallas_call(
        partial_kernel,
        out_shape=[jax.ShapeDtypeStruct(shape, bf16 if step else f32) for step in range(SIDE)],
        in_specs=[scalars()] + [whole()] * 4,
        out_specs=[whole()] * SIDE,
        compiler_params=params(16),
        name="partial_sums",
    )(place, own, *got)


def final_kernel(hidden_ref, own_ref, *refs):
    got, out_ref = refs[:3], refs[3]
    rows = hidden_ref.shape[0]
    value = own_ref[...]
    for part in got:
        value = value + part[...].astype(f32)
    dense = jnp.concatenate(
        [value[t * rows : (t + 1) * rows] for t in range(3)] + [unfolded(value[3 * rows :])], 1
    )
    out_ref[...] = (hidden_ref[...].astype(f32) + dense).astype(bf16)


def final(hidden, parts):
    return pl.pallas_call(
        final_kernel,
        out_shape=jax.ShapeDtypeStruct(hidden.shape, bf16),
        in_specs=[whole()] * 5,
        out_specs=whole(),
        compiler_params=params(12),
        name="final",
    )(hidden, *parts)


def two_way(block):
    dp = lax.axis_index("dp")
    slots, order = [block, other_core(block)], [dp, dp ^ 1]
    up = down = block
    for step in range(1, 4):
        up, down = along_z(up, 1), along_z(down, -1)
        slots += [up, down, other_core(up), other_core(down)]
        order += [dp - 2 * step, dp + 2 * step, (dp ^ 1) - 2 * step, (dp ^ 1) + 2 * step]
    upper, lower = cut_blocks(up, down)
    halves = along_z(upper, 1), along_z(lower, -1)
    order += [dp + 8, (dp ^ 1) + 8]
    return slots, halves, (jnp.stack(order) % DP).astype(jnp.int32)


def shards(
    hidden_in,
    norm_gain,
    w_query,
    w_key,
    w_value,
    w_out,
    key_cache,
    value_cache,
    cache_len,
    tree_parent,
    valid_nodes,
    accepted_path,
    slot_owner,
):
    req_dev, tree_size, part_width = hidden_in.shape
    row_count = req_dev * tree_size
    head_dim = key_cache.shape[-1]
    half_len = key_cache.shape[3]
    dp, mp = lax.axis_index("dp"), lax.axis_index("mp")
    z, core = dp // CORES, dp % CORES
    x, y = mp // SIDE, mp % SIDE
    me_first, me_second = jnp.where(core == 0, y, x), jnp.where(core == 0, x, y)
    half_index = mp % 2
    hidden = hidden_in.reshape(row_count, part_width)

    packed = pack(hidden, norm_gain)
    weights = pack_weights(w_query, w_key.T, w_value.T)

    slots, halves, order = two_way(weights)

    gathered = lax.all_gather(packed, "mp")

    out_weights = lax.all_gather(w_out, "dp")
    strides = jnp.where(core == 0, jnp.array([1, SIDE]), jnp.array([SIDE, 1]))
    place = jnp.concatenate([half_index[None], strides, me_first[None]]).astype(jnp.int32)

    reach = tree_closure(tree_parent)
    depth = jnp.sum(reach, -1) - 1.0
    position = (cache_len[:, None].astype(f32) + depth).reshape(row_count, 1)
    half_dim = head_dim // 2
    inverse = jnp.exp(
        jnp.arange(half_dim, dtype=f32) * (-2.0 * math.log(rope_base) / head_dim)
    )
    angles = position * inverse
    cosine, sine = jnp.cos(angles), jnp.sin(angles)
    cosine = jnp.concatenate([cosine, cosine], -1)
    sine = jnp.concatenate([-sine, sine], -1)
    picks = accepted_path.shape[1]
    pick = (
        jnp.pad(accepted_path, ((0, 0), (0, 16 - picks)))[..., None]
        == jnp.arange(tree_size, dtype=jnp.int32)
    ).astype(bf16)
    counts = jnp.clip(cache_len - half_index * half_len, 0, half_len)
    valid = valid_nodes.reshape(row_count, 1).astype(bf16)

    normed = norm(gathered, row_count)
    furthest = join(*halves)
    total = project(0, True, order, normed, slots + [furthest, other_core(furthest)])

    half_rows = row_count // 2
    others = [partner(own) for own in total]
    arrays, chosen = [], []
    for half, own in enumerate(total):
        at = slice(half * half_rows, (half + 1) * half_rows)
        group = slice(half * req_dev // 2, (half + 1) * req_dev // 2)
        facts = jnp.concatenate([half_index[None], counts[group]]).astype(jnp.int32)
        kept, sent, stats, rows = attention(
            half, facts, own, others[half], cosine, sine, reach, pick,
            key_cache[:, 0, 0], value_cache[:, 0, 0],
        )
        chosen.append(rows)
        arrays += [kept, stats, partner(sent), valid[at]]
    attended = combine(place, arrays)
    two, one = out_terms((2, 1), place, attended, out_weights)
    three, here = out_terms((3, 0), place, attended, out_weights)
    got = [first_axis(two, 2), first_axis(one, 1), first_axis(three, 3)]
    mine = partial_sums(me_second[None].astype(jnp.int32), here, got)
    parts = [mine[0]] + [second_axis(mine[s], s) for s in (2, 1, 3)]
    layer_out = final(hidden, parts).reshape(req_dev, tree_size, part_width)

    rows = jnp.pad(jnp.concatenate(chosen), ((0, 0), (0, 80 - chosen[0].shape[1]), (0, 0)))
    every_row = lax.all_gather(rows, "dp", axis=0, tiled=True)[:, :picks]
    total_reqs = slot_owner.shape[0]
    my_slots = dp * req_dev + jnp.arange(req_dev, dtype=jnp.int32)
    senders = (slot_owner[None, :] == my_slots[:, None]).astype(bf16)
    accepted_kv = (
        jnp.dot(senders, every_row.reshape(total_reqs, -1), preferred_element_type=f32)
        .astype(bf16)
        .reshape(req_dev, picks, 2, -1)
    )
    return (layer_out, accepted_kv)


def solution(mesh):
    placed = (
        P("dp", None, "mp"),
        P("mp"),
        P("dp", "mp"),
        P("dp", "mp"),
        P("dp", "mp"),
        P("mp", "dp"),
        P("dp", "mp", None, None, None),
        P("dp", "mp", None, None, None),
        P("dp"),
        P("dp", None),
        P("dp", None),
        P("dp", None),
        P(),
    )
    return jax.shard_map(
        shards,
        mesh=mesh,
        in_specs=placed,
        out_specs=(P("dp", None, "mp"), P("dp", None, None, "mp")),
        check_vma=False,
    )
```

```python
import functools
import math

import jax
import jax.numpy as jnp
from jax import lax
from jax.experimental import pallas as pl
from jax.experimental.pallas import tpu as pltpu
from jax.sharding import PartitionSpec as P

GROUP = 7
SIDE = 4
epsilon = 1e-05
rope_base = 5000000.0
masked_score = -1e30
bf16 = jnp.bfloat16
f32 = jnp.float32
VMEM = pltpu.VMEM


def whole():
    return pl.BlockSpec(memory_space=VMEM)


def scalars():
    return pl.BlockSpec(memory_space=pltpu.SMEM)


def params(mib):
    return pltpu.CompilerParams(vmem_limit_bytes=mib * 2**20)


DP, CORES, Z = 16, 2, 8
BLOCKS = 16
CUT_COST = 2 * 10**10
ATTENTION_COST = 25 * 10**9


def moved(block, target):
    route = []
    for d in range(DP):
        for m in range(SIDE * SIDE):
            z, core, x, y = target(d // CORES, d % CORES, m // SIDE, m % SIDE)
            to = (z % Z * CORES + core) * SIDE * SIDE + x % SIDE * SIDE + y % SIDE
            route.append((d * SIDE * SIDE + m, to))
    return lax.ppermute(block, ("dp", "mp"), route)


def other_core(block):
    return moved(block, lambda z, c, x, y: (z, c ^ 1, x, y))


def along_z(block, step):
    return moved(block, lambda z, c, x, y: (z + step, c, x, y))


def first_axis(block, step):
    return moved(block, lambda z, c, x, y: (z, c, x, y + step) if c == 0 else (z, c, x + step, y))


def second_axis(block, step):
    return moved(block, lambda z, c, x, y: (z, c, x + step, y) if c == 0 else (z, c, x, y + step))


def partner(block):
    return moved(block, lambda z, c, x, y: (z, c, x, y ^ 1))


def tree_closure(parents):
    width = parents.shape[-1]
    nodes = jnp.arange(width, dtype=jnp.int32)
    onehot = (parents[..., None] == nodes).astype(f32)
    reach = jnp.minimum(jnp.eye(width, dtype=f32) + onehot, 1.0)
    for _ in range((width - 1).bit_length()):
        small = reach.astype(bf16)
        reach = jnp.minimum(
            jnp.einsum("rij,rjk->rik", small, small, preferred_element_type=f32), 1.0
        )
    return reach


def unfolded(tile):
    wide = tile.astype(f32)
    return jnp.concatenate([wide[:, :64], wide[:, 64:]], 0).astype(tile.dtype)


def folded(array):
    half = array.shape[0] // 2
    wide = array.astype(f32)
    return jnp.concatenate([wide[:half], wide[half:]], 1).astype(array.dtype)


def pack_kernel(hidden_ref, gain_ref, x_ref):
    rows = hidden_ref.shape[0]
    for t in range(3):
        x_ref[t * rows : (t + 1) * rows, :] = hidden_ref[:, 128 * t : 128 * t + 128]
    x_ref[3 * rows : 3 * rows + rows // 2, :] = folded(hidden_ref[:, 384:448])
    gain = gain_ref[...].astype(f32).reshape(1, 448)
    gain = jnp.concatenate([gain, jnp.zeros((1, 64), f32)], 1)
    gain = jnp.concatenate(
        [gain[:, 128 * t : 128 * t + 128] for t in range(4)] + [jnp.zeros((28, 128), f32)], 0
    )
    x_ref[3 * rows + rows // 2 :, :] = gain.astype(bf16)


def pack(hidden, gain):
    rows = hidden.shape[0]
    return pl.pallas_call(
        pack_kernel,
        out_shape=jax.ShapeDtypeStruct((rows * 7 // 2 + 32, 128), bf16),
        in_specs=[whole()] * 2,
        out_specs=whole(),
        compiler_params=params(60),
        name="pack",
    )(hidden, gain)


def pack_weights_kernel(query_ref, key_ref, value_ref, w_ref):
    w_ref[:448, :384] = query_ref[:, :384]
    key = jnp.concatenate([key_ref[...].astype(f32), jnp.zeros((64, 64), f32)], 1).T
    w_ref[:448, 384:] = jnp.concatenate([query_ref[:, 384:448].astype(f32), key[:448]], 1).astype(bf16)
    w_ref[448:, :] = jnp.concatenate([value_ref[...].astype(f32), jnp.zeros((64, 64), f32)], 1).astype(bf16)


def pack_weights(w_query, w_key, w_value):
    return pl.pallas_call(
        pack_weights_kernel,
        out_shape=jax.ShapeDtypeStruct((512, 512), bf16),
        in_specs=[whole()] * 3,
        out_specs=whole(),
        compiler_params=params(60),
        name="pack_weights",
    )(w_query, w_key, w_value)


def join_kernel(upper_ref, lower_ref, out_ref):
    cut = upper_ref.shape[0]
    out_ref[:cut, :] = upper_ref[...]
    out_ref[cut:, :] = lower_ref[...]


def join(upper, lower):
    return pl.pallas_call(
        join_kernel,
        out_shape=jax.ShapeDtypeStruct((2 * upper.shape[0], upper.shape[1]), bf16),
        in_specs=[whole(), whole()],
        out_specs=whole(),
        compiler_params=params(4),
        name="join",
    )(upper, lower)


def cut_kernel(up_ref, down_ref, upper_ref, lower_ref):
    cut = upper_ref.shape[0]
    upper_ref[...] = up_ref[:cut, :]
    lower_ref[...] = down_ref[cut:, :]


def cut_blocks(up, down):
    half = jax.ShapeDtypeStruct((up.shape[0] // 2, up.shape[1]), bf16)
    return pl.pallas_call(
        cut_kernel,
        out_shape=[half, half],
        in_specs=[whole(), whole()],
        out_specs=[whole(), whole()],
        compiler_params=params(4),
        cost_estimate=pl.CostEstimate(flops=CUT_COST, bytes_accessed=10**6, transcendentals=0),
        name="cut_blocks",
    )(up, down)


def norm_kernel(x_ref, out_ref, squares, folds, inverse):
    rows = out_ref.shape[1]
    half = rows // 2

    @pl.loop(0, rows // 32)
    def _(chunk):
        total = jnp.zeros((32, 128), f32)
        for b in range(BLOCKS):
            for t in range(3):
                at = pl.ds(pl.multiple_of(t * rows + chunk * 32, 32), 32)
                part = x_ref[b, at, :].astype(f32)
                total = total + part * part
        squares[pl.ds(pl.multiple_of(chunk * 32, 32), 32), :] = total

    @pl.loop(0, half // 32)
    def _(chunk):
        total = jnp.zeros((32, 128), f32)
        at = pl.ds(pl.multiple_of(3 * rows + chunk * 32, 32), 32)
        for b in range(BLOCKS):
            part = x_ref[b, at, :].astype(f32)
            total = total + part * part
        folds[pl.ds(pl.multiple_of(chunk * 32, 32), 32), :] = total

    rest = folds[...]
    rest = jnp.concatenate(
        [jnp.sum(rest[:, :64], -1, keepdims=True), jnp.sum(rest[:, 64:], -1, keepdims=True)], 0
    )
    mean = (jnp.sum(squares[...], -1, keepdims=True) + rest) / (BLOCKS * 448)
    inverse[...] = jnp.broadcast_to(lax.rsqrt(mean + epsilon), inverse.shape)
    for b in range(BLOCKS):
        gain = x_ref[b, 3 * rows + half : 3 * rows + half + 16, :].astype(f32)
        for t in range(3):
            part = x_ref[b, t * rows : (t + 1) * rows, :].astype(f32)
            out_ref[b, :, 128 * t : 128 * t + 128] = (
                part * inverse[...] * gain[t : t + 1]
            ).astype(bf16)
        part = unfolded(x_ref[b, 3 * rows : 3 * rows + half, :]).astype(f32)
        out_ref[b, :, 384:448] = (part * inverse[:, :64] * gain[3:4, :64]).astype(bf16)


def norm(gathered, rows):
    return pl.pallas_call(
        norm_kernel,
        out_shape=jax.ShapeDtypeStruct((BLOCKS, rows, 448), bf16),
        in_specs=[whole()],
        out_specs=whole(),
        scratch_shapes=[
            pltpu.VMEM((rows, 128), f32),
            pltpu.VMEM((rows // 2, 128), f32),
            pltpu.VMEM((rows, 128), f32),
        ],
        compiler_params=params(16),
        cost_estimate=pl.CostEstimate(flops=10**7, bytes_accessed=8 * 10**6, transcendentals=0),
        name="norm",
    )(gathered)


def project_kernel(count, start, last, order, normed_ref, *refs):
    weights, rest = refs[:count], refs[count:]
    if start == 0:
        outs, total = rest, None
    else:
        total, outs = rest[0][...], rest[1:]
    for k in range(count):
        normed = normed_ref[order[start + k]]
        both = jnp.dot(normed, weights[k][:448, :], preferred_element_type=f32)
        value = lax.dot_general(
            normed, weights[k][448:, :448], (((1,), (1,)), ((), ())), preferred_element_type=f32
        )
        term = jnp.concatenate([both, value], 1)
        total = term if total is None else total + term
    if last:
        half = total.shape[0] // 2
        rounded = total.astype(bf16)
        for h in range(2):
            outs[h][...] = rounded[h * half : (h + 1) * half]
    else:
        outs[0][...] = total


def project(start, last, order, normed, slots, *total):
    rows, count = normed.shape[1], len(slots)
    if last:
        shape = [jax.ShapeDtypeStruct((rows // 2, 576), bf16)] * 2
    else:
        shape = [jax.ShapeDtypeStruct((rows, 576), f32)]
    return pl.pallas_call(
        functools.partial(project_kernel, count, start, last),
        out_shape=shape,
        in_specs=[scalars()] + [whole()] * (1 + count + len(total)),
        out_specs=[whole()] * len(shape),
        compiler_params=params(20),
        cost_estimate=pl.CostEstimate(
            flops=2 * rows * 448 * 576 * count, bytes_accessed=10**6 * count, transcendentals=0
        ),
        name="project",
    )(order, normed, *slots, *total)


def attention_kernel(
    facts, own_ref, oth_ref, cos_ref, sin_ref, reach_ref, pick_ref, key_ref, value_ref,
    kept_ref, sent_ref, stats_ref, chosen_ref, scores,
):
    request = pl.program_id(0)
    first = facts[0] == 0
    count = facts[1 + request]
    nodes = own_ref.shape[0]
    q_cols = 448
    cosine, sine = cos_ref[...], sin_ref[...]
    own, other = own_ref[...].astype(f32), oth_ref[...].astype(f32)

    def paired(lo, hi):
        low = jnp.where(first, own[:, lo:hi], other[:, lo:hi])
        high = jnp.where(first, other[:, lo:hi], own[:, lo:hi])
        return jnp.concatenate([low, high], 1)

    def turned(u):
        return (u * cosine + pltpu.roll(u, 64, 1) * sine).astype(bf16)

    query = paired(0, q_cols)
    queries = jnp.concatenate(
        [turned(query[:, 128 * g : 128 * g + 128]) for g in range(GROUP)], 0
    )
    rot_key = turned(paired(448, 512))
    node_value = paired(512, 576).astype(bf16)

    wide = rot_key.astype(f32)
    own_key = jnp.where(first, wide[:, :64], wide[:, 64:])
    kv_rows = jnp.concatenate([own_key, own[:, 512:576]], 1).astype(bf16)
    chosen_ref[0] = jnp.dot(pick_ref[0], kv_rows, preferred_element_type=f32).astype(bf16)

    pieces, rows, span = scores.shape
    nt = (((1,), (1,)), ((), ()))
    tree = lax.dot_general(queries, rot_key, nt, preferred_element_type=f32)
    reach = jnp.concatenate([reach_ref[0]] * GROUP, 0)
    tree = jnp.where(jnp.logical_and(reach > 0.5, first), tree, masked_score)
    highest = jnp.full((rows, 128), masked_score, f32)
    for c in range(pieces):
        part = lax.dot_general(
            queries, key_ref[0, c * span : (c + 1) * span, :], nt, preferred_element_type=f32
        )
        live = lax.broadcasted_iota(jnp.int32, (1, span), 1) + c * span < count
        part = jnp.where(live, part, masked_score)
        scores[c] = part
        for t in range(span // 128):
            highest = jnp.maximum(highest, part[:, 128 * t : 128 * t + 128])
    highest = jnp.maximum(
        jnp.max(highest, -1, keepdims=True), jnp.max(tree, -1, keepdims=True)
    )

    factor = math.log2(math.e) / math.sqrt(128.0)
    ones = jnp.ones((span, 128), bf16)
    weights = jnp.exp2((tree - highest) * factor).astype(bf16)
    summed = jnp.dot(
        weights, jnp.concatenate([node_value, ones[:nodes]], 1), preferred_element_type=f32
    )
    for c in range(pieces):
        weights = jnp.exp2((scores[c] - highest) * factor).astype(bf16)
        values = jnp.concatenate([value_ref[0, c * span : (c + 1) * span, :], ones], 1)
        summed = summed + jnp.dot(weights, values, preferred_element_type=f32)

    total = summed[:, 128:129]
    mean = summed[:, :128] / total
    some = jnp.logical_or(first, count > 0)
    level = jnp.where(some, highest * (1.0 / math.sqrt(128.0)) + jnp.log(total), masked_score)
    every = jnp.concatenate([mean[g * nodes : (g + 1) * nodes] for g in range(GROUP)], 1)
    low, high = every[:, :q_cols], every[:, q_cols:]
    kept_ref[...] = jnp.where(first, low, high)
    levels = jnp.concatenate(
        [level[g * nodes : (g + 1) * nodes] for g in range(GROUP)]
        + [jnp.zeros((nodes, 128 - GROUP), f32)], 1,
    )
    stats_ref[...] = levels
    coarse = levels[:, :16].astype(bf16).astype(f32)
    finer = (levels[:, :16] - coarse).astype(bf16).astype(f32)
    finest = levels[:, :16] - coarse - finer
    sent_ref[...] = jnp.concatenate(
        [jnp.where(first, high, low), coarse, finer, finest, jnp.zeros((nodes, 16), f32)], 1
    ).astype(bf16)


def attention(half, facts, own, other, cosine, sine, reach, pick, keys, values):
    half_len, head = keys.shape[-2:]
    requests = keys.shape[0] // 2
    nodes = own.shape[0] // requests
    columns = own.shape[1]
    base = half * requests

    def rows_of(width, at=0):
        return pl.BlockSpec((nodes, width), lambda r, facts: (at + r, 0))

    def request_of(*shape, at=0):
        return pl.BlockSpec((1,) + shape, lambda r, facts: (at + r, 0, 0))

    span = 512
    return pl.pallas_call(
        attention_kernel,
        grid_spec=pltpu.PrefetchScalarGridSpec(
            num_scalar_prefetch=1,
            grid=(requests,),
            in_specs=[
                rows_of(columns), rows_of(columns), rows_of(head, base), rows_of(head, base),
                request_of(nodes, nodes, at=base), request_of(*pick.shape[1:], at=base),
                request_of(half_len, head, at=base), request_of(half_len, head, at=base),
            ],
            out_specs=[rows_of(448), rows_of(512), rows_of(128), request_of(pick.shape[1], 128)],
            scratch_shapes=[pltpu.VMEM((half_len // span, GROUP * nodes, span), f32)],
        ),
        out_shape=[
            jax.ShapeDtypeStruct((requests * nodes, 448), f32),
            jax.ShapeDtypeStruct((requests * nodes, 512), bf16),
            jax.ShapeDtypeStruct((requests * nodes, 128), f32),
            jax.ShapeDtypeStruct((requests, pick.shape[1], 128), bf16),
        ],
        compiler_params=params(40),
        cost_estimate=pl.CostEstimate(
            flops=requests * ATTENTION_COST,
            bytes_accessed=requests * 2**20,
            transcendentals=requests * 448 * 2112,
        ),
        name="attention",
    )(facts, own, other, cosine, sine, reach, pick, keys, values)


def attend(facts, kept_ref, stats_ref, got_ref, valid_ref):
    first = facts[0] == 0
    got = got_ref[...].astype(f32)
    theirs = got[:, 448:464] + got[:, 464:480] + got[:, 480:496]
    ours = stats_ref[:, :16]
    highest = jnp.maximum(ours, theirs)
    own_factor = jnp.exp(ours - highest)
    other_factor = jnp.exp(theirs - highest)
    both = own_factor + other_factor

    def spread(part):
        rows = part.shape[0]
        every = jnp.concatenate(
            [jnp.broadcast_to(part[:, g : g + 1], (rows, 128)) for g in range(GROUP)], 1
        )
        return jnp.where(first, every[:, :448], every[:, 448:])

    mixed = kept_ref[...] * spread(own_factor / both) + got[:, :448] * spread(other_factor / both)
    return mixed.astype(bf16) * valid_ref[...]


def combine_kernel(place, *refs):
    out_ref = refs[8]
    rows = out_ref.shape[0] // 2
    for h in range(2):
        out_ref[h * rows : (h + 1) * rows, :] = attend(place, *refs[4 * h : 4 * h + 4])


def combine(place, arrays):
    return pl.pallas_call(
        combine_kernel,
        out_shape=jax.ShapeDtypeStruct((2 * arrays[0].shape[0], 448), bf16),
        in_specs=[scalars()] + [whole()] * 8,
        out_specs=whole(),
        compiler_params=params(8),
        name="combine",
    )(place, *arrays)


def out_kernel(steps, place, att_ref, weight_ref, *outs):
    rows = att_ref.shape[0]
    for out, step in zip(outs, steps):
        for along in range(SIDE):
            block = lax.rem(place[3] + step, SIDE) * place[1] + along * place[2]
            terms = jnp.dot(att_ref[...], weight_ref[block], preferred_element_type=f32)
            for t in range(3):
                out[along, t * rows : (t + 1) * rows, :] = terms[:, 128 * t : 128 * t + 128].astype(out.dtype)
            out[along, 3 * rows :, :] = folded(terms[:, 384:]).astype(out.dtype)


def out_terms(steps, place, attended, weights):
    rows = attended.shape[0] * 7 // 2
    return pl.pallas_call(
        functools.partial(out_kernel, steps),
        out_shape=[
            jax.ShapeDtypeStruct((SIDE, rows, 128), bf16 if step else f32) for step in steps
        ],
        in_specs=[scalars(), whole(), whole()],
        out_specs=[whole()] * len(steps),
        compiler_params=params(16),
        cost_estimate=pl.CostEstimate(
            flops=2 * 10**10, bytes_accessed=2 * 10**7, transcendentals=0
        ),
        name="out_terms",
    )(place, attended, weights)


def partial_kernel(place, own_ref, *refs):
    got, outs = refs[:3], refs[3:]
    for step in range(SIDE):
        at = lax.rem(place[0] + step, SIDE)
        value = own_ref[at]
        for part in got:
            value = value + part[at].astype(f32)
        outs[step][...] = value.astype(outs[step].dtype)


def partial_sums(place, own, got):
    shape = own.shape[1:]
    return pl.pallas_call(
        partial_kernel,
        out_shape=[jax.ShapeDtypeStruct(shape, bf16 if step else f32) for step in range(SIDE)],
        in_specs=[scalars()] + [whole()] * 4,
        out_specs=[whole()] * SIDE,
        compiler_params=params(16),
        name="partial_sums",
    )(place, own, *got)


def final_kernel(hidden_ref, own_ref, *refs):
    got, out_ref = refs[:3], refs[3]
    rows = hidden_ref.shape[0]
    value = own_ref[...]
    for part in got:
        value = value + part[...].astype(f32)
    dense = jnp.concatenate(
        [value[t * rows : (t + 1) * rows] for t in range(3)] + [unfolded(value[3 * rows :])], 1
    )
    out_ref[...] = (hidden_ref[...].astype(f32) + dense).astype(bf16)


def final(hidden, parts):
    return pl.pallas_call(
        final_kernel,
        out_shape=jax.ShapeDtypeStruct(hidden.shape, bf16),
        in_specs=[whole()] * 5,
        out_specs=whole(),
        compiler_params=params(12),
        name="final",
    )(hidden, *parts)


def two_way(block):
    dp = lax.axis_index("dp")
    slots, order = [block, other_core(block)], [dp, dp ^ 1]
    up = down = block
    for step in range(1, 4):
        up, down = along_z(up, 1), along_z(down, -1)
        slots += [up, down, other_core(up), other_core(down)]
        order += [dp - 2 * step, dp + 2 * step, (dp ^ 1) - 2 * step, (dp ^ 1) + 2 * step]
    upper, lower = cut_blocks(up, down)
    halves = along_z(upper, 1), along_z(lower, -1)
    order += [dp + 8, (dp ^ 1) + 8]
    return slots, halves, (jnp.stack(order) % DP).astype(jnp.int32)


def shards(
    hidden_in,
    norm_gain,
    w_query,
    w_key,
    w_value,
    w_out,
    key_cache,
    value_cache,
    cache_len,
    tree_parent,
    valid_nodes,
    accepted_path,
    slot_owner,
):
    req_dev, tree_size, part_width = hidden_in.shape
    row_count = req_dev * tree_size
    head_dim = key_cache.shape[-1]
    half_len = key_cache.shape[3]
    dp, mp = lax.axis_index("dp"), lax.axis_index("mp")
    z, core = dp // CORES, dp % CORES
    x, y = mp // SIDE, mp % SIDE
    me_first, me_second = jnp.where(core == 0, y, x), jnp.where(core == 0, x, y)
    half_index = mp % 2
    hidden = hidden_in.reshape(row_count, part_width)

    packed = pack(hidden, norm_gain)
    weights = pack_weights(w_query, w_key.T, w_value.T)

    slots, halves, order = two_way(weights)

    gathered = lax.all_gather(packed, "mp")

    out_weights = lax.all_gather(w_out, "dp")
    strides = jnp.where(core == 0, jnp.array([1, SIDE]), jnp.array([SIDE, 1]))
    place = jnp.concatenate([half_index[None], strides, me_first[None]]).astype(jnp.int32)

    reach = tree_closure(tree_parent)
    depth = jnp.sum(reach, -1) - 1.0
    position = (cache_len[:, None].astype(f32) + depth).reshape(row_count, 1)
    half_dim = head_dim // 2
    inverse = jnp.exp(
        jnp.arange(half_dim, dtype=f32) * (-2.0 * math.log(rope_base) / head_dim)
    )
    angles = position * inverse
    cosine, sine = jnp.cos(angles), jnp.sin(angles)
    cosine = jnp.concatenate([cosine, cosine], -1)
    sine = jnp.concatenate([-sine, sine], -1)
    picks = accepted_path.shape[1]
    pick = (
        jnp.pad(accepted_path, ((0, 0), (0, 16 - picks)))[..., None]
        == jnp.arange(tree_size, dtype=jnp.int32)
    ).astype(bf16)
    counts = jnp.clip(cache_len - half_index * half_len, 0, half_len)
    valid = valid_nodes.reshape(row_count, 1).astype(bf16)

    normed = norm(gathered, row_count)
    furthest = join(*halves)
    total = project(0, True, order, normed, slots + [furthest, other_core(furthest)])

    half_rows = row_count // 2
    others = [partner(own) for own in total]
    arrays, chosen = [], []
    for half, own in enumerate(total):
        at = slice(half * half_rows, (half + 1) * half_rows)
        group = slice(half * req_dev // 2, (half + 1) * req_dev // 2)
        facts = jnp.concatenate([half_index[None], counts[group]]).astype(jnp.int32)
        kept, sent, stats, rows = attention(
            half, facts, own, others[half], cosine, sine, reach, pick,
            key_cache[:, 0, 0], value_cache[:, 0, 0],
        )
        chosen.append(rows)
        arrays += [kept, stats, partner(sent), valid[at]]
    attended = combine(place, arrays)
    two, one = out_terms((2, 1), place, attended, out_weights)
    three, here = out_terms((3, 0), place, attended, out_weights)
    got = [first_axis(two, 2), first_axis(one, 1), first_axis(three, 3)]
    mine = partial_sums(me_second[None].astype(jnp.int32), here, got)
    parts = [mine[0]] + [second_axis(mine[s], s) for s in (2, 1, 3)]
    layer_out = final(hidden, parts).reshape(req_dev, tree_size, part_width)

    rows = jnp.pad(jnp.concatenate(chosen), ((0, 0), (0, 80 - chosen[0].shape[1]), (0, 0)))
    every_row = lax.all_gather(rows, "dp", axis=0, tiled=True)[:, :picks]
    total_reqs = slot_owner.shape[0]
    my_slots = dp * req_dev + jnp.arange(req_dev, dtype=jnp.int32)
    senders = (slot_owner[None, :] == my_slots[:, None]).astype(bf16)
    accepted_kv = (
        jnp.dot(senders, every_row.reshape(total_reqs, -1), preferred_element_type=f32)
        .astype(bf16)
        .reshape(req_dev, picks, 2, -1)
    )
    return (layer_out, accepted_kv)


def solution(mesh):
    placed = (
        P("dp", None, "mp"),
        P("mp"),
        P("dp", "mp"),
        P("dp", "mp"),
        P("dp", "mp"),
        P("mp", "dp"),
        P("dp", "mp", None, None, None),
        P("dp", "mp", None, None, None),
        P("dp"),
        P("dp", None),
        P("dp", None),
        P("dp", None),
        P(),
    )
    return jax.shard_map(
        shards,
        mesh=mesh,
        in_specs=placed,
        out_specs=(P("dp", None, "mp"), P("dp", None, None, "mp")),
        check_vma=False,
    )
```

```python
import functools
import math

import jax
import jax.numpy as jnp
from jax import lax
from jax.experimental import pallas as pl
from jax.experimental.pallas import tpu as pltpu
from jax.sharding import PartitionSpec as P

GROUP = 7
SIDE = 4
epsilon = 1e-05
rope_base = 5000000.0
masked_score = -1e30
bf16 = jnp.bfloat16
f32 = jnp.float32
VMEM = pltpu.VMEM


def whole():
    return pl.BlockSpec(memory_space=VMEM)


def scalars():
    return pl.BlockSpec(memory_space=pltpu.SMEM)


def params(mib):
    return pltpu.CompilerParams(vmem_limit_bytes=mib * 2**20)


DP, CORES, Z = 16, 2, 8
BLOCKS = 16
CUT_COST = 2 * 10**10
ATTENTION_COST = 25 * 10**9


def moved(block, target):
    route = []
    for d in range(DP):
        for m in range(SIDE * SIDE):
            z, core, x, y = target(d // CORES, d % CORES, m // SIDE, m % SIDE)
            to = (z % Z * CORES + core) * SIDE * SIDE + x % SIDE * SIDE + y % SIDE
            route.append((d * SIDE * SIDE + m, to))
    return lax.ppermute(block, ("dp", "mp"), route)


def other_core(block):
    return moved(block, lambda z, c, x, y: (z, c ^ 1, x, y))


def along_z(block, step):
    return moved(block, lambda z, c, x, y: (z + step, c, x, y))


def first_axis(block, step):
    return moved(block, lambda z, c, x, y: (z, c, x, y + step) if c == 0 else (z, c, x + step, y))


def second_axis(block, step):
    return moved(block, lambda z, c, x, y: (z, c, x + step, y) if c == 0 else (z, c, x, y + step))


def partner(block):
    return moved(block, lambda z, c, x, y: (z, c, x, y ^ 1))


def tree_closure(parents):
    width = parents.shape[-1]
    nodes = jnp.arange(width, dtype=jnp.int32)
    onehot = (parents[..., None] == nodes).astype(f32)
    reach = jnp.minimum(jnp.eye(width, dtype=f32) + onehot, 1.0)
    for _ in range((width - 1).bit_length()):
        small = reach.astype(bf16)
        reach = jnp.minimum(
            jnp.einsum("rij,rjk->rik", small, small, preferred_element_type=f32), 1.0
        )
    return reach


def unfolded(tile):
    wide = tile.astype(f32)
    return jnp.concatenate([wide[:, :64], wide[:, 64:]], 0).astype(tile.dtype)


def folded(array):
    half = array.shape[0] // 2
    wide = array.astype(f32)
    return jnp.concatenate([wide[:half], wide[half:]], 1).astype(array.dtype)


def pack_kernel(hidden_ref, gain_ref, x_ref):
    rows = hidden_ref.shape[0]
    for t in range(3):
        x_ref[t * rows : (t + 1) * rows, :] = hidden_ref[:, 128 * t : 128 * t + 128]
    x_ref[3 * rows : 3 * rows + rows // 2, :] = folded(hidden_ref[:, 384:448])
    gain = gain_ref[...].astype(f32).reshape(1, 448)
    gain = jnp.concatenate([gain, jnp.zeros((1, 64), f32)], 1)
    gain = jnp.concatenate(
        [gain[:, 128 * t : 128 * t + 128] for t in range(4)] + [jnp.zeros((28, 128), f32)], 0
    )
    x_ref[3 * rows + rows // 2 :, :] = gain.astype(bf16)


def pack(hidden, gain):
    rows = hidden.shape[0]
    return pl.pallas_call(
        pack_kernel,
        out_shape=jax.ShapeDtypeStruct((rows * 7 // 2 + 32, 128), bf16),
        in_specs=[whole()] * 2,
        out_specs=whole(),
        compiler_params=params(60),
        name="pack",
    )(hidden, gain)


def pack_weights_kernel(query_ref, key_ref, value_ref, w_ref):
    w_ref[:448, :384] = query_ref[:, :384]
    key = jnp.concatenate([key_ref[...].astype(f32), jnp.zeros((64, 64), f32)], 1).T
    w_ref[:448, 384:] = jnp.concatenate([query_ref[:, 384:448].astype(f32), key[:448]], 1).astype(bf16)
    w_ref[448:, :] = jnp.concatenate([value_ref[...].astype(f32), jnp.zeros((64, 64), f32)], 1).astype(bf16)


def pack_weights(w_query, w_key, w_value):
    return pl.pallas_call(
        pack_weights_kernel,
        out_shape=jax.ShapeDtypeStruct((512, 512), bf16),
        in_specs=[whole()] * 3,
        out_specs=whole(),
        compiler_params=params(60),
        name="pack_weights",
    )(w_query, w_key, w_value)


def join_kernel(upper_ref, lower_ref, out_ref):
    cut = upper_ref.shape[0]
    out_ref[:cut, :] = upper_ref[...]
    out_ref[cut:, :] = lower_ref[...]


def join(upper, lower):
    return pl.pallas_call(
        join_kernel,
        out_shape=jax.ShapeDtypeStruct((2 * upper.shape[0], upper.shape[1]), bf16),
        in_specs=[whole(), whole()],
        out_specs=whole(),
        compiler_params=params(4),
        name="join",
    )(upper, lower)


def cut_kernel(up_ref, down_ref, upper_ref, lower_ref):
    cut = upper_ref.shape[0]
    upper_ref[...] = up_ref[:cut, :]
    lower_ref[...] = down_ref[cut:, :]


def cut_blocks(up, down):
    half = jax.ShapeDtypeStruct((up.shape[0] // 2, up.shape[1]), bf16)
    return pl.pallas_call(
        cut_kernel,
        out_shape=[half, half],
        in_specs=[whole(), whole()],
        out_specs=[whole(), whole()],
        compiler_params=params(4),
        cost_estimate=pl.CostEstimate(flops=CUT_COST, bytes_accessed=10**6, transcendentals=0),
        name="cut_blocks",
    )(up, down)


def norm_kernel(x_ref, out_ref, squares, folds, inverse):
    rows = out_ref.shape[1]
    half = rows // 2

    @pl.loop(0, rows // 32)
    def _(chunk):
        total = jnp.zeros((32, 128), f32)
        for b in range(BLOCKS):
            for t in range(3):
                at = pl.ds(pl.multiple_of(t * rows + chunk * 32, 32), 32)
                part = x_ref[b, at, :].astype(f32)
                total = total + part * part
        squares[pl.ds(pl.multiple_of(chunk * 32, 32), 32), :] = total

    @pl.loop(0, half // 32)
    def _(chunk):
        total = jnp.zeros((32, 128), f32)
        at = pl.ds(pl.multiple_of(3 * rows + chunk * 32, 32), 32)
        for b in range(BLOCKS):
            part = x_ref[b, at, :].astype(f32)
            total = total + part * part
        folds[pl.ds(pl.multiple_of(chunk * 32, 32), 32), :] = total

    rest = folds[...]
    rest = jnp.concatenate(
        [jnp.sum(rest[:, :64], -1, keepdims=True), jnp.sum(rest[:, 64:], -1, keepdims=True)], 0
    )
    mean = (jnp.sum(squares[...], -1, keepdims=True) + rest) / (BLOCKS * 448)
    inverse[...] = jnp.broadcast_to(lax.rsqrt(mean + epsilon), inverse.shape)
    for b in range(BLOCKS):
        gain = x_ref[b, 3 * rows + half : 3 * rows + half + 16, :].astype(f32)
        for t in range(3):
            part = x_ref[b, t * rows : (t + 1) * rows, :].astype(f32)
            out_ref[b, :, 128 * t : 128 * t + 128] = (
                part * inverse[...] * gain[t : t + 1]
            ).astype(bf16)
        part = unfolded(x_ref[b, 3 * rows : 3 * rows + half, :]).astype(f32)
        out_ref[b, :, 384:448] = (part * inverse[:, :64] * gain[3:4, :64]).astype(bf16)


def norm(gathered, rows):
    return pl.pallas_call(
        norm_kernel,
        out_shape=jax.ShapeDtypeStruct((BLOCKS, rows, 448), bf16),
        in_specs=[whole()],
        out_specs=whole(),
        scratch_shapes=[
            pltpu.VMEM((rows, 128), f32),
            pltpu.VMEM((rows // 2, 128), f32),
            pltpu.VMEM((rows, 128), f32),
        ],
        compiler_params=params(16),
        cost_estimate=pl.CostEstimate(flops=10**7, bytes_accessed=8 * 10**6, transcendentals=0),
        name="norm",
    )(gathered)


def project_kernel(count, start, last, order, normed_ref, *refs):
    weights, rest = refs[:count], refs[count:]
    if start == 0:
        outs, total = rest, None
    else:
        total, outs = rest[0][...], rest[1:]
    for k in range(count):
        normed = normed_ref[order[start + k]]
        both = jnp.dot(normed, weights[k][:448, :], preferred_element_type=f32)
        value = lax.dot_general(
            normed, weights[k][448:, :448], (((1,), (1,)), ((), ())), preferred_element_type=f32
        )
        term = jnp.concatenate([both, value], 1)
        total = term if total is None else total + term
    if last:
        half = total.shape[0] // 2
        rounded = total.astype(bf16)
        for h in range(2):
            outs[h][...] = rounded[h * half : (h + 1) * half]
    else:
        outs[0][...] = total


def project(start, last, order, normed, slots, *total):
    rows, count = normed.shape[1], len(slots)
    if last:
        shape = [jax.ShapeDtypeStruct((rows // 2, 576), bf16)] * 2
    else:
        shape = [jax.ShapeDtypeStruct((rows, 576), f32)]
    return pl.pallas_call(
        functools.partial(project_kernel, count, start, last),
        out_shape=shape,
        in_specs=[scalars()] + [whole()] * (1 + count + len(total)),
        out_specs=[whole()] * len(shape),
        compiler_params=params(20),
        cost_estimate=pl.CostEstimate(
            flops=2 * rows * 448 * 576 * count, bytes_accessed=10**6 * count, transcendentals=0
        ),
        name="project",
    )(order, normed, *slots, *total)


def attention_kernel(
    facts, own_ref, oth_ref, cos_ref, sin_ref, reach_ref, pick_ref, key_ref, value_ref,
    kept_ref, sent_ref, stats_ref, chosen_ref, scores,
):
    request = pl.program_id(0)
    first = facts[0] == 0
    count = facts[1 + request]
    nodes = own_ref.shape[0]
    q_cols = 448
    cosine, sine = cos_ref[...], sin_ref[...]
    own, other = own_ref[...].astype(f32), oth_ref[...].astype(f32)

    def paired(lo, hi):
        low = jnp.where(first, own[:, lo:hi], other[:, lo:hi])
        high = jnp.where(first, other[:, lo:hi], own[:, lo:hi])
        return jnp.concatenate([low, high], 1)

    def turned(u):
        return (u * cosine + pltpu.roll(u, 64, 1) * sine).astype(bf16)

    query = paired(0, q_cols)
    queries = jnp.concatenate(
        [turned(query[:, 128 * g : 128 * g + 128]) for g in range(GROUP)], 0
    )
    rot_key = turned(paired(448, 512))
    node_value = paired(512, 576).astype(bf16)

    wide = rot_key.astype(f32)
    own_key = jnp.where(first, wide[:, :64], wide[:, 64:])
    kv_rows = jnp.concatenate([own_key, own[:, 512:576]], 1).astype(bf16)
    chosen_ref[0] = jnp.dot(pick_ref[0], kv_rows, preferred_element_type=f32).astype(bf16)

    pieces, rows, span = scores.shape
    nt = (((1,), (1,)), ((), ()))
    tree = lax.dot_general(queries, rot_key, nt, preferred_element_type=f32)
    reach = jnp.concatenate([reach_ref[0]] * GROUP, 0)
    tree = jnp.where(jnp.logical_and(reach > 0.5, first), tree, masked_score)
    highest = jnp.full((rows, 128), masked_score, f32)
    for c in range(pieces):
        part = lax.dot_general(
            queries, key_ref[0, c * span : (c + 1) * span, :], nt, preferred_element_type=f32
        )
        live = lax.broadcasted_iota(jnp.int32, (1, span), 1) + c * span < count
        part = jnp.where(live, part, masked_score)
        scores[c] = part
        for t in range(span // 128):
            highest = jnp.maximum(highest, part[:, 128 * t : 128 * t + 128])
    highest = jnp.maximum(
        jnp.max(highest, -1, keepdims=True), jnp.max(tree, -1, keepdims=True)
    )

    factor = math.log2(math.e) / math.sqrt(128.0)
    ones = jnp.ones((span, 128), bf16)
    weights = jnp.exp2((tree - highest) * factor).astype(bf16)
    summed = jnp.dot(
        weights, jnp.concatenate([node_value, ones[:nodes]], 1), preferred_element_type=f32
    )
    for c in range(pieces):
        weights = jnp.exp2((scores[c] - highest) * factor).astype(bf16)
        values = jnp.concatenate([value_ref[0, c * span : (c + 1) * span, :], ones], 1)
        summed = summed + jnp.dot(weights, values, preferred_element_type=f32)

    total = summed[:, 128:129]
    mean = summed[:, :128] / total
    some = jnp.logical_or(first, count > 0)
    level = jnp.where(some, highest * (1.0 / math.sqrt(128.0)) + jnp.log(total), masked_score)
    every = jnp.concatenate([mean[g * nodes : (g + 1) * nodes] for g in range(GROUP)], 1)
    low, high = every[:, :q_cols], every[:, q_cols:]
    kept_ref[...] = jnp.where(first, low, high)
    levels = jnp.concatenate(
        [level[g * nodes : (g + 1) * nodes] for g in range(GROUP)]
        + [jnp.zeros((nodes, 128 - GROUP), f32)], 1,
    )
    stats_ref[...] = levels
    coarse = levels[:, :16].astype(bf16).astype(f32)
    finer = (levels[:, :16] - coarse).astype(bf16).astype(f32)
    finest = levels[:, :16] - coarse - finer
    sent_ref[...] = jnp.concatenate(
        [jnp.where(first, high, low), coarse, finer, finest, jnp.zeros((nodes, 16), f32)], 1
    ).astype(bf16)


def attention(half, facts, own, other, cosine, sine, reach, pick, keys, values):
    half_len, head = keys.shape[-2:]
    requests = keys.shape[0] // 2
    nodes = own.shape[0] // requests
    columns = own.shape[1]
    base = half * requests

    def rows_of(width, at=0):
        return pl.BlockSpec((nodes, width), lambda r, facts: (at + r, 0))

    def request_of(*shape, at=0):
        return pl.BlockSpec((1,) + shape, lambda r, facts: (at + r, 0, 0))

    span = 512
    return pl.pallas_call(
        attention_kernel,
        grid_spec=pltpu.PrefetchScalarGridSpec(
            num_scalar_prefetch=1,
            grid=(requests,),
            in_specs=[
                rows_of(columns), rows_of(columns), rows_of(head, base), rows_of(head, base),
                request_of(nodes, nodes, at=base), request_of(*pick.shape[1:], at=base),
                request_of(half_len, head, at=base), request_of(half_len, head, at=base),
            ],
            out_specs=[rows_of(448), rows_of(512), rows_of(128), request_of(pick.shape[1], 128)],
            scratch_shapes=[pltpu.VMEM((half_len // span, GROUP * nodes, span), f32)],
        ),
        out_shape=[
            jax.ShapeDtypeStruct((requests * nodes, 448), f32),
            jax.ShapeDtypeStruct((requests * nodes, 512), bf16),
            jax.ShapeDtypeStruct((requests * nodes, 128), f32),
            jax.ShapeDtypeStruct((requests, pick.shape[1], 128), bf16),
        ],
        compiler_params=params(40),
        cost_estimate=pl.CostEstimate(
            flops=requests * ATTENTION_COST,
            bytes_accessed=requests * 2**20,
            transcendentals=requests * 448 * 2112,
        ),
        name="attention",
    )(facts, own, other, cosine, sine, reach, pick, keys, values)


def attend(facts, kept_ref, stats_ref, got_ref, valid_ref):
    first = facts[0] == 0
    got = got_ref[...].astype(f32)
    theirs = got[:, 448:464] + got[:, 464:480] + got[:, 480:496]
    ours = stats_ref[:, :16]
    highest = jnp.maximum(ours, theirs)
    own_factor = jnp.exp(ours - highest)
    other_factor = jnp.exp(theirs - highest)
    both = own_factor + other_factor

    def spread(part):
        rows = part.shape[0]
        every = jnp.concatenate(
            [jnp.broadcast_to(part[:, g : g + 1], (rows, 128)) for g in range(GROUP)], 1
        )
        return jnp.where(first, every[:, :448], every[:, 448:])

    mixed = kept_ref[...] * spread(own_factor / both) + got[:, :448] * spread(other_factor / both)
    return mixed.astype(bf16) * valid_ref[...]


def combine_kernel(place, *refs):
    out_ref = refs[8]
    rows = out_ref.shape[0] // 2
    for h in range(2):
        out_ref[h * rows : (h + 1) * rows, :] = attend(place, *refs[4 * h : 4 * h + 4])


def combine(place, arrays):
    return pl.pallas_call(
        combine_kernel,
        out_shape=jax.ShapeDtypeStruct((2 * arrays[0].shape[0], 448), bf16),
        in_specs=[scalars()] + [whole()] * 8,
        out_specs=whole(),
        compiler_params=params(8),
        name="combine",
    )(place, *arrays)


def out_kernel(steps, place, att_ref, weight_ref, *outs):
    rows = att_ref.shape[0]
    for out, step in zip(outs, steps):
        for along in range(SIDE):
            block = lax.rem(place[3] + step, SIDE) * place[1] + along * place[2]
            terms = jnp.dot(att_ref[...], weight_ref[block], preferred_element_type=f32)
            for t in range(3):
                out[along, t * rows : (t + 1) * rows, :] = terms[:, 128 * t : 128 * t + 128].astype(out.dtype)
            out[along, 3 * rows :, :] = folded(terms[:, 384:]).astype(out.dtype)


def out_terms(steps, place, attended, weights):
    rows = attended.shape[0] * 7 // 2
    return pl.pallas_call(
        functools.partial(out_kernel, steps),
        out_shape=[
            jax.ShapeDtypeStruct((SIDE, rows, 128), bf16 if step else f32) for step in steps
        ],
        in_specs=[scalars(), whole(), whole()],
        out_specs=[whole()] * len(steps),
        compiler_params=params(16),
        cost_estimate=pl.CostEstimate(
            flops=2 * 10**10, bytes_accessed=2 * 10**7, transcendentals=0
        ),
        name="out_terms",
    )(place, attended, weights)


def partial_kernel(place, own_ref, *refs):
    got, outs = refs[:3], refs[3:]
    for step in range(SIDE):
        at = lax.rem(place[0] + step, SIDE)
        value = own_ref[at]
        for part in got:
            value = value + part[at].astype(f32)
        outs[step][...] = value.astype(outs[step].dtype)


def partial_sums(place, own, got):
    shape = own.shape[1:]
    return pl.pallas_call(
        partial_kernel,
        out_shape=[jax.ShapeDtypeStruct(shape, bf16 if step else f32) for step in range(SIDE)],
        in_specs=[scalars()] + [whole()] * 4,
        out_specs=[whole()] * SIDE,
        compiler_params=params(16),
        name="partial_sums",
    )(place, own, *got)


def final_kernel(hidden_ref, own_ref, *refs):
    got, out_ref = refs[:3], refs[3]
    rows = hidden_ref.shape[0]
    value = own_ref[...]
    for part in got:
        value = value + part[...].astype(f32)
    dense = jnp.concatenate(
        [value[t * rows : (t + 1) * rows] for t in range(3)] + [unfolded(value[3 * rows :])], 1
    )
    out_ref[...] = (hidden_ref[...].astype(f32) + dense).astype(bf16)


def final(hidden, parts):
    return pl.pallas_call(
        final_kernel,
        out_shape=jax.ShapeDtypeStruct(hidden.shape, bf16),
        in_specs=[whole()] * 5,
        out_specs=whole(),
        compiler_params=params(12),
        name="final",
    )(hidden, *parts)


def two_way(block):
    dp = lax.axis_index("dp")
    slots, order = [block, other_core(block)], [dp, dp ^ 1]
    up = down = block
    for step in range(1, 4):
        up, down = along_z(up, 1), along_z(down, -1)
        slots += [up, down, other_core(up), other_core(down)]
        order += [dp - 2 * step, dp + 2 * step, (dp ^ 1) - 2 * step, (dp ^ 1) + 2 * step]
    upper, lower = cut_blocks(up, down)
    halves = along_z(upper, 1), along_z(lower, -1)
    order += [dp + 8, (dp ^ 1) + 8]
    return slots, halves, (jnp.stack(order) % DP).astype(jnp.int32)


def shards(
    hidden_in,
    norm_gain,
    w_query,
    w_key,
    w_value,
    w_out,
    key_cache,
    value_cache,
    cache_len,
    tree_parent,
    valid_nodes,
    accepted_path,
    slot_owner,
):
    req_dev, tree_size, part_width = hidden_in.shape
    row_count = req_dev * tree_size
    head_dim = key_cache.shape[-1]
    half_len = key_cache.shape[3]
    dp, mp = lax.axis_index("dp"), lax.axis_index("mp")
    z, core = dp // CORES, dp % CORES
    x, y = mp // SIDE, mp % SIDE
    me_first, me_second = jnp.where(core == 0, y, x), jnp.where(core == 0, x, y)
    half_index = mp % 2
    hidden = hidden_in.reshape(row_count, part_width)

    packed = pack(hidden, norm_gain)
    weights = pack_weights(w_query, w_key.T, w_value.T)

    slots, halves, order = two_way(weights)

    gathered = lax.all_gather(packed, "mp")

    out_weights = lax.all_gather(w_out, "dp")
    strides = jnp.where(core == 0, jnp.array([1, SIDE]), jnp.array([SIDE, 1]))
    place = jnp.concatenate([half_index[None], strides, me_first[None]]).astype(jnp.int32)

    reach = tree_closure(tree_parent)
    depth = jnp.sum(reach, -1) - 1.0
    position = (cache_len[:, None].astype(f32) + depth).reshape(row_count, 1)
    half_dim = head_dim // 2
    inverse = jnp.exp(
        jnp.arange(half_dim, dtype=f32) * (-2.0 * math.log(rope_base) / head_dim)
    )
    angles = position * inverse
    cosine, sine = jnp.cos(angles), jnp.sin(angles)
    cosine = jnp.concatenate([cosine, cosine], -1)
    sine = jnp.concatenate([-sine, sine], -1)
    picks = accepted_path.shape[1]
    pick = (
        jnp.pad(accepted_path, ((0, 0), (0, 16 - picks)))[..., None]
        == jnp.arange(tree_size, dtype=jnp.int32)
    ).astype(bf16)
    counts = jnp.clip(cache_len - half_index * half_len, 0, half_len)
    valid = valid_nodes.reshape(row_count, 1).astype(bf16)

    normed = norm(gathered, row_count)
    furthest = join(*halves)
    total = project(0, True, order, normed, slots + [furthest, other_core(furthest)])

    half_rows = row_count // 2
    others = [partner(own) for own in total]
    arrays, chosen = [], []
    for half, own in enumerate(total):
        at = slice(half * half_rows, (half + 1) * half_rows)
        group = slice(half * req_dev // 2, (half + 1) * req_dev // 2)
        facts = jnp.concatenate([half_index[None], counts[group]]).astype(jnp.int32)
        kept, sent, stats, rows = attention(
            half, facts, own, others[half], cosine, sine, reach, pick,
            key_cache[:, 0, 0], value_cache[:, 0, 0],
        )
        chosen.append(rows)
        arrays += [kept, stats, partner(sent), valid[at]]
    attended = combine(place, arrays)
    one, three = out_terms((1, 3), place, attended, out_weights)
    two, here = out_terms((2, 0), place, attended, out_weights)
    got = [first_axis(one, 1), first_axis(three, 3), first_axis(two, 2)]
    mine = partial_sums(me_second[None].astype(jnp.int32), here, got)
    parts = [mine[0]] + [second_axis(mine[s], s) for s in (2, 1, 3)]
    layer_out = final(hidden, parts).reshape(req_dev, tree_size, part_width)

    rows = jnp.pad(jnp.concatenate(chosen), ((0, 0), (0, 80 - chosen[0].shape[1]), (0, 0)))
    every_row = lax.all_gather(rows, "dp", axis=0, tiled=True)[:, :picks]
    total_reqs = slot_owner.shape[0]
    my_slots = dp * req_dev + jnp.arange(req_dev, dtype=jnp.int32)
    senders = (slot_owner[None, :] == my_slots[:, None]).astype(bf16)
    accepted_kv = (
        jnp.dot(senders, every_row.reshape(total_reqs, -1), preferred_element_type=f32)
        .astype(bf16)
        .reshape(req_dev, picks, 2, -1)
    )
    return (layer_out, accepted_kv)


def solution(mesh):
    placed = (
        P("dp", None, "mp"),
        P("mp"),
        P("dp", "mp"),
        P("dp", "mp"),
        P("dp", "mp"),
        P("mp", "dp"),
        P("dp", "mp", None, None, None),
        P("dp", "mp", None, None, None),
        P("dp"),
        P("dp", None),
        P("dp", None),
        P("dp", None),
        P(),
    )
    return jax.shard_map(
        shards,
        mesh=mesh,
        in_specs=placed,
        out_specs=(P("dp", None, "mp"), P("dp", None, None, "mp")),
        check_vma=False,
    )
```
